32 devices in a mesh: groups: 2 (over x), dp: 4 (over y, core), tensor: 4 (over z).
Axes of the slice: x: 2, y: 2, z: 4, core: 2. Of those that a mesh axis runs over, the one named last changes fastest.
Arguments:
- token_states: bfloat16 [10240, 8192], P(('groups', 'dp'), 'tensor'), parts along dimension 0, may hold values from -6 to 6
- base_weight: bfloat16 [8192, 1024], P('tensor'), may hold values from -0.0625 to 0.0625
- adapter_down: bfloat16 [32, 8192, 64], P(('groups', 'dp'), 'tensor'), parts along dimension 0, may hold values from -0.0625 to 0.0625
- adapter_up: bfloat16 [32, 64, 1024], P(('groups', 'dp'), None, 'tensor'), parts along dimension 0, may hold values from -0.1875 to 0.1875
- slot_of_tenant: int32 [32], P('groups'), parts along dimension 0, may hold values from 0 to 15, as said below
- seq_tenant: int32 [64], P('groups'), parts along dimension 0, may hold values from 0 to 15, as said below
- seq_len: int32 [64], P(('groups', 'dp')), parts along dimension 0, may hold values from 40 to 160, as said below
- token_mask: int32 [10240], P(('groups', 'dp')), parts along dimension 0, may hold values 0 or 1
- logp_gap: float32 [10240], P(('groups', 'dp')), parts along dimension 0, may hold values from -3 to 3
- out_sens: bfloat16 [10240, 1024], P(('groups', 'dp')), parts along dimension 0, may hold values from -0.59765625 to 0.59765625
- advantage: float32 [64], P(('groups', 'dp')), parts along dimension 0, may hold values from -4 to 4
Outputs:
- layer_out: bfloat16 [10240, 1024], P(('groups', 'dp', 'tensor')), parts along dimension 0
- seq_loss: float32 [64], P(('groups', 'dp')), parts along dimension 0
- token_state_gradient: bfloat16 [10240, 8192], P(('groups', 'dp'), 'tensor'), parts along dimension 0
- down_grad: bfloat16 [32, 8192, 64], P(('groups', 'dp'), 'tensor'), parts along dimension 0
- up_grad: bfloat16 [32, 64, 1024], P(('groups', 'dp'), None, 'tensor'), parts along dimension 0
The draws below stay inside these ranges and needn't reach their ends.
There are 2 independent parts, one for each index of `groups`. The reference program is written for one: setup_inputs(seed, part) draws one part's arguments, and reference() takes and returns one part's arrays. A program takes and returns all parts, laid end to end along the dimension named above; an argument that names none is the same for every part. Nothing has to cross between parts.
Inputs may be any that keep to these rules, and one draw needn't show every extreme that they name: slot_of_tenant is a permutation; slot s lies on index s // 4 of dp. `seq_tenant`: sequence b lies on index b // 8 of dp. Among the sequences of one index of dp at most 2 have tenants whose slots lie on one index of dp, and in every draw one index of dp holds the slots of exactly 2 sequences of every index of dp. `seq_len`: every index of dp has a sequence of 160 tokens and one of 40.
All inputs are finite; a program needn't handle non-finite values. No bound on the sum of `token_mask` on one device may be relied on, other than what follows from the above.
Results may differ from the reference program's by a relative error of at most 0.0064.
Values may be sent and summed in bfloat16 or wider, within the bound.
No kernel may reach another device: no remote copies, remote signals or barrier semaphores. Data moves between devices by JAX's collectives and lax.ppermute only.
A program may use at most 128 MiB of HBM per device.

```python
import jax
import jax.numpy as jnp
from jax import lax

D = 8192
KV = 1024
R = 64
SLOT_DEV = 4
CAP = 2
BLOCKS_DEV = 8
LEN = 160
TENANTS = 16
BLOCKS = 32
TOKENS = 5120


def tenant_slots(key):
    return jax.random.permutation(jax.random.fold_in(key, 101), TENANTS).astype(jnp.int32)


def draw_slot_of_tenant(key, part):
    slot_table = tenant_slots(key)
    return slot_table


def draw_seq_tenant(key, part):
    slot_table = tenant_slots(key)
    key = jax.random.fold_in(key, 2)
    devices = BLOCKS // BLOCKS_DEV
    tenant_at = jnp.argsort(slot_table).astype(jnp.int32)
    hot_owner = jax.random.randint(jax.random.fold_in(key, 1), (), 0, devices).astype(jnp.int32)
    others = jnp.arange(devices - 1, dtype=jnp.int32)
    others = others + (others >= hot_owner).astype(jnp.int32)
    owner_pool = jnp.tile(others, CAP)

    def one_device(device_key):
        shuffled = jax.random.permutation(jax.random.fold_in(device_key, 1), owner_pool.shape[0])
        chosen = jnp.concatenate([jnp.full((CAP,), hot_owner, jnp.int32), owner_pool[shuffled[:BLOCKS_DEV - CAP]]])
        placing = jax.random.permutation(jax.random.fold_in(device_key, 2), BLOCKS_DEV)
        owner_ids = chosen[placing]
        local_pick = jax.random.randint(jax.random.fold_in(device_key, 3), (BLOCKS_DEV,), 0, SLOT_DEV).astype(jnp.int32)
        return tenant_at[owner_ids * SLOT_DEV + local_pick]
    device_keys = jax.random.split(jax.random.fold_in(key, 4), devices)
    return jax.vmap(one_device)(device_keys).reshape(BLOCKS).astype(jnp.int32)


def draw_seq_len(key, part):
    key = jax.random.fold_in(key, 5)
    devices = BLOCKS // BLOCKS_DEV
    lengths = jax.random.randint(jax.random.fold_in(key, 1), (devices, BLOCKS_DEV), LEN // 4, LEN + 1)
    full_pick = jax.random.randint(jax.random.fold_in(key, 2), (devices, 1), 0, BLOCKS_DEV)
    short_step = jax.random.randint(jax.random.fold_in(key, 3), (devices, 1), 1, BLOCKS_DEV)
    short_pick = (full_pick + short_step) % BLOCKS_DEV
    column_ids = jnp.arange(BLOCKS_DEV, dtype=jnp.int32)[None, :]
    lengths = jnp.where(column_ids == full_pick, LEN, lengths)
    lengths = jnp.where(column_ids == short_pick, LEN // 4, lengths)
    return lengths.reshape(BLOCKS).astype(jnp.int32)


def draw_logp_gap(key, part):
    key = jax.random.fold_in(key, 7)
    offset = jax.random.uniform(jax.random.fold_in(key, 1), (BLOCKS, 1), jnp.float32, -0.4, 0.4)
    token_noise = jnp.clip(0.5 * jax.random.normal(jax.random.fold_in(key, 2), (BLOCKS, LEN), jnp.float32), -2.0, 2.0)
    return (offset + token_noise).reshape(TOKENS).astype(jnp.float32)


def with_ends(values, rng, least, high):
    shape = values.shape
    spot = [jax.random.randint(jax.random.fold_in(rng, axis), (), 0, shape[axis]) for axis in range(len(shape))]
    values = values.at[tuple(spot)].set(least)
    longest = shape.index(max(shape))
    spot[longest] = (spot[longest] + 1) % shape[longest]
    return values.at[tuple(spot)].set(high)


def block_scale(stream_key, extent, shards, least, top_value):
    factor_of = 1.0
    for dim, shards_of in shards:
        draws = jax.random.uniform(jax.random.fold_in(jax.random.fold_in(stream_key, 6), dim), (shards_of,), jnp.float32, least / len(shards), top_value / len(shards))
        factor_of = factor_of * jnp.repeat(jnp.exp(draws), extent[dim] // shards_of).reshape((-1,) + (1,) * (len(extent) - 1 - dim))
    return factor_of


def scatter_about(stream_key, shape, width, reach, shards=(), kind=jnp.bfloat16):
    array = jax.random.normal(stream_key, shape, jnp.float32) * width
    if len(shards) > 0:
        array = block_scale(stream_key, shape, shards, -0.22, 0.18) * array
    return jnp.clip(array, min=-reach, max=reach).astype(kind)


def setup_inputs(seed: int = 0, part: int = 0) -> dict:
    seeds = jax.random.split(jax.random.key(seed), 12)
    part_keys = jax.random.split(jax.random.fold_in(seeds[11], part), 12)
    return {
        "token_states": scatter_about(part_keys[0], (TOKENS, D), 1.0, 6.0, ((0, 4), (1, 4))),
        "base_weight": scatter_about(seeds[1], (D, KV), D ** -0.5, 0.0625, ((0, 4),)),
        "adapter_down": scatter_about(part_keys[2], (TENANTS, D, R), D ** -0.5, 0.0625, ((0, 4), (1, 4))),
        "adapter_up": scatter_about(part_keys[3], (TENANTS, R, KV), (16 * R) ** -0.5, 0.1875, ((0, 4), (2, 4))),
        "slot_of_tenant": draw_slot_of_tenant(jax.random.fold_in(jax.random.fold_in(seeds[11], part), 71), part),
        "seq_tenant": draw_seq_tenant(jax.random.fold_in(jax.random.fold_in(seeds[11], part), 71), part),
        "seq_len": draw_seq_len(jax.random.fold_in(jax.random.fold_in(seeds[11], part), 71), part),
        "token_mask": with_ends((jax.random.randint(part_keys[7], (TOKENS,), 0, 4) < 3).astype(jnp.int32), jax.random.fold_in(part_keys[7], 1), 0, 1),
        "logp_gap": draw_logp_gap(jax.random.fold_in(jax.random.fold_in(seeds[11], part), 71), part),
        "out_sens": scatter_about(part_keys[9], (TOKENS, KV), 0.1, 0.59765625, ((0, 4),)),
        "advantage": scatter_about(part_keys[10], (BLOCKS,), 1.0, 4.0, ((0, 4),), jnp.float32),
    }


adapter_scale = 2.0
loss_scale = 1024.0
clip_eps = 0.2


def reference(token_states, base_weight, adapter_down, adapter_up, slot_of_tenant, seq_tenant, seq_len, token_mask, logp_gap, out_sens, advantage):
    slot_index = slot_of_tenant[seq_tenant].astype(jnp.int32)
    states = token_states.reshape(BLOCKS, LEN, D)
    sens_blocks = out_sens.reshape(BLOCKS, LEN, KV)

    def forward_block(pieces):
        block_states, block_sens, slot_now = pieces
        down_panel = adapter_down[slot_now]
        up_panel = adapter_up[slot_now]
        hidden_rows = jnp.dot(block_states, down_panel, preferred_element_type=jnp.float32).astype(jnp.bfloat16)
        frozen_contribution = jnp.dot(block_states, base_weight, preferred_element_type=jnp.float32)
        adapted_output = jnp.dot(hidden_rows, up_panel, preferred_element_type=jnp.float32)
        layer_row_states = (frozen_contribution + adapter_scale * adapted_output).astype(jnp.bfloat16)
        projected_values = jnp.dot(block_sens, up_panel.T, preferred_element_type=jnp.float32)
        return layer_row_states, hidden_rows, projected_values

    layer_row_states, hidden_states_list, projected_values = lax.map(forward_block, (states, sens_blocks, slot_index))
    positions = jnp.arange(LEN, dtype=jnp.int32)
    live_mask = (token_mask.reshape(BLOCKS, LEN) * (positions[None, :] < seq_len[:, None]).astype(jnp.int32)).astype(jnp.float32)
    lengths = seq_len.astype(jnp.float32)
    linear_projection = adapter_scale * jnp.sum(hidden_states_list.astype(jnp.float32) * projected_values, axis=2)
    seq_log = jnp.sum(live_mask * (logp_gap.reshape(BLOCKS, LEN) + linear_projection), axis=1) / lengths
    seq_ratio = jnp.exp(seq_log)
    clipped = jnp.clip(seq_ratio, 1.0 - clip_eps, 1.0 + clip_eps)
    seq_loss = -jnp.minimum(seq_ratio * advantage, clipped * advantage)
    active = jnp.where(advantage >= 0, seq_ratio <= 1.0 + clip_eps, seq_ratio >= 1.0 - clip_eps)
    ratio_grad = jnp.where(active, -advantage * seq_ratio, jnp.float32(0.0))
    value_weight = loss_scale * ratio_grad[:, None] * live_mask / lengths[:, None]
    out_cot = (value_weight[:, :, None] * sens_blocks.astype(jnp.float32)).astype(jnp.bfloat16)
    hidden_cotangent = (adapter_scale * value_weight[:, :, None] * projected_values).astype(jnp.bfloat16)

    def backward_block(pieces):
        block_states, hidden_rows, block_cotangent, block_hcot, slot_now = pieces
        down_panel = adapter_down[slot_now]
        grad_in = jnp.dot(block_cotangent, base_weight.T, preferred_element_type=jnp.float32) + jnp.dot(block_hcot, down_panel.T, preferred_element_type=jnp.float32)
        grad_down = jnp.dot(block_states.T, block_hcot, preferred_element_type=jnp.float32).astype(jnp.bfloat16)
        up_matrix_gradient = (adapter_scale * jnp.dot(hidden_rows.T, block_cotangent, preferred_element_type=jnp.float32)).astype(jnp.bfloat16)
        return grad_in.astype(jnp.bfloat16), grad_down, up_matrix_gradient

    grad_rows, block_down, block_up = lax.map(backward_block, (states, hidden_states_list, out_cot, hidden_cotangent, slot_index))
    down_grad = jax.ops.segment_sum(block_down.astype(jnp.float32), slot_index, num_segments=TENANTS).astype(jnp.bfloat16)
    up_grad = jax.ops.segment_sum(block_up.astype(jnp.float32), slot_index, num_segments=TENANTS).astype(jnp.bfloat16)
    return (layer_row_states.reshape(TOKENS, KV), seq_loss, grad_rows.reshape(TOKENS, D), down_grad, up_grad)
```

```python
import functools

import jax
import jax.numpy as jnp
from jax import lax
from jax.experimental import pallas as pl
from jax.experimental.pallas import tpu as pltpu
from jax.sharding import PartitionSpec as P

CAP = 2
PAD = 16
LANES = 128

adapter_scale = 2.0
loss_scale = 1024.0
clip_eps = 0.2

BF = jnp.bfloat16
F32 = jnp.float32
VMEM_LIMIT = 48 * 1024 * 1024

ANY = pl.BlockSpec(memory_space=pl.ANY)
SMEM = pl.BlockSpec(memory_space=pltpu.SMEM)
VMEM = pl.BlockSpec(memory_space=pltpu.VMEM)


def params(**kw):
    return pltpu.CompilerParams(vmem_limit_bytes=VMEM_LIMIT, **kw)


def cost(flops, nbytes):
    return pl.CostEstimate(flops=int(flops), bytes_accessed=int(nbytes), transcendentals=0)


def nt(a, b):
    return lax.dot_general(a, b, (((1,), (1,)), ((), ())), preferred_element_type=F32)


def tn(a, b):
    return lax.dot_general(a, b, (((0,), (0,)), ((), ())), preferred_element_type=F32)


def nn(a, b):
    return jnp.dot(a, b, preferred_element_type=F32)


def route_kernel(n, slots, blocks, where, slot_ref, tenant_ref, down_ref, *rest):
    send_ref, seq_ref, pos_ref = rest[:3]
    out_refs = rest[3 : 3 + n - 1]
    count_ref, sem = rest[3 + n - 1 :]
    me = where[0]
    for i in range(n * CAP):
        send_ref[i] = -1
        seq_ref[i] = -1
    for k in range(n):
        count_ref[k] = 0

    def asked(i, used):
        k, b = i // blocks, lax.rem(i, blocks)
        slot = slot_ref[tenant_ref[(me ^ k) * blocks + b]] - me * slots
        used = jnp.where(b == 0, 0, used)
        mine = (slot >= 0) & (slot < slots) & (used < CAP)

        @pl.when(mine)
        def _():
            send_ref[k * CAP + used] = slot

        return used + mine.astype(jnp.int32)

    lax.fori_loop(0, n * blocks, asked, jnp.int32(0))

    def copies(k, r):
        return pltpu.make_async_copy(
            down_ref.at[jnp.maximum(send_ref[k * CAP + r], 0)], out_refs[k - 1].at[r], sem
        )

    for k in range(n - 1, 0, -1):
        for r in range(CAP):
            copies(k, r).start()

    def own(b, carry):
        k = me ^ (slot_ref[tenant_ref[me * blocks + b]] // slots)
        at = k * CAP + count_ref[k]
        count_ref[k] += 1
        seq_ref[at] = b
        pos_ref[b] = at
        return carry

    lax.fori_loop(0, blocks, own, 0)
    for k in range(n - 1, 0, -1):
        for r in range(CAP):
            copies(k, r).wait()


def route(n, where, slot_of_tenant, seq_tenant, down_t, blocks):
    slots, rank, rows = down_t.shape
    out = pl.pallas_call(
        functools.partial(route_kernel, n, slots, blocks),
        out_shape=[
            jax.ShapeDtypeStruct((n * CAP,), jnp.int32),
            jax.ShapeDtypeStruct((n * CAP,), jnp.int32),
            jax.ShapeDtypeStruct((blocks,), jnp.int32),
        ]
        + [jax.ShapeDtypeStruct((CAP, rank, rows), BF)] * (n - 1),
        in_specs=[SMEM, SMEM, SMEM, ANY],
        out_specs=[SMEM, SMEM, SMEM] + [ANY] * (n - 1),
        scratch_shapes=[pltpu.SMEM((n,), jnp.int32), pltpu.SemaphoreType.DMA],
        compiler_params=params(),
        cost_estimate=cost(0, 4 * (n - 1) * CAP * rank * rows),
        name="route",
    )(where, slot_of_tenant, seq_tenant, down_t)
    return out[0], out[1], out[2], out[3:]


def frozen_kernel(x_ref, w_ref, o_ref):
    o_ref[0] = nn(x_ref[0], w_ref[...]).astype(BF)


def frozen(states, weight, parts):
    tokens, rows = states.shape
    width = weight.shape[1]
    piece = tokens // parts
    return pl.pallas_call(
        frozen_kernel,
        grid=(parts,),
        out_shape=jax.ShapeDtypeStruct((parts, piece, width), BF),
        in_specs=[
            pl.BlockSpec((1, piece, rows), lambda i: (i, 0, 0)),
            pl.BlockSpec((rows, width), lambda i: (0, 0)),
        ],
        out_specs=pl.BlockSpec((1, piece, width), lambda i: (i, 0, 0)),
        compiler_params=params(),
        cost_estimate=cost(2 * tokens * rows * width, 2 * (tokens * rows + rows * width)),
        name="frozen",
    )(states.reshape(parts, piece, rows), weight)


def pick_up_kernel(n, t, where, send_ref, *rest):
    parts, outs = rest[:t], rest[t:]
    z = where[1]
    for d in range(t):
        source = lax.rem(z + t - d, t)
        for k in range(n):
            for r in range(CAP):
                slot = jnp.maximum(send_ref[k * CAP + r], 0)
                outs[k][source, r] = parts[d][slot]


def pick_up(n, t, where, send_tab, parts):
    slots, rank, cols = parts[0].shape
    return pl.pallas_call(
        functools.partial(pick_up_kernel, n, t),
        out_shape=[jax.ShapeDtypeStruct((t, CAP, rank, cols), BF)] * n,
        in_specs=[SMEM, SMEM] + [VMEM] * t,
        out_specs=[VMEM] * n,
        compiler_params=params(),
        cost_estimate=cost(0, 4 * n * t * CAP * rank * cols),
        name="pick_up",
    )(where, send_tab, *parts)


def panel_grad_kernel(ks, t, cols, blocks, seq_tab, sens_ref, states_ref, live_ref, *rest):
    ups = rest[: len(ks)]
    rest = rest[len(ks) + 1 :]
    proj_ref, outs = rest[0], rest[1 : 1 + len(ks)]
    panel = rest[1 + len(ks)]
    g = pl.program_id(0)
    for i in range(len(ks)):

        @pl.when(g // CAP == i)
        def _():
            for c in range(t):
                panel[:, c * cols : (c + 1) * cols] = ups[i][c, 0]

    sens = sens_ref[0]
    proj_ref[0] = nt(sens, panel[...])
    turned = nt(panel[...], sens)
    live = live_ref[0]
    grad = nn((adapter_scale * turned * live).astype(BF), states_ref[0]).astype(BF)
    for i in range(len(ks)):

        @pl.when(g // CAP == i)
        def _():
            outs[i][0] = grad


def panel_grad(ks, seq_tab, sens_blocks, state_blocks, live, ups, proj_before):
    t, _, rank, cols = ups[0].shape
    blocks, length, width = sens_blocks.shape
    rows = state_blocks.shape[2]
    first = ks[0]
    step = ks[1] - ks[0] if len(ks) > 1 else 1

    def seq_at(g, tab):
        return tab[(first + step * (g // CAP)) * CAP + lax.rem(g, CAP)]

    def seq_or_first(g, tab):
        return jnp.maximum(seq_at(g, tab), 0)

    def seq_or_spare(g, tab):
        b = seq_at(g, tab)
        return jnp.where(b < 0, blocks, b)

    def rank_in(i):
        return lambda g, tab: jnp.clip(g - i * CAP, 0, CAP - 1)

    up_maps = [
        pl.BlockSpec((t, 1, rank, cols), functools.partial(lambda f, g, tab: (0, f(g, tab), 0, 0), rank_in(i)))
        for i in range(len(ks))
    ]
    out_maps = [
        pl.BlockSpec((1, rank, rows), functools.partial(lambda f, g, tab: (f(g, tab), 0, 0), rank_in(i)))
        for i in range(len(ks))
    ]
    steps = len(ks) * CAP
    out = pl.pallas_call(
        functools.partial(panel_grad_kernel, ks, t, cols, blocks),
        grid_spec=pltpu.PrefetchScalarGridSpec(
            num_scalar_prefetch=1,
            grid=(steps,),
            in_specs=[
                pl.BlockSpec((1, length, width), lambda g, tab: (seq_or_first(g, tab), 0, 0)),
                pl.BlockSpec((1, length, rows), lambda g, tab: (seq_or_first(g, tab), 0, 0)),
                pl.BlockSpec((1, 1, length), lambda g, tab: (seq_or_first(g, tab), 0, 0)),
            ]
            + up_maps
            + [ANY],
            out_specs=[pl.BlockSpec((1, length, rank), lambda g, tab: (seq_or_spare(g, tab), 0, 0))] + out_maps,
            scratch_shapes=[pltpu.VMEM((rank, t * cols), BF)],
        ),
        out_shape=[jax.ShapeDtypeStruct((blocks + 1, length, rank), F32)]
        + [jax.ShapeDtypeStruct((CAP, rank, rows), BF)] * len(ks),
        input_output_aliases={4 + len(ks): 0},
        compiler_params=params(),
        cost_estimate=cost(
            2 * steps * length * rank * (2 * width + rows), 2 * steps * (length * (width + rows) + rank * rows)
        ),
        name="panel_grad",
    )(seq_tab, sens_blocks, state_blocks, live, *ups, proj_before)
    return out[0], out[1:]


def hidden_kernel(n, per, rank, pos_ref, send_ref, states_ref, down_ref, *rest):
    others = rest[: n - 1]
    hid_ref, panel_ref, stack, sem = rest[n - 1 :]
    b = pl.program_id(0)

    def pieces():
        for k in range(n):
            if k == 0:
                for r in range(CAP):
                    yield pltpu.make_async_copy(
                        down_ref.at[jnp.maximum(send_ref[r], 0)], stack.at[r], sem
                    )
            else:
                yield pltpu.make_async_copy(
                    others[k - 1], stack.at[pl.ds(k * CAP, CAP)], sem
                )

    @pl.when(b == 0)
    def _():
        for copy in pieces():
            copy.start()
        for copy in pieces():
            copy.wait()

    panel = stack[pos_ref[b]]
    panel_ref[0] = panel
    hidden = nt(states_ref[0], panel)
    for h in range(per):

        @pl.when(lax.rem(b, per) == h)
        def _():
            hid_ref[0, :, h * rank : (h + 1) * rank] = hidden


def hidden_parts(n, t, pos, send_tab, state_blocks, down_t, received):
    blocks, length, rows = state_blocks.shape
    slots, rank, _ = down_t.shape
    per = blocks // t
    return pl.pallas_call(
        functools.partial(hidden_kernel, n, per, rank),
        grid_spec=pltpu.PrefetchScalarGridSpec(
            num_scalar_prefetch=2,
            grid=(blocks,),
            in_specs=[pl.BlockSpec((1, length, rows), lambda b, p, s: (b, 0, 0))] + [ANY] * n,
            out_specs=[
                pl.BlockSpec((1, length, per * rank), lambda b, p, s: (b // per, 0, 0)),
                pl.BlockSpec((1, rank, rows), lambda b, p, s: (b, 0, 0)),
            ],
            scratch_shapes=[pltpu.VMEM((n * CAP, rank, rows), BF), pltpu.SemaphoreType.DMA],
        ),
        out_shape=[
            jax.ShapeDtypeStruct((t, length, per * rank), F32),
            jax.ShapeDtypeStruct((blocks, rank, rows), BF),
        ],
        compiler_params=params(),
        cost_estimate=cost(2 * blocks * length * rows * rank, 2 * blocks * rows * (length + 2 * rank)),
        name="hidden",
    )(pos, send_tab, state_blocks, down_t, *received)


def thirds(value):
    high = value.astype(BF)
    rest = value - high.astype(F32)
    middle = rest.astype(BF)
    return high, middle, (rest - middle.astype(F32)).astype(BF)


def own_kernel(t, per, rank, blocks, where, part_ref, proj_ref, live_ref, gap_ref, len_ref, out_ref):
    z = where[1]
    length = part_ref.shape[1]
    total = part_ref[0]
    for j in range(1, t):
        total = total + part_ref[j]
    hidden = total.astype(BF)
    out_ref[0:length, 0 : per * rank] = hidden
    lane = lax.broadcasted_iota(jnp.int32, (1, LANES), 1)
    seq_log = jnp.zeros((1, LANES), F32)
    for h in range(per):
        b = z * per + h
        product = hidden[:, h * rank : (h + 1) * rank].astype(F32) * proj_ref[b]
        mine = (lax.broadcasted_iota(jnp.int32, (length, LANES), 1) == b).astype(F32)
        live = jnp.sum(live_ref[...] * mine, axis=1, keepdims=True)
        gap = jnp.sum(gap_ref[...] * mine, axis=1, keepdims=True)
        linear = adapter_scale * jnp.sum(product, axis=1, keepdims=True)
        value = jnp.sum(live * (gap + linear), axis=0, keepdims=True)
        seq_log = seq_log + jnp.where(lane == b, value, 0.0)
    seq_log = seq_log / len_ref[...]
    row = lax.broadcasted_iota(jnp.int32, (PAD, LANES), 0)
    tail = jnp.zeros((PAD, LANES), F32)
    for i, piece in enumerate(thirds(seq_log)):
        tail = jnp.where(row == i, piece.astype(F32), tail)
    out_ref[length : length + PAD, 0:LANES] = tail.astype(BF)


def own_hidden(t, where, parts, proj, live_t, gap_t, len_row, per, rank):
    _, length, packed = parts.shape
    wide = max(packed, LANES)
    blocks = per * t
    return pl.pallas_call(
        functools.partial(own_kernel, t, per, rank, blocks),
        out_shape=jax.ShapeDtypeStruct((length + PAD, wide), BF),
        in_specs=[SMEM, VMEM, VMEM, VMEM, VMEM, VMEM],
        out_specs=VMEM,
        compiler_params=params(),
        cost_estimate=cost(0, 4 * t * length * wide),
        name="own_hidden",
    )(where, parts, proj, live_t, gap_t, len_row)


def up_grad_kernel(n, t, per, rank, blocks, where, pos_ref, sens_ref, live_ref, len_ref, adv_ref, *rest):
    msgs = rest[:t]
    factor_ref, loss_ref = rest[t : t + 2]
    outs = rest[t + 2 : t + 2 + n]
    stack, ups = rest[t + 2 + n :]
    z = where[1]
    length = live_ref.shape[0]
    cols = sens_ref.shape[1]
    seq_log = jnp.zeros((PAD, LANES), F32)
    for d in range(t):
        stack[lax.rem(z + t - d, t)] = msgs[d][...]
        seq_log = seq_log + msgs[d][length : length + PAD, 0:LANES].astype(F32)
    seq_log = seq_log[0:1] + seq_log[1:2] + seq_log[2:3]
    advantage = adv_ref[...]
    ratio = jnp.exp(seq_log)
    clipped = jnp.clip(ratio, 1.0 - clip_eps, 1.0 + clip_eps)
    loss_ref[...] = -jnp.minimum(ratio * advantage, clipped * advantage)
    active = ((advantage >= 0) & (ratio <= 1.0 + clip_eps)) | ((advantage < 0) & (ratio >= 1.0 - clip_eps))
    ratio_grad = jnp.where(active, -advantage * ratio, 0.0)
    factor = loss_scale * ratio_grad / len_ref[...]
    factor_ref[...] = factor
    row = lax.broadcasted_iota(jnp.int32, (PAD, cols), 0)
    for b in range(blocks):
        j, h = b // per, b % per
        mine = factor[:, b : b + 1]
        weight = mine * live_ref[:, b : b + 1]
        out_cot = (weight * sens_ref[b * length : (b + 1) * length, :].astype(F32)).astype(BF)
        hidden = stack[j, 0:length, h * rank : (h + 1) * rank]
        at = pos_ref[b]
        ups[at, 0:rank, :] = (adapter_scale * tn(hidden, out_cot)).astype(BF)
        tail = jnp.zeros((PAD, cols), F32)
        for i, piece in enumerate(thirds(mine)):
            tail = jnp.where(row == i, piece.astype(F32), tail)
        ups[at, rank : rank + PAD, :] = tail.astype(BF)
    for k in range(n):
        outs[k][...] = ups[k * CAP : (k + 1) * CAP]


def up_grads(n, t, where, pos, sens, live_t, len_row, adv_row, msgs, cols, rank, blocks):
    tokens, width = sens.shape
    length = tokens // blocks
    per = blocks // t
    packed = msgs[0].shape[1]
    row = jax.ShapeDtypeStruct((1, LANES), F32)
    whole = lambda shape: pl.BlockSpec(shape, lambda i, w, p: (0,) * len(shape))
    out = pl.pallas_call(
        functools.partial(up_grad_kernel, n, t, per, rank, blocks),
        grid_spec=pltpu.PrefetchScalarGridSpec(
            num_scalar_prefetch=2,
            grid=(1,),
            in_specs=[
                pl.BlockSpec((tokens, cols), lambda i, w, p: (0, w[1])),
                whole((length, LANES)),
                whole((1, LANES)),
                whole((1, LANES)),
            ]
            + [whole((length + PAD, packed))] * t,
            out_specs=[whole((1, LANES))] * 2 + [whole((CAP, rank + PAD, cols))] * n,
            scratch_shapes=[
                pltpu.VMEM((t, length + PAD, packed), BF),
                pltpu.VMEM((n * CAP, rank + PAD, cols), BF),
            ],
        ),
        out_shape=[row, row] + [jax.ShapeDtypeStruct((CAP, rank + PAD, cols), BF)] * n,
        compiler_params=params(),
        cost_estimate=cost(2 * tokens * cols * rank, 2 * tokens * cols),
        name="up_grads",
    )(where, pos, sens, live_t, len_row, adv_row, *msgs)
    return out[0], out[1], out[2:]


def state_grad_kernel(blocks, length, pair, factor_ref, live_ref, sens_ref, proj_ref, w_ref, panel_ref, o_ref, cot, hcot):
    @pl.when(pl.program_id(0) == 0)
    def _():
        for b in range(blocks):
            weight = factor_ref[:, b : b + 1] * live_ref[:, b : b + 1]
            rows = slice(b * length, (b + 1) * length)
            cot[rows, :] = (weight * sens_ref[rows, :].astype(F32)).astype(BF)
            hcot[b] = (adapter_scale * weight * proj_ref[b]).astype(BF)

    for p in range(blocks // pair):
        rows = slice(p * pair * length, (p + 1) * pair * length)
        frozen_part = nt(cot[rows, :], w_ref[...])
        for q in range(pair):
            b = p * pair + q
            adapter = nn(hcot[b], panel_ref[b])
            o_ref[b * length : (b + 1) * length, :] = (
                frozen_part[q * length : (q + 1) * length] + adapter
            ).astype(BF)


def state_grad(factor, live_t, sens, proj, weight, panels):
    tokens, width = sens.shape
    blocks, rank, rows = panels.shape
    length = tokens // blocks
    tile = min(512, rows)
    pair = 2 if blocks % 2 == 0 else 1
    whole = lambda shape: pl.BlockSpec(shape, lambda i: (0,) * len(shape))
    return pl.pallas_call(
        functools.partial(state_grad_kernel, blocks, length, pair),
        grid=(rows // tile,),
        out_shape=jax.ShapeDtypeStruct((tokens, rows), BF),
        in_specs=[
            whole((1, LANES)),
            whole((length, LANES)),
            whole((tokens, width)),
            whole(proj.shape),
            pl.BlockSpec((tile, width), lambda i: (i, 0)),
            pl.BlockSpec((blocks, rank, tile), lambda i: (0, 0, i)),
        ],
        out_specs=pl.BlockSpec((tokens, tile), lambda i: (0, i)),
        scratch_shapes=[pltpu.VMEM((tokens, width), BF), pltpu.VMEM((blocks, length, rank), BF)],
        compiler_params=params(),
        cost_estimate=cost(
            2 * tokens * rows * (width + rank), 2 * (tokens * (width + rows) + rows * width)
        ),
        name="state_grad",
    )(factor, live_t, sens, proj, weight, panels)


def slot_sum_kernel(n, rank, send_ref, *rest):
    grads, msgs = rest[:n], rest[n : 2 * n]
    down_ref, up_ref, acc, up_acc = rest[2 * n :]
    acc[...] = jnp.zeros_like(acc)
    up_acc[...] = jnp.zeros_like(up_acc)
    for k in range(n):
        for r in range(CAP):
            slot = send_ref[k * CAP + r]

            @pl.when(slot >= 0)
            def _():
                tail = jnp.sum(msgs[k][r, rank : rank + PAD, 0:LANES].astype(F32), axis=0, keepdims=True)
                factor = tail[:, 0:1]
                part = (factor * grads[k][r].astype(F32)).astype(BF).astype(F32)
                acc[slot] += part
                up_acc[slot] += msgs[k][r, 0:rank, :].astype(F32)

    down_ref[...] = acc[...].astype(BF)
    up_ref[...] = up_acc[...].astype(BF)


def slot_sum(n, slots, send_tab, grads, msgs):
    _, rank, rows = grads[0].shape
    cols = msgs[0].shape[2]
    tile = min(512, rows)
    return pl.pallas_call(
        functools.partial(slot_sum_kernel, n, rank),
        grid_spec=pltpu.PrefetchScalarGridSpec(
            num_scalar_prefetch=1,
            grid=(rows // tile,),
            in_specs=[pl.BlockSpec((CAP, rank, tile), lambda i, s: (0, 0, i))] * n
            + [pl.BlockSpec((CAP, rank + PAD, cols), lambda i, s: (0, 0, 0))] * n,
            out_specs=[
                pl.BlockSpec((slots, rank, tile), lambda i, s: (0, 0, i)),
                pl.BlockSpec((slots, rank, cols), lambda i, s: (0, 0, 0)),
            ],
            scratch_shapes=[pltpu.VMEM((slots, rank, tile), F32), pltpu.VMEM((slots, rank, cols), F32)],
        ),
        out_shape=[
            jax.ShapeDtypeStruct((slots, rank, rows), BF),
            jax.ShapeDtypeStruct((slots, rank, cols), BF),
        ],
        compiler_params=params(),
        cost_estimate=cost(0, 2 * (n * CAP + slots) * rank * rows),
        name="slot_sum",
    )(send_tab, *grads, *msgs)


def layer_out_kernel(n, t, per, rank, where, pos_ref, part_ref, msg_ref, *rest):
    ups, sums = rest[:n], rest[n:-3]
    o_ref, stack, panel = rest[-3:]
    z = where[1]
    length = msg_ref.shape[0] - PAD
    cols = ups[0].shape[3]
    for k in range(n):
        stack[k] = ups[k][...]
    for h in range(per):
        at = pos_ref[z * per + h]
        k, r = at // CAP, lax.rem(at, CAP)
        for c in range(t):
            panel[:, c * cols : (c + 1) * cols] = stack[k, c, r]
        hidden = msg_ref[0:length, h * rank : (h + 1) * rank]
        rows = slice(h * length, (h + 1) * length)
        total = part_ref[0, rows, :].astype(F32) + adapter_scale * nn(hidden, panel[...])
        for other in sums:
            total = total + other[rows, :].astype(F32)
        o_ref[rows, :] = total.astype(BF)


def layer_out(n, t, where, pos, partial, own_msg, ups, sums, per):
    _, piece, width = partial.shape
    _, _, rank, cols = ups[0].shape
    whole = lambda shape: pl.BlockSpec(shape, lambda i, w, p: (0,) * len(shape))
    return pl.pallas_call(
        functools.partial(layer_out_kernel, n, t, per, rank),
        grid_spec=pltpu.PrefetchScalarGridSpec(
            num_scalar_prefetch=2,
            grid=(1,),
            in_specs=[pl.BlockSpec((1, piece, width), lambda i, w, p: (w[1], 0, 0)), whole(own_msg.shape)]
            + [whole(u.shape) for u in ups]
            + [whole(s.shape) for s in sums],
            out_specs=whole((piece, width)),
            scratch_shapes=[pltpu.VMEM((n, t, CAP, rank, cols), BF), pltpu.VMEM((rank, width), BF)],
        ),
        out_shape=jax.ShapeDtypeStruct((piece, width), BF),
        compiler_params=params(),
        cost_estimate=cost(2 * piece * rank * width, 2 * piece * width * (2 + len(sums))),
        name="layer_out",
    )(where, pos, partial, own_msg, *ups, *sums)


def swap(value, axis, k):
    size = lax.axis_size(axis)
    return lax.ppermute(value, axis, [(i, i ^ k) for i in range(size)])


def shift(value, axis, k):
    size = lax.axis_size(axis)
    return lax.ppermute(value, axis, [(i, (i + k) % size) for i in range(size)])


def chain(partial, t, z):
    arrived = {}
    for level in range(t - 1):
        for j in range(t - 1, level, -1):
            piece = lax.dynamic_index_in_dim(partial, jnp.where(z == level, j, t - 1 - j), 0, keepdims=False)
            if level > 0:
                piece = (piece.astype(F32) + arrived[level - 1, j].astype(F32)).astype(BF)
            pairs = [(level, level + 1), (t - 1 - level, t - 2 - level)]
            arrived[level, j] = lax.ppermute(piece, "tensor", pairs)
    return [arrived[level, level + 1] for level in range(t - 1)]


def shards(
    token_states,
    base_weight,
    adapter_down,
    adapter_up,
    slot_of_tenant,
    seq_tenant,
    seq_len,
    token_mask,
    logp_gap,
    out_sens,
    advantage,
):
    n = lax.axis_size("dp")
    t = lax.axis_size("tensor")
    z = lax.axis_index("tensor")
    slots, rows, rank = adapter_down.shape
    cols = adapter_up.shape[2]
    width = out_sens.shape[1]
    blocks = seq_len.shape[0]
    tokens = token_states.shape[0]
    length = tokens // blocks
    per = blocks // t
    where = jnp.stack([lax.axis_index("dp"), z]).astype(jnp.int32)
    state_blocks = token_states.reshape(blocks, length, rows)
    sens_blocks = out_sens.reshape(blocks, length, width)
    down_t = jnp.swapaxes(adapter_down, 1, 2)

    up_parts = [adapter_up] + [shift(adapter_up, "tensor", k) for k in range(1, t)]
    send_tab, seq_tab, pos, down_send = route(n, where, slot_of_tenant, seq_tenant, down_t, blocks)
    down_recv = [swap(down_send[k - 1], "dp", k) for k in range(1, n)]
    partial = frozen(token_states, base_weight, t)
    up_send = pick_up(n, t, where, send_tab, up_parts)
    ups = [up_send[0]] + [swap(up_send[k], "dp", k) for k in range(1, n)]

    position = jnp.arange(length, dtype=jnp.int32)
    live = (token_mask.reshape(blocks, length) * (position[None, :] < seq_len[:, None])).astype(F32)
    spread = ((0, 0), (0, LANES - blocks))
    live_t = jnp.pad(live.T, spread)
    gap_t = jnp.pad(logp_gap.reshape(blocks, length).T, spread)
    len_row = jnp.pad(seq_len.astype(F32)[None], spread, constant_values=1.0)
    adv_row = jnp.pad(advantage[None], spread)
    live_rows = live[:, None, :]

    far = list(range(2, n)) if n > 2 else list(range(1, n))
    near = [k for k in range(n) if k not in far]
    blank = jnp.zeros((blocks + 1, length, rank), F32)
    proj, far_grads = panel_grad(
        far, seq_tab, sens_blocks, state_blocks, live_rows, [ups[k] for k in far], blank
    )
    proj, near_grads = panel_grad(
        near, seq_tab, sens_blocks, state_blocks, live_rows, [ups[k] for k in near], proj
    )
    grads = dict(zip(far + near, list(far_grads) + list(near_grads)))
    grads_in = [grads[0]] + [swap(grads[k], "dp", k) for k in range(1, n)]

    hidden, panels = hidden_parts(n, t, pos, send_tab, state_blocks, down_t, down_recv)
    hidden_all = lax.all_to_all(hidden, "tensor", 0, 0, tiled=True)
    own_msg = own_hidden(t, where, hidden_all, proj, live_t, gap_t, len_row, per, rank)
    msgs = [own_msg] + [shift(own_msg, "tensor", k) for k in range(1, t)]
    factor, loss, up_out = up_grads(
        n, t, where, pos, out_sens, live_t, len_row, adv_row, msgs, cols, rank, blocks
    )
    up_in = [up_out[0]] + [swap(up_out[k], "dp", k) for k in range(1, n)]
    token_state_gradient = state_grad(factor, live_t, out_sens, proj, base_weight, panels)
    down_grad, up_grad = slot_sum(n, slots, send_tab, grads_in, up_in)
    out = layer_out(n, t, where, pos, partial, own_msg, ups, chain(partial, t, z), per)
    return (
        out,
        loss[0, :blocks],
        token_state_gradient,
        jnp.swapaxes(down_grad, 1, 2),
        up_grad,
    )


def solution(mesh):
    in_specs = (
        P(("groups", "dp"), "tensor"),
        P("tensor", None),
        P(("groups", "dp"), "tensor", None),
        P(("groups", "dp"), None, "tensor"),
        P("groups"),
        P("groups"),
        P(("groups", "dp")),
        P(("groups", "dp")),
        P(("groups", "dp")),
        P(("groups", "dp"), None),
        P(("groups", "dp")),
    )
    out_specs = (
        P(("groups", "dp", "tensor"), None),
        P(("groups", "dp")),
        P(("groups", "dp"), "tensor"),
        P(("groups", "dp"), "tensor", None),
        P(("groups", "dp"), None, "tensor"),
    )
    return jax.shard_map(shards, mesh=mesh, in_specs=in_specs, out_specs=out_specs, check_vma=False)
```

```python
import functools

import jax
import jax.numpy as jnp
from jax import lax
from jax.experimental import pallas as pl
from jax.experimental.pallas import tpu as pltpu
from jax.sharding import PartitionSpec as P

CAP = 2
PAD = 16
LATE = 16
LANES = 128

adapter_scale = 2.0
loss_scale = 1024.0
clip_eps = 0.2

BF = jnp.bfloat16
F32 = jnp.float32
VMEM_LIMIT = 58 * 1024 * 1024

ANY = pl.BlockSpec(memory_space=pl.ANY)
SMEM = pl.BlockSpec(memory_space=pltpu.SMEM)
VMEM = pl.BlockSpec(memory_space=pltpu.VMEM)


def params(**kw):
    return pltpu.CompilerParams(vmem_limit_bytes=VMEM_LIMIT, **kw)


def cost(flops, nbytes, share=1):
    return pl.CostEstimate(flops=int(flops) // share, bytes_accessed=int(nbytes) // share, transcendentals=0)


def fetch(source, target, sem):
    copy = pltpu.make_async_copy(source, target, sem)
    copy.start()
    return copy


def dmas(count):
    return pltpu.SemaphoreType.DMA((count,))


def nt(a, b):
    return lax.dot_general(a, b, (((1,), (1,)), ((), ())), preferred_element_type=F32)


def tn(a, b):
    return lax.dot_general(a, b, (((0,), (0,)), ((), ())), preferred_element_type=F32)


def nn(a, b):
    return jnp.dot(a, b, preferred_element_type=F32)


def route_kernel(n, slots, blocks, where, slot_ref, tenant_ref, down_ref, send_ref, pos_ref, out_ref, send_tab, count, sems):
    me = where[0]
    asked = [[slot_ref[tenant_ref[o * blocks + b]] for b in range(blocks)] for o in range(n)]
    for i in range(n * CAP):
        send_tab[i] = -1
    for o in range(n):
        count[o] = 0
    copies = []
    for o in range(n):
        used = jnp.int32(0)
        for slot in asked[o]:
            local = slot - me * slots
            mine = (local >= 0) & (local < slots) & (used < CAP)
            send_tab[jnp.where(mine, o * CAP + used, n * CAP)] = local
            used = used + mine.astype(jnp.int32)
        for r in range(CAP):
            at = o * CAP + r
            copies.append(fetch(down_ref.at[jnp.maximum(send_tab[at], 0)], out_ref.at[o, r], sems.at[at]))
    for b in range(blocks):
        o = slot_ref[tenant_ref[me * blocks + b]] // slots
        pos_ref[b] = o * CAP + count[o]
        count[o] += 1
    for i in range(n * CAP):
        send_ref[i] = send_tab[i]
    for copy in copies:
        copy.wait()


def route(n, where, slot_of_tenant, seq_tenant, down_t, blocks):
    slots, rank, rows = down_t.shape
    return pl.pallas_call(
        functools.partial(route_kernel, n, slots, blocks),
        out_shape=[
            jax.ShapeDtypeStruct((n * CAP,), jnp.int32),
            jax.ShapeDtypeStruct((blocks,), jnp.int32),
            jax.ShapeDtypeStruct((n, CAP, rank, rows), BF),
        ],
        in_specs=[SMEM] * 3 + [ANY],
        out_specs=[SMEM] * 2 + [VMEM],
        scratch_shapes=[pltpu.SMEM((n * CAP + 1,), jnp.int32), pltpu.SMEM((n,), jnp.int32), dmas(n * CAP)],
        compiler_params=params(),
        cost_estimate=cost(0, 4 * n * CAP * rank * rows),
        name="route",
    )(where, slot_of_tenant, seq_tenant, down_t)


def prepare_kernel(blocks, len_ref, mask_ref, gap_ref, adv_ref, live_ref, cols_ref, rows_ref, square):
    length = mask_ref.shape[1]
    square[...] = jnp.zeros_like(square)
    position = lax.broadcasted_iota(jnp.int32, (1, length), 1)
    for b in range(blocks):
        live = (mask_ref[b : b + 1, :] * (position < len_ref[b]).astype(jnp.int32)).astype(F32)
        live_ref[b] = live
        square[b : b + 1, 0:length] = live
    square[blocks : 2 * blocks, 0:length] = gap_ref[...]
    cols_ref[...] = square[...].T[0:length, :]
    lane = lax.broadcasted_iota(jnp.int32, (1, LANES), 1)
    lengths = jnp.ones((1, LANES), F32)
    for b in range(blocks):
        lengths = jnp.where(lane == b, len_ref[b].astype(F32), lengths)
    rows_ref[...] = jnp.zeros_like(rows_ref)
    rows_ref[0:1, :] = lengths
    rows_ref[1:2, 0:blocks] = adv_ref[...]


def prepare(seq_len, mask, gap, advantage):
    blocks, length = mask.shape
    wide = -(-length // LANES) * LANES
    return pl.pallas_call(
        functools.partial(prepare_kernel, blocks),
        out_shape=[
            jax.ShapeDtypeStruct((blocks, 1, length), F32),
            jax.ShapeDtypeStruct((length, LANES), F32),
            jax.ShapeDtypeStruct((8, LANES), F32),
        ],
        in_specs=[SMEM] + [VMEM] * 3,
        out_specs=[VMEM] * 3,
        scratch_shapes=[pltpu.VMEM((LANES, wide), F32)],
        compiler_params=params(),
        cost_estimate=cost(0, 8 * blocks * length),
        name="prepare",
    )(seq_len, mask, gap, advantage)


def frozen_kernel(t, order, split, where, x_ref, w_ref, *rest):
    outs, (x_buf, w_buf, o_buf, x_sem, w_sem, o_sem) = rest[-5 - split - len(order) : -6], rest[-6:]
    z = where[1]
    piece = x_ref.shape[0] // t
    half = w_ref.shape[1] // 2
    some = piece // split
    loads, weights, stores = [], [], []

    def load(i):
        start = pl.multiple_of((z ^ order[i]) * piece, 16)
        loads.append(fetch(x_ref.at[pl.ds(start, piece), :], x_buf.at[i], x_sem.at[i]))

    load(0)
    for side in range(2):
        cols = pl.ds(side * half, half)
        weights.append(fetch(w_ref.at[:, cols], w_buf.at[side], w_sem.at[side]))
    for i in range(1, len(order)):
        load(i)
    for i in range(len(order)):
        loads[i].wait()
        for side in range(2):
            if i == 0:
                weights[side].wait()
            o_buf[i, :, side * half : (side + 1) * half] = nn(x_buf[i], w_buf[side]).astype(BF)
        if i > 0:
            at = split + i - 1
            stores.append(fetch(o_buf.at[i], outs[at], o_sem.at[at]))
        else:
            for p in range(split):
                stores.append(fetch(o_buf.at[i, pl.ds(p * some, some)], outs[p], o_sem.at[p]))
    for store in stores:
        store.wait()


def frozen(t, order, split, where, states, weight, after=()):
    tokens, rows = states.shape
    width = weight.shape[1]
    piece = tokens // t
    count = len(order)
    return pl.pallas_call(
        functools.partial(frozen_kernel, t, order, split),
        out_shape=[jax.ShapeDtypeStruct((piece // split, width), BF)] * split
        + [jax.ShapeDtypeStruct((piece, width), BF)] * (count - 1),
        in_specs=[SMEM, ANY, ANY] + [ANY] * len(after),
        out_specs=[ANY] * (count - 1 + split),
        scratch_shapes=[
            pltpu.VMEM((count, piece, rows), BF),
            pltpu.VMEM((2, rows, width // 2), BF),
            pltpu.VMEM((count, piece, width), BF),
            dmas(count),
            dmas(2),
            dmas(count - 1 + split),
        ],
        compiler_params=params(),
        cost_estimate=cost(2 * count * piece * rows * width, 2 * (count * piece * rows + rows * width)),
        name="frozen",
    )(where, states, weight, *after)


def pick_up_kernel(n, t, where, send_ref, *rest):
    parts, outs = rest[:t], rest[-n:]
    me, z = where[0], where[1]
    for k in range(n):
        for r in range(CAP):
            slot = jnp.maximum(send_ref[(me ^ k) * CAP + r], 0)
            for d in range(t):
                outs[k][z ^ d, r] = parts[d][slot]


def pick_up(n, t, where, send_tab, parts, after=()):
    slots, rank, cols = parts[0].shape
    return pl.pallas_call(
        functools.partial(pick_up_kernel, n, t),
        out_shape=[jax.ShapeDtypeStruct((t, CAP, rank, cols), BF)] * n,
        in_specs=[SMEM, SMEM] + [VMEM] * t + [ANY] * len(after),
        out_specs=[VMEM] * n,
        compiler_params=params(),
        cost_estimate=cost(0, 4 * n * t * CAP * rank * cols),
        name="pick_up",
    )(where, send_tab, *parts, *after)


def hidden_kernel(t, per, where, pos_ref, states_ref, down_ref, *rest):
    outs = rest[-5 - t + 1 : -4]
    down_buf, state_buf, down_sem, state_sem = rest[-4:]
    z = where[1]
    rank = down_buf.shape[2]
    panels = fetch(down_ref, down_buf, down_sem)
    order = list(range(t - 1, -1, -1))
    loads = [
        fetch(states_ref.at[pl.ds((z ^ k) * per, per)], state_buf.at[k], state_sem.at[k]) for k in order
    ]
    panels.wait()
    for i, k in enumerate(order):
        loads[i].wait()
        for h in range(per):
            at = pos_ref[(z ^ k) * per + h]
            panel = down_buf[at // CAP, lax.rem(at, CAP)]
            outs[k][:, h * rank : (h + 1) * rank] = nt(state_buf[k, h], panel)


def hidden_parts(t, where, pos, state_blocks, down_recv, after=()):
    blocks, length, rows = state_blocks.shape
    rank = down_recv.shape[2]
    per = blocks // t
    return pl.pallas_call(
        functools.partial(hidden_kernel, t, per),
        in_specs=[SMEM, SMEM] + [ANY] * (2 + len(after)),
        out_specs=[VMEM] * t,
        out_shape=[jax.ShapeDtypeStruct((length, per * rank), F32)] * t,
        scratch_shapes=[
            pltpu.VMEM(down_recv.shape, BF),
            pltpu.VMEM((t, per, length, rows), BF),
            pltpu.SemaphoreType.DMA,
            dmas(t),
        ],
        compiler_params=params(),
        cost_estimate=cost(2 * blocks * length * rows * rank, 2 * blocks * rows * (length + rank)),
        name="hidden",
    )(where, pos, state_blocks, down_recv, *after)


def panel_kernel(pos_ref, cols_ref, proj_ref, states_ref, *rest):
    out_ref, state_buf, grad_buf, state_sem, grad_sem = rest[-5:]
    blocks = states_ref.shape[0]
    states = []
    for p in range(blocks // 2):
        some = pl.ds(p * 2, 2)
        states.append(fetch(states_ref.at[some], state_buf.at[some], state_sem.at[p]))
    for b in range(blocks):
        turned = (adapter_scale * cols_ref[:, b : b + 1] * proj_ref[b]).T.astype(BF)
        if b % 2 == 0:
            states[b // 2].wait()
        at = pos_ref[b]
        grad_buf[at // CAP, lax.rem(at, CAP)] = nn(turned, state_buf[b]).astype(BF)
    store = fetch(grad_buf, out_ref, grad_sem)
    store.wait()


def panel_grads(n, pos, columns, proj, state_blocks, after=()):
    blocks, length, rank = proj.shape
    rows = state_blocks.shape[2]
    return pl.pallas_call(
        panel_kernel,
        in_specs=[SMEM, VMEM, VMEM] + [ANY] * (1 + len(after)),
        out_specs=ANY,
        scratch_shapes=[
            pltpu.VMEM((blocks, length, rows), BF),
            pltpu.VMEM((n, CAP, rank, rows), BF),
            dmas(blocks // 2),
            pltpu.SemaphoreType.DMA,
        ],
        out_shape=jax.ShapeDtypeStruct((n, CAP, rank, rows), BF),
        compiler_params=params(),
        cost_estimate=cost(2 * blocks * length * rank * rows, 2 * blocks * (length * rows + rank * rows)),
        name="panel_grads",
    )(pos, columns, proj, state_blocks, *after)


def thirds(value):
    high = value.astype(BF)
    rest = value - high.astype(F32)
    middle = rest.astype(BF)
    return high, middle, (rest - middle.astype(F32)).astype(BF)


def own_kernel(t, per, rank, blocks, where, proj_ref, cols_ref, rows_ref, *rest):
    parts = rest[:t]
    out_ref, proj_buf, sem = rest[-3:]
    z = where[1]
    load = fetch(proj_ref.at[pl.ds(z * per, per)], proj_buf, sem)
    length = parts[0].shape[0]
    total = parts[0][...]
    for part in parts[1:]:
        total = total + part[...]
    hidden = total.astype(BF)
    out_ref[0:length, 0 : per * rank] = hidden
    lane = lax.broadcasted_iota(jnp.int32, (1, LANES), 1)
    lanes = lax.broadcasted_iota(jnp.int32, (length, LANES), 1)
    columns = cols_ref[...]
    load.wait()
    seq_log = jnp.zeros((1, LANES), F32)
    for h in range(per):
        b = z * per + h
        product = hidden[:, h * rank : (h + 1) * rank].astype(F32) * proj_buf[h]
        live = jnp.sum(jnp.where(lanes == b, columns, 0.0), axis=1, keepdims=True)
        gap = jnp.sum(jnp.where(lanes == b + blocks, columns, 0.0), axis=1, keepdims=True)
        linear = adapter_scale * jnp.sum(product, axis=1, keepdims=True)
        value = jnp.sum(live * (gap + linear), axis=0, keepdims=True)
        seq_log = seq_log + jnp.where(lane == b, value, 0.0)
    seq_log = seq_log / rows_ref[0:1, :]
    row = lax.broadcasted_iota(jnp.int32, (PAD, LANES), 0)
    tail = jnp.zeros((PAD, LANES), F32)
    for i, piece in enumerate(thirds(seq_log)):
        tail = jnp.where(row == i, piece.astype(F32), tail)
    out_ref[length : length + PAD, 0:LANES] = tail.astype(BF)


def own_hidden(t, where, parts, proj, columns, rows, per, rank, after=()):
    length, packed = parts[0].shape
    wide = max(packed, LANES)
    return pl.pallas_call(
        functools.partial(own_kernel, t, per, rank, per * t),
        out_shape=jax.ShapeDtypeStruct((length + PAD, wide), BF),
        in_specs=[SMEM, ANY] + [VMEM] * (2 + t) + [ANY] * len(after),
        out_specs=VMEM,
        scratch_shapes=[pltpu.VMEM((per, length, rank), F32), pltpu.SemaphoreType.DMA],
        compiler_params=params(),
        cost_estimate=cost(0, 4 * t * length * wide, LATE),
        name="own_hidden",
    )(where, proj, columns, rows, *parts, *after)


def up_grad_kernel(n, t, per, rank, where, pos_ref, sens_ref, cols_ref, rows_ref, *rest):
    msgs = rest[:t]
    factor_ref, loss_ref = rest[t : t + 2]
    outs = rest[t + 2 : -4]
    stack, ups, sens_buf, sem = rest[-4:]
    n = len(outs)
    z = where[1]
    blocks, length, width = sens_ref.shape
    cols = width // t
    start = pl.multiple_of(z * cols, LANES)
    load = fetch(sens_ref.at[:, :, pl.ds(start, cols)], sens_buf, sem)
    seq_log = jnp.zeros((PAD, LANES), F32)
    for d in range(t):
        stack[z ^ d] = msgs[d][...]
        seq_log = seq_log + msgs[d][length : length + PAD, 0:LANES].astype(F32)
    seq_log = seq_log[0:1] + seq_log[1:2] + seq_log[2:3]
    advantage = rows_ref[1:2, :]
    ratio = jnp.exp(seq_log)
    clipped = jnp.clip(ratio, 1.0 - clip_eps, 1.0 + clip_eps)
    loss_ref[...] = -jnp.minimum(ratio * advantage, clipped * advantage)
    active = ((advantage >= 0) & (ratio <= 1.0 + clip_eps)) | ((advantage < 0) & (ratio >= 1.0 - clip_eps))
    ratio_grad = jnp.where(active, -advantage * ratio, 0.0)
    factor = loss_scale * ratio_grad / rows_ref[0:1, :]
    factor_ref[...] = factor
    row = lax.broadcasted_iota(jnp.int32, (PAD, cols), 0)
    load.wait()
    for b in range(blocks):
        j, h = b // per, b % per
        mine = factor[:, b : b + 1]
        weight = mine * cols_ref[:, b : b + 1]
        out_cot = (weight * sens_buf[b].astype(F32)).astype(BF)
        hidden = stack[j, 0:length, h * rank : (h + 1) * rank]
        at = pos_ref[b]
        at = (at // CAP, lax.rem(at, CAP))
        ups[at[0], at[1], 0:rank, :] = (adapter_scale * tn(hidden, out_cot)).astype(BF)
        tail = jnp.zeros((PAD, cols), F32)
        for i, piece in enumerate(thirds(mine)):
            tail = jnp.where(row == i, piece.astype(F32), tail)
        ups[at[0], at[1], rank : rank + PAD, :] = tail.astype(BF)
    for k in range(n):
        outs[k][...] = ups[where[0] ^ k]


def up_grads(n, t, where, pos, sens_blocks, columns, rows, msgs, rank):
    blocks, length, width = sens_blocks.shape
    cols = width // t
    row = jax.ShapeDtypeStruct((1, LANES), F32)
    out = pl.pallas_call(
        functools.partial(up_grad_kernel, n, t, blocks // t, rank),
        in_specs=[SMEM, SMEM, ANY] + [VMEM] * (2 + t),
        out_specs=[VMEM] * (2 + n),
        scratch_shapes=[
            pltpu.VMEM((t,) + msgs[0].shape, BF),
            pltpu.VMEM((n, CAP, rank + PAD, cols), BF),
            pltpu.VMEM((blocks, length, cols), BF),
            pltpu.SemaphoreType.DMA,
        ],
        out_shape=[row, row] + [jax.ShapeDtypeStruct((CAP, rank + PAD, cols), BF)] * n,
        compiler_params=params(),
        cost_estimate=cost(2 * blocks * length * cols * rank, 2 * blocks * length * cols, LATE),
        name="up_grads",
    )(where, pos, sens_blocks, columns, rows, *msgs)
    return out[0], out[1], out[2:]


def back_kernel(n, per, where, pos_ref, sens_ref, w_ref, *rest):
    ups = rest[:n]
    o_ref, proj_ref, own_ref, s_buf, w_buf, o_buf, up_buf, s_sem, w_sem, o_sem, up_sem = rest[-11:]
    me, z = where[0], where[1]
    t = ups[0].shape[0]
    tiles, tile, _ = w_buf.shape
    blocks, length, _ = s_buf.shape
    half = blocks // 2
    loads = [fetch(sens_ref.at[pl.ds(p * half, half)], s_buf.at[pl.ds(p * half, half)], s_sem.at[p]) for p in range(2)]
    weights = [fetch(w_ref.at[pl.ds(0, tile), :], w_buf.at[0], w_sem.at[0])]
    loads += [fetch(ups[k], up_buf.at[me ^ k], up_sem.at[k]) for k in range(n)]
    for i in range(1, tiles):
        weights.append(fetch(w_ref.at[pl.ds(i * tile, tile), :], w_buf.at[i], w_sem.at[i]))

    def panel(at):
        o, r = at // CAP, lax.rem(at, CAP)
        return jnp.concatenate([up_buf[o, c, r] for c in range(t)], axis=1)

    stores = []
    for i in range(tiles):
        weights[i].wait()
        for p in range(2):
            if i == 0:
                loads[p].wait()
            rows = slice(p * half, (p + 1) * half)
            o_buf[i, p * half * length : (p + 1) * half * length, :] = nt(
                s_buf[rows].reshape(half * length, s_buf.shape[2]), w_buf[i]
            ).astype(BF)
        stores.append(fetch(o_buf.at[i], o_ref.at[:, pl.ds(i * tile, tile)], o_sem.at[i]))
    for load in loads[2:]:
        load.wait()
    for b in range(blocks):
        proj_ref[b] = nt(s_buf[b], panel(pos_ref[b]))
    for h in range(per):
        own_ref[h] = panel(pos_ref[z * per + h])
    for store in stores:
        store.wait()


def back(n, where, pos, sens_blocks, weight, ups, after=()):
    blocks, length, width = sens_blocks.shape
    t, _, rank, cols = ups[0].shape
    per = blocks // t
    tokens = blocks * length
    rows = weight.shape[0]
    tiles = max(rows // 512, 1)
    return pl.pallas_call(
        functools.partial(back_kernel, n, per),
        out_shape=[
            jax.ShapeDtypeStruct((tokens, rows), BF),
            jax.ShapeDtypeStruct((blocks, length, rank), F32),
            jax.ShapeDtypeStruct((per, rank, width), BF),
        ],
        in_specs=[SMEM, SMEM] + [ANY] * (2 + n + len(after)),
        out_specs=[ANY, VMEM, VMEM],
        scratch_shapes=[
            pltpu.VMEM((blocks, length, width), BF),
            pltpu.VMEM((tiles, rows // tiles, width), BF),
            pltpu.VMEM((tiles, tokens, rows // tiles), BF),
            pltpu.VMEM((n, t, CAP, rank, cols), BF),
            dmas(2),
            dmas(tiles),
            dmas(tiles),
            dmas(n),
        ],
        compiler_params=params(),
        cost_estimate=cost(2 * tokens * rows * width, 2 * (tokens * (width + rows) + rows * width)),
        name="back",
    )(where, pos, sens_blocks, weight, *ups, *after)


def state_grad_kernel(pos_ref, factor_ref, cols_ref, proj_ref, back_ref, down_ref, o_ref, *rest):
    panels, in_buf, out_buf, panel_sem, in_sem, out_sem = rest
    blocks, length, _ = back_ref.shape
    half = blocks // 2
    loads = [fetch(down_ref, panels, panel_sem)]
    for p in range(half):
        some = pl.ds(2 * p, 2)
        loads.append(fetch(back_ref.at[some], in_buf.at[some], in_sem.at[p]))
    weight = factor_ref[...] * cols_ref[...]
    loads[0].wait()
    stores = []
    for b in range(blocks):
        if b % 2 == 0:
            loads[1 + b // 2].wait()
        hcot = (adapter_scale * proj_ref[b]).astype(BF)
        at = pos_ref[b]
        total = in_buf[b].astype(F32) + nn(hcot, panels[at // CAP, lax.rem(at, CAP)])
        out_buf[b] = (weight[:, b : b + 1] * total).astype(BF)
        if b % 2 == 1:
            some = pl.ds(b - 1, 2)
            stores.append(fetch(out_buf.at[some], o_ref.at[some], out_sem.at[b // 2]))
    for store in stores:
        store.wait()


def state_grad(pos, factor, columns, proj, backward, down_recv):
    blocks, length, rows = backward.shape
    rank = down_recv.shape[2]
    return pl.pallas_call(
        state_grad_kernel,
        out_shape=jax.ShapeDtypeStruct((blocks, length, rows), BF),
        in_specs=[SMEM, VMEM, VMEM, VMEM, ANY, ANY],
        out_specs=ANY,
        scratch_shapes=[
            pltpu.VMEM(down_recv.shape, BF),
            pltpu.VMEM((blocks, length, rows), BF),
            pltpu.VMEM((blocks, length, rows), BF),
            pltpu.SemaphoreType.DMA,
            dmas(blocks // 2),
            dmas(blocks // 2),
        ],
        compiler_params=params(),
        cost_estimate=cost(2 * blocks * length * rows * rank, 4 * blocks * length * rows, LATE),
        name="state_grad",
    )(pos, factor, columns, proj, backward, down_recv)


def slot_sum_kernel(n, rank, where, send_ref, grad_ref, *rest):
    msgs, (down_ref, up_ref, acc, up_acc, buf, out_buf, sems, out_sems) = rest[:n], rest[n:]
    me = where[0]
    slots = acc.shape[0]
    loads = [fetch(grad_ref.at[me ^ k], buf.at[k], sems.at[k]) for k in range(n)]
    acc[...] = jnp.zeros_like(acc)
    up_acc[...] = jnp.zeros_like(up_acc)
    for k in range(n):
        loads[k].wait()
        for r in range(CAP):
            slot = send_ref[(me ^ k) * CAP + r]
            used = slot >= 0
            slot = jnp.maximum(slot, 0)
            tail = jnp.sum(msgs[k][r, rank : rank + PAD, 0:LANES].astype(F32), axis=0, keepdims=True)
            part = (tail[:, 0:1] * buf[k, r].astype(F32)).astype(BF).astype(F32)
            acc[slot] += jnp.where(used, part, 0.0)
            up_acc[slot] += jnp.where(used, msgs[k][r, 0:rank, :].astype(F32), 0.0)
    stores = []
    for s in range(slots):
        out_buf[s] = acc[s].astype(BF)
        stores.append(fetch(out_buf.at[s], down_ref.at[s], out_sems.at[s]))
    up_ref[...] = up_acc[...].astype(BF)
    for store in stores:
        store.wait()


def slot_sum(slots, where, send_tab, grads, msgs):
    n, _, rank, rows = grads.shape
    cols = msgs[0].shape[2]
    return pl.pallas_call(
        functools.partial(slot_sum_kernel, n, rank),
        in_specs=[SMEM, SMEM, ANY] + [VMEM] * n,
        out_specs=[ANY, VMEM],
        scratch_shapes=[
            pltpu.VMEM((slots, rank, rows), F32),
            pltpu.VMEM((slots, rank, cols), F32),
            pltpu.VMEM(grads.shape, BF),
            pltpu.VMEM((slots, rank, rows), BF),
            dmas(n),
            dmas(slots),
        ],
        out_shape=[
            jax.ShapeDtypeStruct((slots, rank, rows), BF),
            jax.ShapeDtypeStruct((slots, rank, cols), BF),
        ],
        compiler_params=params(),
        cost_estimate=cost(0, 2 * (n * CAP + slots) * rank * rows, LATE),
        name="slot_sum",
    )(where, send_tab, grads, *msgs)


def layer_out_kernel(per, total, msg_ref, up_ref, *rest):
    parts, (o_ref, buf, sems) = rest[:total], rest[-3:]
    length = msg_ref.shape[0] - PAD
    rank = up_ref.shape[1]
    count = buf.shape[0]
    piece = buf.shape[1]
    loads = [fetch(part, buf.at[i], sems.at[i]) for i, part in enumerate(parts[: count - 1])]
    halves = parts[count - 1 :]
    some = piece // len(halves)
    for p, part in enumerate(halves):
        loads.append(fetch(part, buf.at[count - 1, pl.ds(p * some, some)], sems.at[count - 1 + p]))
    for load in loads:
        load.wait()
    for h in range(per):
        hidden = msg_ref[0:length, h * rank : (h + 1) * rank]
        rows = slice(h * length, (h + 1) * length)
        total = adapter_scale * nn(hidden, up_ref[h])
        for i in range(count):
            total = total + buf[i, rows, :].astype(F32)
        o_ref[rows, :] = total.astype(BF)


def layer_out(own_msg, up_own, whole, halves, after=()):
    piece, width = whole[0].shape
    parts = whole + halves
    per, rank, _ = up_own.shape
    return pl.pallas_call(
        functools.partial(layer_out_kernel, per, len(parts)),
        in_specs=[VMEM, VMEM] + [ANY] * (len(parts) + len(after)),
        out_specs=VMEM,
        scratch_shapes=[pltpu.VMEM((len(whole) + 1, piece, width), BF), dmas(len(parts))],
        out_shape=jax.ShapeDtypeStruct((piece, width), BF),
        compiler_params=params(),
        cost_estimate=cost(2 * piece * rank * width, 2 * piece * width * (1 + len(parts)), LATE),
        name="layer_out",
    )(own_msg, up_own, *parts, *after)


def exchange(value, axis):
    return lax.all_to_all(value, axis, 0, 0, tiled=True)


def swap(value, axis, k):
    size = lax.axis_size(axis)
    return lax.ppermute(value, axis, [(i, i ^ k) for i in range(size)])


def shards(
    token_states,
    base_weight,
    adapter_down,
    adapter_up,
    slot_of_tenant,
    seq_tenant,
    seq_len,
    token_mask,
    logp_gap,
    out_sens,
    advantage,
):
    n = lax.axis_size("dp")
    t = lax.axis_size("tensor")
    slots, rows, rank = adapter_down.shape
    width = out_sens.shape[1]
    blocks = seq_len.shape[0]
    length = token_states.shape[0] // blocks
    per = blocks // t
    where = jnp.stack([lax.axis_index("dp"), lax.axis_index("tensor")]).astype(jnp.int32)
    state_blocks = token_states.reshape(blocks, length, rows)
    sens_blocks = out_sens.reshape(blocks, length, width)
    down_t = jnp.swapaxes(adapter_down, 1, 2)

    up_parts = [adapter_up] + [swap(adapter_up, "tensor", k) for k in range(1, t)]
    send_tab, pos, down_send = route(n, where, slot_of_tenant, seq_tenant, down_t, blocks)
    down_recv = exchange(down_send, "dp")
    middle = t // 2
    others = [k for k in range(t - 1, -1, -1) if k != middle]
    parts = frozen(t, [middle] + others, 2, where, token_states, base_weight, (down_send, up_parts[1]))
    chunks = dict(zip(others, parts[2:]))
    up_send = pick_up(n, t, where, send_tab, up_parts, (chunks[0],))
    ups = [up_send[0]] + [swap(up_send[k], "dp", k) for k in range(1, n)]
    live, columns, seq_rows = prepare(
        seq_len, token_mask.reshape(blocks, length), logp_gap.reshape(blocks, length), advantage[None]
    )
    hidden = hidden_parts(t, where, pos, state_blocks, down_recv, (up_send[0],))
    hidden = [hidden[0]] + [swap(hidden[k], "tensor", k) for k in range(1, t)]
    second, _ = lax.optimization_barrier((parts[1], hidden[1]))
    early = [swap(half, "tensor", middle) for half in (parts[0], second)]
    backward, proj, up_own = back(n, where, pos, sens_blocks, base_weight, ups, (hidden[1], early[0]))
    own_msg = own_hidden(t, where, hidden, proj, columns, seq_rows, per, rank)
    msgs = [own_msg] + [swap(own_msg, "tensor", k) for k in range(1, t)]
    grads = panel_grads(n, pos, columns, proj, state_blocks, (*msgs[1:], early[1]))
    grads_in = exchange(grads, "dp")
    factor, loss, up_out = up_grads(n, t, where, pos, sens_blocks, columns, seq_rows, msgs, rank)
    up_in = [up_out[0]] + [swap(up_out[k], "dp", k) for k in range(1, n)]
    token_state_gradient = state_grad(
        pos, factor, columns, proj, backward.reshape(blocks, length, rows), down_recv
    )
    down_grad, up_grad = slot_sum(slots, where, send_tab, grads_in, up_in)
    sums = [chunks[0]]
    for k in others[:-1]:
        piece, _ = lax.optimization_barrier((chunks[k], msgs[1:]))
        sums.append(swap(piece, "tensor", k))
    out = layer_out(own_msg, up_own, sums, early, (up_grad,))
    return (
        out,
        loss[0, :blocks],
        token_state_gradient.reshape(blocks * length, rows),
        jnp.swapaxes(down_grad, 1, 2),
        up_grad,
    )


def solution(mesh):
    in_specs = (
        P(("groups", "dp"), "tensor"),
        P("tensor", None),
        P(("groups", "dp"), "tensor", None),
        P(("groups", "dp"), None, "tensor"),
        P("groups"),
        P("groups"),
        P(("groups", "dp")),
        P(("groups", "dp")),
        P(("groups", "dp")),
        P(("groups", "dp"), None),
        P(("groups", "dp")),
    )
    out_specs = (
        P(("groups", "dp", "tensor"), None),
        P(("groups", "dp")),
        P(("groups", "dp"), "tensor"),
        P(("groups", "dp"), "tensor", None),
        P(("groups", "dp"), None, "tensor"),
    )
    return jax.shard_map(shards, mesh=mesh, in_specs=in_specs, out_specs=out_specs, check_vma=False)
```

```python
import functools

import jax
import jax.numpy as jnp
from jax import lax
from jax.experimental import pallas as pl
from jax.experimental.pallas import tpu as pltpu
from jax.sharding import PartitionSpec as P

CAP = 2
PAD = 16
LATE = 16
LANES = 128

adapter_scale = 2.0
loss_scale = 1024.0
clip_eps = 0.2

BF = jnp.bfloat16
F32 = jnp.float32
VMEM_LIMIT = 58 * 1024 * 1024
SMALL_LIMIT = 20 * 1024 * 1024

ANY = pl.BlockSpec(memory_space=pl.ANY)
SMEM = pl.BlockSpec(memory_space=pltpu.SMEM)
VMEM = pl.BlockSpec(memory_space=pltpu.VMEM)


def params(limit=VMEM_LIMIT):
    return pltpu.CompilerParams(vmem_limit_bytes=limit)


def cost(flops, nbytes, share=1):
    return pl.CostEstimate(flops=int(flops) // share, bytes_accessed=int(nbytes) // share, transcendentals=0)


def fetch(source, target, sem):
    copy = pltpu.make_async_copy(source, target, sem)
    copy.start()
    return copy


def dmas(count):
    return pltpu.SemaphoreType.DMA((count,))


def nt(a, b):
    return lax.dot_general(a, b, (((1,), (1,)), ((), ())), preferred_element_type=F32)


def tn(a, b):
    return lax.dot_general(a, b, (((0,), (0,)), ((), ())), preferred_element_type=F32)


def nn(a, b):
    return jnp.dot(a, b, preferred_element_type=F32)


def route_kernel(n, slots, blocks, where, slot_ref, tenant_ref, down_ref, send_ref, pos_ref, out_ref, send_tab, count, sems):
    me = where[0]
    asked = [[slot_ref[tenant_ref[o * blocks + b]] for b in range(blocks)] for o in range(n)]
    for i in range(n * CAP):
        send_tab[i] = -1
    for o in range(n):
        count[o] = 0
    copies = []
    for o in range(n):
        used = jnp.int32(0)
        for slot in asked[o]:
            local = slot - me * slots
            mine = (local >= 0) & (local < slots) & (used < CAP)
            send_tab[jnp.where(mine, o * CAP + used, n * CAP)] = local
            used = used + mine.astype(jnp.int32)
        for r in range(CAP):
            at = o * CAP + r
            copies.append(fetch(down_ref.at[jnp.maximum(send_tab[at], 0)], out_ref.at[o, r], sems.at[at]))
    for b in range(blocks):
        o = slot_ref[tenant_ref[me * blocks + b]] // slots
        pos_ref[b] = o * CAP + count[o]
        count[o] += 1
    for i in range(n * CAP):
        send_ref[i] = send_tab[i]
    for copy in copies:
        copy.wait()


def route(n, where, slot_of_tenant, seq_tenant, down_t, blocks):
    slots, rank, rows = down_t.shape
    return pl.pallas_call(
        functools.partial(route_kernel, n, slots, blocks),
        out_shape=[
            jax.ShapeDtypeStruct((n * CAP,), jnp.int32),
            jax.ShapeDtypeStruct((blocks,), jnp.int32),
            jax.ShapeDtypeStruct((n, CAP, rank, rows), BF),
        ],
        in_specs=[SMEM] * 3 + [ANY],
        out_specs=[SMEM] * 2 + [VMEM],
        scratch_shapes=[pltpu.SMEM((n * CAP + 1,), jnp.int32), pltpu.SMEM((n,), jnp.int32), dmas(n * CAP)],
        compiler_params=params(),
        cost_estimate=cost(0, 4 * n * CAP * rank * rows),
        name="route",
    )(where, slot_of_tenant, seq_tenant, down_t)


def prepare_kernel(blocks, len_ref, mask_ref, gap_ref, adv_ref, live_ref, cols_ref, rows_ref, square):
    length = mask_ref.shape[1]
    square[...] = jnp.zeros_like(square)
    position = lax.broadcasted_iota(jnp.int32, (1, length), 1)
    for b in range(blocks):
        live = (mask_ref[b : b + 1, :] * (position < len_ref[b]).astype(jnp.int32)).astype(F32)
        live_ref[b] = live
        square[b : b + 1, 0:length] = live
    square[blocks : 2 * blocks, 0:length] = gap_ref[...]
    cols_ref[...] = square[...].T[0:length, :]
    lane = lax.broadcasted_iota(jnp.int32, (1, LANES), 1)
    lengths = jnp.ones((1, LANES), F32)
    for b in range(blocks):
        lengths = jnp.where(lane == b, len_ref[b].astype(F32), lengths)
    rows_ref[...] = jnp.zeros_like(rows_ref)
    rows_ref[0:1, :] = lengths
    rows_ref[1:2, 0:blocks] = adv_ref[...]


def prepare(seq_len, mask, gap, advantage):
    blocks, length = mask.shape
    wide = -(-length // LANES) * LANES
    return pl.pallas_call(
        functools.partial(prepare_kernel, blocks),
        out_shape=[
            jax.ShapeDtypeStruct((blocks, 1, length), F32),
            jax.ShapeDtypeStruct((length, LANES), F32),
            jax.ShapeDtypeStruct((8, LANES), F32),
        ],
        in_specs=[SMEM] + [VMEM] * 3,
        out_specs=[VMEM] * 3,
        scratch_shapes=[pltpu.VMEM((LANES, wide), F32)],
        compiler_params=params(),
        cost_estimate=cost(0, 8 * blocks * length),
        name="prepare",
    )(seq_len, mask, gap, advantage)


def frozen_kernel(t, order, halved, where, x_ref, w_ref, *rest):
    x_buf, w_buf, o_buf, x_sem, w_sem, o_sem = rest[-6:]
    outs = rest[-6 - len(order) - halved : -6]
    z = where[1]
    piece = x_ref.shape[0] // t
    sides, _, wide = w_buf.shape
    half = piece // 2
    loads, weights, stores = [], [], []

    def load(i):
        start = pl.multiple_of((z ^ order[i]) * piece, 16)
        loads.append(fetch(x_ref.at[pl.ds(start, piece), :], x_buf.at[i], x_sem.at[i]))

    load(0)
    for side in range(sides):
        cols = pl.ds(side * wide, wide)
        weights.append(fetch(w_ref.at[:, cols], w_buf.at[side], w_sem.at[side]))
    for i in range(1, len(order)):
        load(i)
    for i in range(len(order)):
        loads[i].wait()
        for side in range(sides):
            if i == 0:
                weights[side].wait()
            o_buf[i, :, side * wide : (side + 1) * wide] = nn(x_buf[i], w_buf[side]).astype(BF)
        if i < halved:
            for p in range(2):
                at = 2 * i + p
                stores.append(fetch(o_buf.at[i, pl.ds(p * half, half)], outs[at], o_sem.at[at]))
        else:
            stores.append(fetch(o_buf.at[i], outs[halved + i], o_sem.at[halved + i]))
    for store in stores:
        store.wait()


def frozen(t, order, halved, where, states, weight, after=()):
    tokens, rows = states.shape
    width = weight.shape[1]
    piece = tokens // t
    count = len(order)
    sides = 2
    return pl.pallas_call(
        functools.partial(frozen_kernel, t, order, halved),
        out_shape=[jax.ShapeDtypeStruct((piece // 2, width), BF)] * (2 * halved)
        + [jax.ShapeDtypeStruct((piece, width), BF)] * (count - halved),
        in_specs=[SMEM, ANY, ANY] + [ANY] * len(after),
        out_specs=[ANY] * (count + halved),
        scratch_shapes=[
            pltpu.VMEM((count, piece, rows), BF),
            pltpu.VMEM((sides, rows, width // sides), BF),
            pltpu.VMEM((count, piece, width), BF),
            dmas(count),
            dmas(sides),
            dmas(count + halved),
        ],
        compiler_params=params(),
        cost_estimate=cost(2 * count * piece * rows * width, 2 * (count * piece * rows + rows * width)),
        name="frozen",
    )(where, states, weight, *after)


def pick_up_kernel(n, t, where, send_ref, *rest):
    parts, outs = rest[:t], rest[-n:]
    me, z = where[0], where[1]
    for k in range(n):
        for r in range(CAP):
            slot = jnp.maximum(send_ref[(me ^ k) * CAP + r], 0)
            for d in range(t):
                outs[k][z ^ d, r] = parts[d][slot]


def pick_up(n, t, where, send_tab, parts, after=()):
    slots, rank, cols = parts[0].shape
    return pl.pallas_call(
        functools.partial(pick_up_kernel, n, t),
        out_shape=[jax.ShapeDtypeStruct((t, CAP, rank, cols), BF)] * n,
        in_specs=[SMEM, SMEM] + [VMEM] * t + [ANY] * len(after),
        out_specs=[VMEM] * n,
        compiler_params=params(),
        cost_estimate=cost(0, 4 * n * t * CAP * rank * cols),
        name="pick_up",
    )(where, send_tab, *parts, *after)


def hidden_kernel(t, per, where, pos_ref, down_ref, states_ref, *rest):
    outs, (state_buf, state_sem) = rest[-2 - t : -2], rest[-2:]
    z = where[1]
    rank = down_ref.shape[2]
    order = list(range(t - 1, -1, -1))
    loads = [
        fetch(states_ref.at[pl.ds((z ^ k) * per, per)], state_buf.at[k], state_sem.at[k]) for k in order
    ]
    for i, k in enumerate(order):
        loads[i].wait()
        for h in range(per):
            at = pos_ref[(z ^ k) * per + h]
            panel = down_ref[at // CAP, lax.rem(at, CAP)]
            outs[k][:, h * rank : (h + 1) * rank] = nt(state_buf[k, h], panel)


def hidden_parts(t, where, pos, state_blocks, down_recv, after=()):
    blocks, length, rows = state_blocks.shape
    rank = down_recv.shape[2]
    per = blocks // t
    return pl.pallas_call(
        functools.partial(hidden_kernel, t, per),
        in_specs=[SMEM, SMEM, VMEM] + [ANY] * (1 + len(after)),
        out_specs=[VMEM] * t,
        out_shape=[jax.ShapeDtypeStruct((length, per * rank), F32)] * t,
        scratch_shapes=[pltpu.VMEM((t, per, length, rows), BF), dmas(t)],
        compiler_params=params(),
        cost_estimate=cost(2 * blocks * length * rows * rank, 2 * blocks * rows * (length + rank)),
        name="hidden",
    )(where, pos, down_recv, state_blocks, *after)


def panel_kernel(ks, where, pos_ref, cols_ref, proj_ref, states_ref, *rest):
    outs, (state_buf, grad_buf, state_sem, grad_sem) = rest[-4 - len(ks) : -4], rest[-4:]
    blocks, length, _ = states_ref.shape
    lanes = lax.broadcasted_iota(jnp.int32, (length, LANES), 1)
    columns = cols_ref[...]
    places = [pos_ref[b] for b in range(blocks)]
    rows, loads = [], []
    for i, k in enumerate(ks):
        for r in range(CAP):
            row = jnp.int32(0)
            for b in range(1, blocks):
                row = jnp.where(places[b] == (where[0] ^ k) * CAP + r, b, row)
            rows.append(row)
            at = i * CAP + r
            loads.append(fetch(states_ref.at[row], state_buf.at[at], state_sem.at[at]))
    stores = []
    for i, k in enumerate(ks):
        for r in range(CAP):
            at = i * CAP + r
            live = jnp.sum(jnp.where(lanes == rows[at], columns, 0.0), axis=1, keepdims=True)
            turned = (adapter_scale * live * proj_ref[rows[at]]).T.astype(BF)
            loads[at].wait()
            grad_buf[i, r] = nn(turned, state_buf[at]).astype(BF)
        stores.append(fetch(grad_buf.at[i], outs[i], grad_sem.at[i]))
    for store in stores:
        store.wait()


def panel_grads(ks, where, pos, columns, proj, state_blocks, after=()):
    blocks, length, rank = proj.shape
    rows = state_blocks.shape[2]
    steps = len(ks) * CAP
    return pl.pallas_call(
        functools.partial(panel_kernel, ks),
        in_specs=[SMEM, SMEM, VMEM, VMEM] + [ANY] * (1 + len(after)),
        out_specs=[ANY] * len(ks),
        scratch_shapes=[
            pltpu.VMEM((steps, length, rows), BF),
            pltpu.VMEM((len(ks), CAP, rank, rows), BF),
            dmas(steps),
            dmas(len(ks)),
        ],
        out_shape=[jax.ShapeDtypeStruct((CAP, rank, rows), BF)] * len(ks),
        compiler_params=params(),
        cost_estimate=cost(2 * steps * length * rank * rows, 2 * steps * (length * rows + rank * rows)),
        name="panel_grads",
    )(where, pos, columns, proj, state_blocks, *after)


def thirds(value):
    high = value.astype(BF)
    rest = value - high.astype(F32)
    middle = rest.astype(BF)
    return high, middle, (rest - middle.astype(F32)).astype(BF)


def own_kernel(t, per, rank, blocks, where, proj_ref, cols_ref, rows_ref, *rest):
    parts = rest[:t]
    out_ref, proj_buf, sem = rest[-3:]
    z = where[1]
    load = fetch(proj_ref.at[pl.ds(z * per, per)], proj_buf, sem)
    length = parts[0].shape[0]
    total = parts[0][...]
    for part in parts[1:]:
        total = total + part[...]
    hidden = total.astype(BF)
    out_ref[0:length, 0 : per * rank] = hidden
    lane = lax.broadcasted_iota(jnp.int32, (1, LANES), 1)
    lanes = lax.broadcasted_iota(jnp.int32, (length, LANES), 1)
    columns = cols_ref[...]
    load.wait()
    seq_log = jnp.zeros((1, LANES), F32)
    for h in range(per):
        b = z * per + h
        product = hidden[:, h * rank : (h + 1) * rank].astype(F32) * proj_buf[h]
        live = jnp.sum(jnp.where(lanes == b, columns, 0.0), axis=1, keepdims=True)
        gap = jnp.sum(jnp.where(lanes == b + blocks, columns, 0.0), axis=1, keepdims=True)
        linear = adapter_scale * jnp.sum(product, axis=1, keepdims=True)
        value = jnp.sum(live * (gap + linear), axis=0, keepdims=True)
        seq_log = seq_log + jnp.where(lane == b, value, 0.0)
    seq_log = seq_log / rows_ref[0:1, :]
    row = lax.broadcasted_iota(jnp.int32, (PAD, LANES), 0)
    tail = jnp.zeros((PAD, LANES), F32)
    for i, piece in enumerate(thirds(seq_log)):
        tail = jnp.where(row == i, piece.astype(F32), tail)
    out_ref[length : length + PAD, 0:LANES] = tail.astype(BF)


def own_hidden(t, where, parts, proj, columns, rows, per, rank, after=()):
    length, packed = parts[0].shape
    wide = max(packed, LANES)
    return pl.pallas_call(
        functools.partial(own_kernel, t, per, rank, per * t),
        out_shape=jax.ShapeDtypeStruct((length + PAD, wide), BF),
        in_specs=[SMEM, ANY] + [VMEM] * (2 + t) + [ANY] * len(after),
        out_specs=VMEM,
        scratch_shapes=[pltpu.VMEM((per, length, rank), F32), pltpu.SemaphoreType.DMA],
        compiler_params=params(SMALL_LIMIT),
        cost_estimate=cost(0, 4 * t * length * wide, LATE),
        name="own_hidden",
    )(where, proj, columns, rows, *parts, *after)


def up_grad_kernel(n, t, per, rank, where, pos_ref, sens_ref, cols_ref, rows_ref, *rest):
    msgs = rest[:t]
    factor_ref, loss_ref, ups, stack, sens_buf, sem = rest[-6:]
    z = where[1]
    blocks, length, width = sens_ref.shape
    cols = width // t
    start = pl.multiple_of(z * cols, LANES)
    load = fetch(sens_ref.at[:, :, pl.ds(start, cols)], sens_buf, sem)
    seq_log = jnp.zeros((PAD, LANES), F32)
    for d in range(t):
        stack[z ^ d] = msgs[d][...]
        seq_log = seq_log + msgs[d][length : length + PAD, 0:LANES].astype(F32)
    seq_log = seq_log[0:1] + seq_log[1:2] + seq_log[2:3]
    advantage = rows_ref[1:2, :]
    ratio = jnp.exp(seq_log)
    clipped = jnp.clip(ratio, 1.0 - clip_eps, 1.0 + clip_eps)
    loss_ref[...] = -jnp.minimum(ratio * advantage, clipped * advantage)
    active = ((advantage >= 0) & (ratio <= 1.0 + clip_eps)) | ((advantage < 0) & (ratio >= 1.0 - clip_eps))
    ratio_grad = jnp.where(active, -advantage * ratio, 0.0)
    factor = loss_scale * ratio_grad / rows_ref[0:1, :]
    factor_ref[...] = factor
    row = lax.broadcasted_iota(jnp.int32, (PAD, cols), 0)
    load.wait()
    for b in range(blocks):
        j, h = b // per, b % per
        mine = factor[:, b : b + 1]
        weight = mine * cols_ref[:, b : b + 1]
        out_cot = (weight * sens_buf[b].astype(F32)).astype(BF)
        hidden = stack[j, 0:length, h * rank : (h + 1) * rank]
        at = pos_ref[b]
        at = (at // CAP, lax.rem(at, CAP))
        ups[at[0], at[1], 0:rank, :] = (adapter_scale * tn(hidden, out_cot)).astype(BF)
        tail = jnp.zeros((PAD, cols), F32)
        for i, piece in enumerate(thirds(mine)):
            tail = jnp.where(row == i, piece.astype(F32), tail)
        ups[at[0], at[1], rank : rank + PAD, :] = tail.astype(BF)


def up_grads(n, t, where, pos, sens_blocks, columns, rows, msgs, rank, after=()):
    blocks, length, width = sens_blocks.shape
    cols = width // t
    row = jax.ShapeDtypeStruct((1, LANES), F32)
    out = pl.pallas_call(
        functools.partial(up_grad_kernel, n, t, blocks // t, rank),
        in_specs=[SMEM, SMEM, ANY] + [VMEM] * (2 + t) + [ANY] * len(after),
        out_specs=[VMEM] * 3,
        scratch_shapes=[
            pltpu.VMEM((t,) + msgs[0].shape, BF),
            pltpu.VMEM((blocks, length, cols), BF),
            pltpu.SemaphoreType.DMA,
        ],
        out_shape=[row, row, jax.ShapeDtypeStruct((n, CAP, rank + PAD, cols), BF)],
        compiler_params=params(SMALL_LIMIT),
        cost_estimate=cost(2 * blocks * length * cols * rank, 2 * blocks * length * cols, LATE),
        name="up_grads",
    )(where, pos, sens_blocks, columns, rows, *msgs, *after)
    return out


def back_kernel(n, per, where, pos_ref, sens_ref, w_ref, *rest):
    ups = rest[:n]
    o_ref, proj_ref, own_ref, s_buf, w_buf, o_buf, up_buf, s_sem, w_sem, o_sem, up_sem = rest[-11:]
    me, z = where[0], where[1]
    t = ups[0].shape[0]
    tiles, tile, _ = w_buf.shape
    blocks, length, _ = s_buf.shape
    half = blocks // 2
    loads = [fetch(sens_ref.at[pl.ds(p * half, half)], s_buf.at[pl.ds(p * half, half)], s_sem.at[p]) for p in range(2)]
    weights = [fetch(w_ref.at[pl.ds(0, tile), :], w_buf.at[0], w_sem.at[0])]
    loads += [fetch(ups[k], up_buf.at[me ^ k], up_sem.at[k]) for k in range(n)]
    for i in range(1, tiles):
        weights.append(fetch(w_ref.at[pl.ds(i * tile, tile), :], w_buf.at[i], w_sem.at[i]))

    def panel(at):
        o, r = at // CAP, lax.rem(at, CAP)
        return jnp.concatenate([up_buf[o, c, r] for c in range(t)], axis=1)

    stores = []
    for i in range(tiles):
        weights[i].wait()
        for p in range(2):
            if i == 0:
                loads[p].wait()
            rows = slice(p * half, (p + 1) * half)
            o_buf[i, p * half * length : (p + 1) * half * length, :] = nt(
                s_buf[rows].reshape(half * length, s_buf.shape[2]), w_buf[i]
            ).astype(BF)
        stores.append(fetch(o_buf.at[i], o_ref.at[:, pl.ds(i * tile, tile)], o_sem.at[i]))
    for load in loads[2:]:
        load.wait()
    for b in range(blocks):
        proj_ref[b] = nt(s_buf[b], panel(pos_ref[b]))
    for h in range(per):
        own_ref[h] = panel(pos_ref[z * per + h])
    for store in stores:
        store.wait()


def back(n, where, pos, sens_blocks, weight, ups, after=()):
    blocks, length, width = sens_blocks.shape
    t, _, rank, cols = ups[0].shape
    per = blocks // t
    tokens = blocks * length
    rows = weight.shape[0]
    tiles = max(rows // 512, 1)
    return pl.pallas_call(
        functools.partial(back_kernel, n, per),
        out_shape=[
            jax.ShapeDtypeStruct((tokens, rows), BF),
            jax.ShapeDtypeStruct((blocks, length, rank), F32),
            jax.ShapeDtypeStruct((per, rank, width), BF),
        ],
        in_specs=[SMEM, SMEM] + [ANY] * (2 + n + len(after)),
        out_specs=[ANY, VMEM, VMEM],
        scratch_shapes=[
            pltpu.VMEM((blocks, length, width), BF),
            pltpu.VMEM((tiles, rows // tiles, width), BF),
            pltpu.VMEM((tiles, tokens, rows // tiles), BF),
            pltpu.VMEM((n, t, CAP, rank, cols), BF),
            dmas(2),
            dmas(tiles),
            dmas(tiles),
            dmas(n),
        ],
        compiler_params=params(),
        cost_estimate=cost(2 * tokens * rows * width, 2 * (tokens * (width + rows) + rows * width)),
        name="back",
    )(where, pos, sens_blocks, weight, *ups, *after)


def state_grad_kernel(pos_ref, factor_ref, cols_ref, proj_ref, back_ref, down_ref, o_ref, *rest):
    in_buf, out_buf, in_sem, out_sem = rest
    blocks, length, _ = back_ref.shape
    half = blocks // 2
    loads = []
    for p in range(half):
        some = pl.ds(2 * p, 2)
        loads.append(fetch(back_ref.at[some], in_buf.at[some], in_sem.at[p]))
    weight = factor_ref[...] * cols_ref[...]
    stores = []
    for b in range(blocks):
        if b % 2 == 0:
            loads[b // 2].wait()
        hcot = (adapter_scale * proj_ref[b]).astype(BF)
        at = pos_ref[b]
        total = in_buf[b].astype(F32) + nn(hcot, down_ref[at // CAP, lax.rem(at, CAP)])
        out_buf[b] = (weight[:, b : b + 1] * total).astype(BF)
        if b % 2 == 1:
            some = pl.ds(b - 1, 2)
            stores.append(fetch(out_buf.at[some], o_ref.at[some], out_sem.at[b // 2]))
    for store in stores:
        store.wait()


def state_grad(pos, factor, columns, proj, backward, down_recv):
    blocks, length, rows = backward.shape
    rank = down_recv.shape[2]
    return pl.pallas_call(
        state_grad_kernel,
        out_shape=jax.ShapeDtypeStruct((blocks, length, rows), BF),
        in_specs=[SMEM, VMEM, VMEM, VMEM, ANY, VMEM],
        out_specs=ANY,
        scratch_shapes=[
            pltpu.VMEM((blocks, length, rows), BF),
            pltpu.VMEM((blocks, length, rows), BF),
            dmas(blocks // 2),
            dmas(blocks // 2),
        ],
        compiler_params=params(),
        cost_estimate=cost(2 * blocks * length * rows * rank, 4 * blocks * length * rows, LATE),
        name="state_grad",
    )(pos, factor, columns, proj, backward, down_recv)


def slot_sum_kernel(n, rank, where, send_ref, *rest):
    grads, rest = rest[:n], rest[n:]
    msg_ref, (down_ref, up_ref, acc, up_acc, out_buf, out_sems) = rest[0], rest[-6:]
    me = where[0]
    slots = acc.shape[0]
    acc[...] = jnp.zeros_like(acc)
    up_acc[...] = jnp.zeros_like(up_acc)
    for k in range(n):
        for r in range(CAP):
            slot = send_ref[(me ^ k) * CAP + r]
            used = slot >= 0
            slot = jnp.maximum(slot, 0)
            tail = jnp.sum(msg_ref[me ^ k, r, rank : rank + PAD, 0:LANES].astype(F32), axis=0, keepdims=True)
            part = tail[:, 0:1] * grads[k][r].astype(F32)
            acc[slot] += jnp.where(used, part, 0.0)
            up_acc[slot] += jnp.where(used, msg_ref[me ^ k, r, 0:rank, :].astype(F32), 0.0)
    stores = []
    for s in range(slots):
        out_buf[s] = acc[s].astype(BF)
        stores.append(fetch(out_buf.at[s], down_ref.at[s], out_sems.at[s]))
    up_ref[...] = up_acc[...].astype(BF)
    for store in stores:
        store.wait()


def slot_sum(slots, where, send_tab, grads, msgs, after=()):
    n = len(grads)
    _, rank, rows = grads[0].shape
    cols = msgs.shape[3]
    return pl.pallas_call(
        functools.partial(slot_sum_kernel, n, rank),
        in_specs=[SMEM, SMEM] + [VMEM] * (n + 1) + [ANY] * len(after),
        out_specs=[ANY, VMEM],
        scratch_shapes=[
            pltpu.VMEM((slots, rank, rows), F32),
            pltpu.VMEM((slots, rank, cols), F32),
            pltpu.VMEM((slots, rank, rows), BF),
            dmas(slots),
        ],
        out_shape=[
            jax.ShapeDtypeStruct((slots, rank, rows), BF),
            jax.ShapeDtypeStruct((slots, rank, cols), BF),
        ],
        compiler_params=params(SMALL_LIMIT),
        cost_estimate=cost(0, 2 * (n * CAP + slots) * rank * rows, LATE),
        name="slot_sum",
    )(where, send_tab, *grads, msgs, *after)


def layer_out_kernel(per, whole, halved, msg_ref, up_ref, *rest):
    parts, o_ref = rest[: whole + 2 * halved], rest[-1]
    length = msg_ref.shape[0] - PAD
    rank = up_ref.shape[1]
    piece = o_ref.shape[0]
    for h in range(per):
        hidden = msg_ref[0:length, h * rank : (h + 1) * rank]
        adapter = adapter_scale * nn(hidden, up_ref[h])
        cuts = sorted({h * length, (h + 1) * length} | ({piece // 2} if per == 1 else set()))
        for low, high in zip(cuts[:-1], cuts[1:]):
            total = adapter[low - h * length : high - h * length]
            for part in parts[:whole]:
                total = total + part[low:high, :].astype(F32)
            p = low // (piece // 2)
            base = p * (piece // 2)
            for i in range(halved):
                total = total + parts[whole + 2 * i + p][low - base : high - base, :].astype(F32)
            o_ref[low:high, :] = total.astype(BF)


def layer_out(own_msg, up_own, whole, halves, after=()):
    piece, width = whole[0].shape
    per, rank, _ = up_own.shape
    return pl.pallas_call(
        functools.partial(layer_out_kernel, per, len(whole), len(halves) // 2),
        in_specs=[VMEM] * (2 + len(whole) + len(halves)) + [ANY] * len(after),
        out_specs=VMEM,
        out_shape=jax.ShapeDtypeStruct((piece, width), BF),
        compiler_params=params(),
        cost_estimate=cost(2 * piece * rank * width, 2 * piece * width * (2 + len(whole)), LATE),
        name="layer_out",
    )(own_msg, up_own, *whole, *halves, *after)


def exchange(value, axis):
    return lax.all_to_all(value, axis, 0, 0, tiled=True)


def swap(value, axis, k):
    size = lax.axis_size(axis)
    return lax.ppermute(value, axis, [(i, i ^ k) for i in range(size)])


def shards(
    token_states,
    base_weight,
    adapter_down,
    adapter_up,
    slot_of_tenant,
    seq_tenant,
    seq_len,
    token_mask,
    logp_gap,
    out_sens,
    advantage,
):
    n = lax.axis_size("dp")
    t = lax.axis_size("tensor")
    slots, rows, rank = adapter_down.shape
    width = out_sens.shape[1]
    blocks = seq_len.shape[0]
    length = token_states.shape[0] // blocks
    per = blocks // t
    where = jnp.stack([lax.axis_index("dp"), lax.axis_index("tensor")]).astype(jnp.int32)
    state_blocks = token_states.reshape(blocks, length, rows)
    sens_blocks = out_sens.reshape(blocks, length, width)
    down_t = jnp.swapaxes(adapter_down, 1, 2)

    up_parts = [adapter_up] + [swap(adapter_up, "tensor", k) for k in range(1, t)]
    send_tab, pos, down_send = route(n, where, slot_of_tenant, seq_tenant, down_t, blocks)
    down_recv = exchange(down_send, "dp")
    middle = t // 2
    halved = [middle]
    others = [k for k in range(t - 1, -1, -1) if k not in halved]
    parts = frozen(t, halved + others, 1, where, token_states, base_weight, (down_send, up_parts[1]))
    chunks = dict(zip(others, parts[2:]))
    up_send = pick_up(n, t, where, send_tab, up_parts, (chunks[0],))
    ups = [up_send[0]] + [swap(up_send[k], "dp", k) for k in range(1, n)]
    live, columns, seq_rows = prepare(
        seq_len, token_mask.reshape(blocks, length), logp_gap.reshape(blocks, length), advantage[None]
    )
    hidden = hidden_parts(t, where, pos, state_blocks, down_recv, (up_send[0],))
    hidden = [hidden[0]] + [swap(hidden[k], "tensor", k) for k in range(1, t)]
    early = [swap(parts[0], "tensor", middle)]
    piece, _ = lax.optimization_barrier((parts[1], hidden[1]))
    early.append(swap(piece, "tensor", middle))
    backward, proj, up_own = back(n, where, pos, sens_blocks, base_weight, ups, (hidden[1], early[0]))
    own_msg = own_hidden(t, where, hidden, proj, columns, seq_rows, per, rank)
    msgs = [own_msg] + [swap(own_msg, "tensor", k) for k in range(1, t)]
    far, near = list(range(2, n)), list(range(min(n, 2)))
    grads = dict(zip(far, panel_grads(far, where, pos, columns, proj, state_blocks, (own_msg,))))
    grads |= dict(zip(near, panel_grads(near, where, pos, columns, proj, state_blocks, (*msgs[1:], early[1]))))
    grads_in = [grads[0]] + [swap(grads[k], "dp", k) for k in range(1, n)]
    factor, loss, up_out = up_grads(n, t, where, pos, sens_blocks, columns, seq_rows, msgs, rank)
    up_in = exchange(up_out, "dp")
    token_state_gradient = state_grad(
        pos, factor, columns, proj, backward.reshape(blocks, length, rows), down_recv
    )
    late = {}
    for k in others[:-1]:
        piece, _ = lax.optimization_barrier((chunks[k], msgs[1:]))
        late[k] = swap(piece, "tensor", k)
    whole = [chunks[0]] + [late[k] for k in others[:-1]]
    out = layer_out(own_msg, up_own, whole, early)
    down_grad, up_grad = slot_sum(slots, where, send_tab, grads_in, up_in, (out,))
    return (
        out,
        loss[0, :blocks],
        token_state_gradient.reshape(blocks * length, rows),
        jnp.swapaxes(down_grad, 1, 2),
        up_grad,
    )


def solution(mesh):
    in_specs = (
        P(("groups", "dp"), "tensor"),
        P("tensor", None),
        P(("groups", "dp"), "tensor", None),
        P(("groups", "dp"), None, "tensor"),
        P("groups"),
        P("groups"),
        P(("groups", "dp")),
        P(("groups", "dp")),
        P(("groups", "dp")),
        P(("groups", "dp"), None),
        P(("groups", "dp")),
    )
    out_specs = (
        P(("groups", "dp", "tensor"), None),
        P(("groups", "dp")),
        P(("groups", "dp"), "tensor"),
        P(("groups", "dp"), "tensor", None),
        P(("groups", "dp"), None, "tensor"),
    )
    return jax.shard_map(shards, mesh=mesh, in_specs=in_specs, out_specs=out_specs, check_vma=False)
```

```python
import functools

import jax
import jax.numpy as jnp
from jax import lax
from jax.experimental import pallas as pl
from jax.experimental.pallas import tpu as pltpu
from jax.sharding import PartitionSpec as P

CAP = 2
PAD = 16
LATE = 16
LANES = 128

adapter_scale = 2.0
loss_scale = 1024.0
clip_eps = 0.2

BF = jnp.bfloat16
F32 = jnp.float32
VMEM_LIMIT = 58 * 1024 * 1024
SMALL_LIMIT = 20 * 1024 * 1024

ANY = pl.BlockSpec(memory_space=pl.ANY)
SMEM = pl.BlockSpec(memory_space=pltpu.SMEM)
VMEM = pl.BlockSpec(memory_space=pltpu.VMEM)


def params(limit=VMEM_LIMIT):
    return pltpu.CompilerParams(vmem_limit_bytes=limit)


def cost(flops, nbytes, share=1):
    return pl.CostEstimate(flops=int(flops) // share, bytes_accessed=int(nbytes) // share, transcendentals=0)


def fetch(source, target, sem):
    copy = pltpu.make_async_copy(source, target, sem)
    copy.start()
    return copy


def dmas(count):
    return pltpu.SemaphoreType.DMA((count,))


def nt(a, b):
    return lax.dot_general(a, b, (((1,), (1,)), ((), ())), preferred_element_type=F32)


def tn(a, b):
    return lax.dot_general(a, b, (((0,), (0,)), ((), ())), preferred_element_type=F32)


def nn(a, b):
    return jnp.dot(a, b, preferred_element_type=F32)


def route_kernel(n, slots, blocks, where, slot_ref, tenant_ref, down_ref, send_ref, pos_ref, out_ref, send_tab, count, sems):
    me = where[0]
    asked = [[slot_ref[tenant_ref[o * blocks + b]] for b in range(blocks)] for o in range(n)]
    for i in range(n * CAP):
        send_tab[i] = -1
    for o in range(n):
        count[o] = 0
    copies = []
    for o in range(n):
        used = jnp.int32(0)
        for slot in asked[o]:
            local = slot - me * slots
            mine = (local >= 0) & (local < slots) & (used < CAP)
            send_tab[jnp.where(mine, o * CAP + used, n * CAP)] = local
            used = used + mine.astype(jnp.int32)
        for r in range(CAP):
            at = o * CAP + r
            copies.append(fetch(down_ref.at[jnp.maximum(send_tab[at], 0)], out_ref.at[o, r], sems.at[at]))
    for b in range(blocks):
        o = slot_ref[tenant_ref[me * blocks + b]] // slots
        pos_ref[b] = o * CAP + count[o]
        count[o] += 1
    for i in range(n * CAP):
        send_ref[i] = send_tab[i]
    for copy in copies:
        copy.wait()


def route(n, where, slot_of_tenant, seq_tenant, down_t, blocks):
    slots, rank, rows = down_t.shape
    return pl.pallas_call(
        functools.partial(route_kernel, n, slots, blocks),
        out_shape=[
            jax.ShapeDtypeStruct((n * CAP,), jnp.int32),
            jax.ShapeDtypeStruct((blocks,), jnp.int32),
            jax.ShapeDtypeStruct((n, CAP, rank, rows), BF),
        ],
        in_specs=[SMEM] * 3 + [ANY],
        out_specs=[SMEM] * 2 + [VMEM],
        scratch_shapes=[pltpu.SMEM((n * CAP + 1,), jnp.int32), pltpu.SMEM((n,), jnp.int32), dmas(n * CAP)],
        compiler_params=params(),
        cost_estimate=cost(0, 4 * n * CAP * rank * rows),
        name="route",
    )(where, slot_of_tenant, seq_tenant, down_t)


def prepare_kernel(blocks, len_ref, mask_ref, gap_ref, adv_ref, live_ref, cols_ref, rows_ref, square):
    length = mask_ref.shape[1]
    square[...] = jnp.zeros_like(square)
    position = lax.broadcasted_iota(jnp.int32, (1, length), 1)
    for b in range(blocks):
        live = (mask_ref[b : b + 1, :] * (position < len_ref[b]).astype(jnp.int32)).astype(F32)
        live_ref[b] = live
        square[b : b + 1, 0:length] = live
    square[blocks : 2 * blocks, 0:length] = gap_ref[...]
    cols_ref[...] = square[...].T[0:length, :]
    lane = lax.broadcasted_iota(jnp.int32, (1, LANES), 1)
    lengths = jnp.ones((1, LANES), F32)
    for b in range(blocks):
        lengths = jnp.where(lane == b, len_ref[b].astype(F32), lengths)
    rows_ref[...] = jnp.zeros_like(rows_ref)
    rows_ref[0:1, :] = lengths
    rows_ref[1:2, 0:blocks] = adv_ref[...]


def prepare(seq_len, mask, gap, advantage):
    blocks, length = mask.shape
    wide = -(-length // LANES) * LANES
    return pl.pallas_call(
        functools.partial(prepare_kernel, blocks),
        out_shape=[
            jax.ShapeDtypeStruct((blocks, 1, length), F32),
            jax.ShapeDtypeStruct((length, LANES), F32),
            jax.ShapeDtypeStruct((8, LANES), F32),
        ],
        in_specs=[SMEM] + [VMEM] * 3,
        out_specs=[VMEM] * 3,
        scratch_shapes=[pltpu.VMEM((LANES, wide), F32)],
        compiler_params=params(),
        cost_estimate=cost(0, 8 * blocks * length),
        name="prepare",
    )(seq_len, mask, gap, advantage)


def frozen_kernel(t, order, halved, where, x_ref, w_ref, *rest):
    x_buf, w_buf, o_buf, x_sem, w_sem, o_sem = rest[-6:]
    outs = rest[-6 - len(order) - halved : -6]
    z = where[1]
    piece = x_ref.shape[0] // t
    sides, _, wide = w_buf.shape
    half = piece // 2
    loads, weights, stores = [], [], []

    def load(i):
        start = pl.multiple_of((z ^ order[i]) * piece, 16)
        loads.append(fetch(x_ref.at[pl.ds(start, piece), :], x_buf.at[i], x_sem.at[i]))

    load(0)
    for side in range(sides):
        cols = pl.ds(side * wide, wide)
        weights.append(fetch(w_ref.at[:, cols], w_buf.at[side], w_sem.at[side]))
    for i in range(1, len(order)):
        load(i)
    for i in range(len(order)):
        loads[i].wait()
        for side in range(sides):
            if i == 0:
                weights[side].wait()
            o_buf[i, :, side * wide : (side + 1) * wide] = nn(x_buf[i], w_buf[side]).astype(BF)
        if i < halved:
            for p in range(2):
                at = 2 * i + p
                stores.append(fetch(o_buf.at[i, pl.ds(p * half, half)], outs[at], o_sem.at[at]))
        else:
            stores.append(fetch(o_buf.at[i], outs[halved + i], o_sem.at[halved + i]))
    for store in stores:
        store.wait()


def frozen(t, order, halved, where, states, weight, after=()):
    tokens, rows = states.shape
    width = weight.shape[1]
    piece = tokens // t
    count = len(order)
    sides = 2
    return pl.pallas_call(
        functools.partial(frozen_kernel, t, order, halved),
        out_shape=[jax.ShapeDtypeStruct((piece // 2, width), BF)] * (2 * halved)
        + [jax.ShapeDtypeStruct((piece, width), BF)] * (count - halved),
        in_specs=[SMEM, ANY, ANY] + [ANY] * len(after),
        out_specs=[ANY] * (count + halved),
        scratch_shapes=[
            pltpu.VMEM((count, piece, rows), BF),
            pltpu.VMEM((sides, rows, width // sides), BF),
            pltpu.VMEM((count, piece, width), BF),
            dmas(count),
            dmas(sides),
            dmas(count + halved),
        ],
        compiler_params=params(),
        cost_estimate=cost(2 * count * piece * rows * width, 2 * (count * piece * rows + rows * width)),
        name="frozen",
    )(where, states, weight, *after)


def pick_up_kernel(n, t, where, send_ref, *rest):
    parts, outs = rest[:t], rest[-n:]
    me, z = where[0], where[1]
    for k in range(n):
        for r in range(CAP):
            slot = jnp.maximum(send_ref[(me ^ k) * CAP + r], 0)
            for d in range(t):
                outs[k][z ^ d, r] = parts[d][slot]


def pick_up(n, t, where, send_tab, parts, after=()):
    slots, rank, cols = parts[0].shape
    return pl.pallas_call(
        functools.partial(pick_up_kernel, n, t),
        out_shape=[jax.ShapeDtypeStruct((t, CAP, rank, cols), BF)] * n,
        in_specs=[SMEM, SMEM] + [VMEM] * t + [ANY] * len(after),
        out_specs=[VMEM] * n,
        compiler_params=params(),
        cost_estimate=cost(0, 4 * n * t * CAP * rank * cols),
        name="pick_up",
    )(where, send_tab, *parts, *after)


def hidden_kernel(t, per, where, pos_ref, down_ref, states_ref, *rest):
    outs, (state_buf, state_sem) = rest[-2 - t : -2], rest[-2:]
    z = where[1]
    rank = down_ref.shape[2]
    order = list(range(t - 1, -1, -1))
    loads = [
        fetch(states_ref.at[pl.ds((z ^ k) * per, per)], state_buf.at[k], state_sem.at[k]) for k in order
    ]
    for i, k in enumerate(order):
        loads[i].wait()
        for h in range(per):
            at = pos_ref[(z ^ k) * per + h]
            panel = down_ref[at // CAP, lax.rem(at, CAP)]
            outs[k][:, h * rank : (h + 1) * rank] = nt(state_buf[k, h], panel)


def hidden_parts(t, where, pos, state_blocks, down_recv, after=()):
    blocks, length, rows = state_blocks.shape
    rank = down_recv.shape[2]
    per = blocks // t
    return pl.pallas_call(
        functools.partial(hidden_kernel, t, per),
        in_specs=[SMEM, SMEM, VMEM] + [ANY] * (1 + len(after)),
        out_specs=[VMEM] * t,
        out_shape=[jax.ShapeDtypeStruct((length, per * rank), F32)] * t,
        scratch_shapes=[pltpu.VMEM((t, per, length, rows), BF), dmas(t)],
        compiler_params=params(),
        cost_estimate=cost(2 * blocks * length * rows * rank, 2 * blocks * rows * (length + rank)),
        name="hidden",
    )(where, pos, down_recv, state_blocks, *after)


def panel_kernel(ks, where, pos_ref, cols_ref, proj_ref, states_ref, *rest):
    outs, (state_buf, grad_buf, state_sem, grad_sem) = rest[-4 - len(ks) : -4], rest[-4:]
    blocks, length, _ = states_ref.shape
    lanes = lax.broadcasted_iota(jnp.int32, (length, LANES), 1)
    columns = cols_ref[...]
    places = [pos_ref[b] for b in range(blocks)]
    rows, loads = [], []
    for i, k in enumerate(ks):
        for r in range(CAP):
            row = jnp.int32(0)
            for b in range(1, blocks):
                row = jnp.where(places[b] == (where[0] ^ k) * CAP + r, b, row)
            rows.append(row)
            at = i * CAP + r
            loads.append(fetch(states_ref.at[row], state_buf.at[at], state_sem.at[at]))
    stores = []
    for i, k in enumerate(ks):
        for r in range(CAP):
            at = i * CAP + r
            live = jnp.sum(jnp.where(lanes == rows[at], columns, 0.0), axis=1, keepdims=True)
            turned = (adapter_scale * live * proj_ref[rows[at]]).T.astype(BF)
            loads[at].wait()
            grad_buf[i, r] = nn(turned, state_buf[at]).astype(BF)
        stores.append(fetch(grad_buf.at[i], outs[i], grad_sem.at[i]))
    for store in stores:
        store.wait()


def panel_grads(ks, where, pos, columns, proj, state_blocks, after=()):
    blocks, length, rank = proj.shape
    rows = state_blocks.shape[2]
    steps = len(ks) * CAP
    return pl.pallas_call(
        functools.partial(panel_kernel, ks),
        in_specs=[SMEM, SMEM, VMEM, VMEM] + [ANY] * (1 + len(after)),
        out_specs=[ANY] * len(ks),
        scratch_shapes=[
            pltpu.VMEM((steps, length, rows), BF),
            pltpu.VMEM((len(ks), CAP, rank, rows), BF),
            dmas(steps),
            dmas(len(ks)),
        ],
        out_shape=[jax.ShapeDtypeStruct((CAP, rank, rows), BF)] * len(ks),
        compiler_params=params(SMALL_LIMIT),
        cost_estimate=cost(2 * steps * length * rank * rows, 2 * steps * (length * rows + rank * rows)),
        name="panel_grads",
    )(where, pos, columns, proj, state_blocks, *after)


def thirds(value):
    high = value.astype(BF)
    rest = value - high.astype(F32)
    middle = rest.astype(BF)
    return high, middle, (rest - middle.astype(F32)).astype(BF)


def own_kernel(t, per, rank, blocks, where, proj_ref, cols_ref, rows_ref, *rest):
    parts = rest[:t]
    out_ref, proj_buf, sem = rest[-3:]
    z = where[1]
    load = fetch(proj_ref.at[pl.ds(z * per, per)], proj_buf, sem)
    length = parts[0].shape[0]
    total = parts[0][...]
    for part in parts[1:]:
        total = total + part[...]
    hidden = total.astype(BF)
    out_ref[0:length, 0 : per * rank] = hidden
    lane = lax.broadcasted_iota(jnp.int32, (1, LANES), 1)
    lanes = lax.broadcasted_iota(jnp.int32, (length, LANES), 1)
    columns = cols_ref[...]
    load.wait()
    seq_log = jnp.zeros((1, LANES), F32)
    for h in range(per):
        b = z * per + h
        product = hidden[:, h * rank : (h + 1) * rank].astype(F32) * proj_buf[h]
        live = jnp.sum(jnp.where(lanes == b, columns, 0.0), axis=1, keepdims=True)
        gap = jnp.sum(jnp.where(lanes == b + blocks, columns, 0.0), axis=1, keepdims=True)
        linear = adapter_scale * jnp.sum(product, axis=1, keepdims=True)
        value = jnp.sum(live * (gap + linear), axis=0, keepdims=True)
        seq_log = seq_log + jnp.where(lane == b, value, 0.0)
    seq_log = seq_log / rows_ref[0:1, :]
    row = lax.broadcasted_iota(jnp.int32, (PAD, LANES), 0)
    tail = jnp.zeros((PAD, LANES), F32)
    for i, piece in enumerate(thirds(seq_log)):
        tail = jnp.where(row == i, piece.astype(F32), tail)
    out_ref[length : length + PAD, 0:LANES] = tail.astype(BF)


def own_hidden(t, where, parts, proj, columns, rows, per, rank, after=()):
    length, packed = parts[0].shape
    wide = max(packed, LANES)
    return pl.pallas_call(
        functools.partial(own_kernel, t, per, rank, per * t),
        out_shape=jax.ShapeDtypeStruct((length + PAD, wide), BF),
        in_specs=[SMEM, ANY] + [VMEM] * (2 + t) + [ANY] * len(after),
        out_specs=VMEM,
        scratch_shapes=[pltpu.VMEM((per, length, rank), F32), pltpu.SemaphoreType.DMA],
        compiler_params=params(SMALL_LIMIT),
        cost_estimate=cost(0, 4 * t * length * wide, LATE),
        name="own_hidden",
    )(where, proj, columns, rows, *parts, *after)


def up_grad_kernel(n, t, per, rank, where, pos_ref, sens_ref, cols_ref, rows_ref, *rest):
    msgs = rest[:t]
    factor_ref, loss_ref, ups, stack, sens_buf, sem = rest[-6:]
    z = where[1]
    blocks, length, width = sens_ref.shape
    cols = width // t
    start = pl.multiple_of(z * cols, LANES)
    load = fetch(sens_ref.at[:, :, pl.ds(start, cols)], sens_buf, sem)
    seq_log = jnp.zeros((PAD, LANES), F32)
    for d in range(t):
        stack[z ^ d] = msgs[d][...]
        seq_log = seq_log + msgs[d][length : length + PAD, 0:LANES].astype(F32)
    seq_log = seq_log[0:1] + seq_log[1:2] + seq_log[2:3]
    advantage = rows_ref[1:2, :]
    ratio = jnp.exp(seq_log)
    clipped = jnp.clip(ratio, 1.0 - clip_eps, 1.0 + clip_eps)
    loss_ref[...] = -jnp.minimum(ratio * advantage, clipped * advantage)
    active = ((advantage >= 0) & (ratio <= 1.0 + clip_eps)) | ((advantage < 0) & (ratio >= 1.0 - clip_eps))
    ratio_grad = jnp.where(active, -advantage * ratio, 0.0)
    factor = loss_scale * ratio_grad / rows_ref[0:1, :]
    factor_ref[...] = factor
    row = lax.broadcasted_iota(jnp.int32, (PAD, cols), 0)
    load.wait()
    for b in range(blocks):
        j, h = b // per, b % per
        mine = factor[:, b : b + 1]
        weight = mine * cols_ref[:, b : b + 1]
        out_cot = (weight * sens_buf[b].astype(F32)).astype(BF)
        hidden = stack[j, 0:length, h * rank : (h + 1) * rank]
        at = pos_ref[b]
        at = (at // CAP, lax.rem(at, CAP))
        ups[at[0], at[1], 0:rank, :] = (adapter_scale * tn(hidden, out_cot)).astype(BF)
        tail = jnp.zeros((PAD, cols), F32)
        for i, piece in enumerate(thirds(mine)):
            tail = jnp.where(row == i, piece.astype(F32), tail)
        ups[at[0], at[1], rank : rank + PAD, :] = tail.astype(BF)


def up_grads(n, t, where, pos, sens_blocks, columns, rows, msgs, rank, after=()):
    blocks, length, width = sens_blocks.shape
    cols = width // t
    row = jax.ShapeDtypeStruct((1, LANES), F32)
    out = pl.pallas_call(
        functools.partial(up_grad_kernel, n, t, blocks // t, rank),
        in_specs=[SMEM, SMEM, ANY] + [VMEM] * (2 + t) + [ANY] * len(after),
        out_specs=[VMEM] * 3,
        scratch_shapes=[
            pltpu.VMEM((t,) + msgs[0].shape, BF),
            pltpu.VMEM((blocks, length, cols), BF),
            pltpu.SemaphoreType.DMA,
        ],
        out_shape=[row, row, jax.ShapeDtypeStruct((n, CAP, rank + PAD, cols), BF)],
        compiler_params=params(SMALL_LIMIT),
        cost_estimate=cost(2 * blocks * length * cols * rank, 2 * blocks * length * cols, LATE),
        name="up_grads",
    )(where, pos, sens_blocks, columns, rows, *msgs, *after)
    return out


def back_kernel(n, per, where, pos_ref, sens_ref, w_ref, *rest):
    ups = rest[:n]
    o_ref, proj_ref, own_ref, s_buf, w_buf, o_buf, up_buf, s_sem, w_sem, o_sem, up_sem = rest[-11:]
    me, z = where[0], where[1]
    t = ups[0].shape[0]
    tiles, tile, _ = w_buf.shape
    blocks, length, _ = s_buf.shape
    half = blocks // 2
    loads = [fetch(sens_ref.at[pl.ds(p * half, half)], s_buf.at[pl.ds(p * half, half)], s_sem.at[p]) for p in range(2)]
    weights = [fetch(w_ref.at[pl.ds(0, tile), :], w_buf.at[0], w_sem.at[0])]
    loads += [fetch(ups[k], up_buf.at[me ^ k], up_sem.at[k]) for k in range(n)]
    for i in range(1, tiles):
        weights.append(fetch(w_ref.at[pl.ds(i * tile, tile), :], w_buf.at[i], w_sem.at[i]))

    def panel(at):
        o, r = at // CAP, lax.rem(at, CAP)
        return jnp.concatenate([up_buf[o, c, r] for c in range(t)], axis=1)

    stores = []
    for i in range(tiles):
        weights[i].wait()
        for p in range(2):
            if i == 0:
                loads[p].wait()
            rows = slice(p * half, (p + 1) * half)
            o_buf[i, p * half * length : (p + 1) * half * length, :] = nt(
                s_buf[rows].reshape(half * length, s_buf.shape[2]), w_buf[i]
            ).astype(BF)
        stores.append(fetch(o_buf.at[i], o_ref.at[:, pl.ds(i * tile, tile)], o_sem.at[i]))
    for load in loads[2:]:
        load.wait()
    for b in range(blocks):
        proj_ref[b] = nt(s_buf[b], panel(pos_ref[b]))
    for h in range(per):
        own_ref[h] = panel(pos_ref[z * per + h])
    for store in stores:
        store.wait()


def back(n, where, pos, sens_blocks, weight, ups, after=()):
    blocks, length, width = sens_blocks.shape
    t, _, rank, cols = ups[0].shape
    per = blocks // t
    tokens = blocks * length
    rows = weight.shape[0]
    tiles = max(rows // 512, 1)
    return pl.pallas_call(
        functools.partial(back_kernel, n, per),
        out_shape=[
            jax.ShapeDtypeStruct((tokens, rows), BF),
            jax.ShapeDtypeStruct((blocks, length, rank), F32),
            jax.ShapeDtypeStruct((per, rank, width), BF),
        ],
        in_specs=[SMEM, SMEM] + [ANY] * (2 + n + len(after)),
        out_specs=[ANY, VMEM, VMEM],
        scratch_shapes=[
            pltpu.VMEM((blocks, length, width), BF),
            pltpu.VMEM((tiles, rows // tiles, width), BF),
            pltpu.VMEM((tiles, tokens, rows // tiles), BF),
            pltpu.VMEM((n, t, CAP, rank, cols), BF),
            dmas(2),
            dmas(tiles),
            dmas(tiles),
            dmas(n),
        ],
        compiler_params=params(),
        cost_estimate=cost(2 * tokens * rows * width, 2 * (tokens * (width + rows) + rows * width)),
        name="back",
    )(where, pos, sens_blocks, weight, *ups, *after)


def state_grad_kernel(pos_ref, factor_ref, cols_ref, proj_ref, back_ref, down_ref, o_ref, *rest):
    in_buf, out_buf, in_sem, out_sem = rest
    blocks, length, _ = back_ref.shape
    half = blocks // 2
    loads = []
    for p in range(half):
        some = pl.ds(2 * p, 2)
        loads.append(fetch(back_ref.at[some], in_buf.at[some], in_sem.at[p]))
    weight = factor_ref[...] * cols_ref[...]
    stores = []
    for b in range(blocks):
        if b % 2 == 0:
            loads[b // 2].wait()
        hcot = (adapter_scale * proj_ref[b]).astype(BF)
        at = pos_ref[b]
        total = in_buf[b].astype(F32) + nn(hcot, down_ref[at // CAP, lax.rem(at, CAP)])
        out_buf[b] = (weight[:, b : b + 1] * total).astype(BF)
        if b % 2 == 1:
            some = pl.ds(b - 1, 2)
            stores.append(fetch(out_buf.at[some], o_ref.at[some], out_sem.at[b // 2]))
    for store in stores:
        store.wait()


def state_grad(pos, factor, columns, proj, backward, down_recv):
    blocks, length, rows = backward.shape
    rank = down_recv.shape[2]
    return pl.pallas_call(
        state_grad_kernel,
        out_shape=jax.ShapeDtypeStruct((blocks, length, rows), BF),
        in_specs=[SMEM, VMEM, VMEM, VMEM, ANY, VMEM],
        out_specs=ANY,
        scratch_shapes=[
            pltpu.VMEM((blocks, length, rows), BF),
            pltpu.VMEM((blocks, length, rows), BF),
            dmas(blocks // 2),
            dmas(blocks // 2),
        ],
        compiler_params=params(),
        cost_estimate=cost(2 * blocks * length * rows * rank, 4 * blocks * length * rows, LATE),
        name="state_grad",
    )(pos, factor, columns, proj, backward, down_recv)


def slot_sum_kernel(n, rank, where, send_ref, *rest):
    grads, rest = rest[:n], rest[n:]
    msg_ref, (down_ref, up_ref, acc, up_acc, out_buf, out_sems) = rest[0], rest[-6:]
    me = where[0]
    slots = acc.shape[0]
    acc[...] = jnp.zeros_like(acc)
    up_acc[...] = jnp.zeros_like(up_acc)
    for k in range(n):
        for r in range(CAP):
            slot = send_ref[(me ^ k) * CAP + r]
            used = slot >= 0
            slot = jnp.maximum(slot, 0)
            tail = jnp.sum(msg_ref[me ^ k, r, rank : rank + PAD, 0:LANES].astype(F32), axis=0, keepdims=True)
            part = tail[:, 0:1] * grads[k][r].astype(F32)
            acc[slot] += jnp.where(used, part, 0.0)
            up_acc[slot] += jnp.where(used, msg_ref[me ^ k, r, 0:rank, :].astype(F32), 0.0)
    stores = []
    for s in range(slots):
        out_buf[s] = acc[s].astype(BF)
        stores.append(fetch(out_buf.at[s], down_ref.at[s], out_sems.at[s]))
    up_ref[...] = up_acc[...].astype(BF)
    for store in stores:
        store.wait()


def slot_sum(slots, where, send_tab, grads, msgs, after=()):
    n = len(grads)
    _, rank, rows = grads[0].shape
    cols = msgs.shape[3]
    return pl.pallas_call(
        functools.partial(slot_sum_kernel, n, rank),
        in_specs=[SMEM, SMEM] + [VMEM] * (n + 1) + [ANY] * len(after),
        out_specs=[ANY, VMEM],
        scratch_shapes=[
            pltpu.VMEM((slots, rank, rows), F32),
            pltpu.VMEM((slots, rank, cols), F32),
            pltpu.VMEM((slots, rank, rows), BF),
            dmas(slots),
        ],
        out_shape=[
            jax.ShapeDtypeStruct((slots, rank, rows), BF),
            jax.ShapeDtypeStruct((slots, rank, cols), BF),
        ],
        compiler_params=params(SMALL_LIMIT),
        cost_estimate=cost(0, 2 * (n * CAP + slots) * rank * rows, LATE),
        name="slot_sum",
    )(where, send_tab, *grads, msgs, *after)


def layer_out_kernel(per, whole, halved, msg_ref, up_ref, *rest):
    parts, o_ref = rest[: whole + 2 * halved], rest[-1]
    length = msg_ref.shape[0] - PAD
    rank = up_ref.shape[1]
    piece = o_ref.shape[0]
    for h in range(per):
        hidden = msg_ref[0:length, h * rank : (h + 1) * rank]
        adapter = adapter_scale * nn(hidden, up_ref[h])
        cuts = sorted({h * length, (h + 1) * length} | ({piece // 2} if per == 1 else set()))
        for low, high in zip(cuts[:-1], cuts[1:]):
            total = adapter[low - h * length : high - h * length]
            for part in parts[:whole]:
                total = total + part[low:high, :].astype(F32)
            p = low // (piece // 2)
            base = p * (piece // 2)
            for i in range(halved):
                total = total + parts[whole + 2 * i + p][low - base : high - base, :].astype(F32)
            o_ref[low:high, :] = total.astype(BF)


def layer_out(own_msg, up_own, whole, halves, after=()):
    piece, width = whole[0].shape
    per, rank, _ = up_own.shape
    return pl.pallas_call(
        functools.partial(layer_out_kernel, per, len(whole), len(halves) // 2),
        in_specs=[VMEM] * (2 + len(whole) + len(halves)) + [ANY] * len(after),
        out_specs=VMEM,
        out_shape=jax.ShapeDtypeStruct((piece, width), BF),
        compiler_params=params(),
        cost_estimate=cost(2 * piece * rank * width, 2 * piece * width * (2 + len(whole)), LATE),
        name="layer_out",
    )(own_msg, up_own, *whole, *halves, *after)


def exchange(value, axis):
    return lax.all_to_all(value, axis, 0, 0, tiled=True)


def swap(value, axis, k):
    size = lax.axis_size(axis)
    return lax.ppermute(value, axis, [(i, i ^ k) for i in range(size)])


def shards(
    token_states,
    base_weight,
    adapter_down,
    adapter_up,
    slot_of_tenant,
    seq_tenant,
    seq_len,
    token_mask,
    logp_gap,
    out_sens,
    advantage,
):
    n = lax.axis_size("dp")
    t = lax.axis_size("tensor")
    slots, rows, rank = adapter_down.shape
    width = out_sens.shape[1]
    blocks = seq_len.shape[0]
    length = token_states.shape[0] // blocks
    per = blocks // t
    where = jnp.stack([lax.axis_index("dp"), lax.axis_index("tensor")]).astype(jnp.int32)
    state_blocks = token_states.reshape(blocks, length, rows)
    sens_blocks = out_sens.reshape(blocks, length, width)
    down_t = jnp.swapaxes(adapter_down, 1, 2)

    up_parts = [adapter_up] + [swap(adapter_up, "tensor", k) for k in range(1, t)]
    send_tab, pos, down_send = route(n, where, slot_of_tenant, seq_tenant, down_t, blocks)
    down_recv = exchange(down_send, "dp")
    middle = t // 2
    halved = [middle]
    others = [k for k in range(t - 1, -1, -1) if k not in halved]
    parts = frozen(t, halved + others, 1, where, token_states, base_weight, (down_send, up_parts[1]))
    chunks = dict(zip(others, parts[2:]))
    up_send = pick_up(n, t, where, send_tab, up_parts, (chunks[0],))
    ups = [up_send[0]] + [swap(up_send[k], "dp", k) for k in range(1, n)]
    live, columns, seq_rows = prepare(
        seq_len, token_mask.reshape(blocks, length), logp_gap.reshape(blocks, length), advantage[None]
    )
    hidden = hidden_parts(t, where, pos, state_blocks, down_recv, (up_send[0],))
    hidden = [hidden[0]] + [swap(hidden[k], "tensor", k) for k in range(1, t)]
    early = [swap(parts[0], "tensor", middle)]
    piece, _ = lax.optimization_barrier((parts[1], hidden[1]))
    early.append(swap(piece, "tensor", middle))
    backward, proj, up_own = back(n, where, pos, sens_blocks, base_weight, ups, (hidden[1], early[0]))
    own_msg = own_hidden(t, where, hidden, proj, columns, seq_rows, per, rank)
    msgs = [own_msg] + [swap(own_msg, "tensor", k) for k in range(1, t)]
    far, near = list(range(2, n)), list(range(min(n, 2)))
    grads = dict(zip(far, panel_grads(far, where, pos, columns, proj, state_blocks, (own_msg,))))
    grads |= dict(zip(near, panel_grads(near, where, pos, columns, proj, state_blocks, (*msgs[1:], early[1]))))
    grads_in = [grads[0]] + [swap(grads[k], "dp", k) for k in range(1, n)]
    factor, loss, up_out = up_grads(n, t, where, pos, sens_blocks, columns, seq_rows, msgs, rank)
    up_in = exchange(up_out, "dp")
    token_state_gradient = state_grad(
        pos, factor, columns, proj, backward.reshape(blocks, length, rows), down_recv
    )
    late = {}
    for k in others[:-1]:
        piece, _ = lax.optimization_barrier((chunks[k], (msgs[1:], [grads[i] for i in far])))
        late[k] = swap(piece, "tensor", k)
    whole = [chunks[0]] + [late[k] for k in others[:-1]]
    down_grad, up_grad = slot_sum(slots, where, send_tab, grads_in, up_in)
    out = layer_out(own_msg, up_own, whole, early, (up_grad,))
    return (
        out,
        loss[0, :blocks],
        token_state_gradient.reshape(blocks * length, rows),
        jnp.swapaxes(down_grad, 1, 2),
        up_grad,
    )


def solution(mesh):
    in_specs = (
        P(("groups", "dp"), "tensor"),
        P("tensor", None),
        P(("groups", "dp"), "tensor", None),
        P(("groups", "dp"), None, "tensor"),
        P("groups"),
        P("groups"),
        P(("groups", "dp")),
        P(("groups", "dp")),
        P(("groups", "dp")),
        P(("groups", "dp"), None),
        P(("groups", "dp")),
    )
    out_specs = (
        P(("groups", "dp", "tensor"), None),
        P(("groups", "dp")),
        P(("groups", "dp"), "tensor"),
        P(("groups", "dp"), "tensor", None),
        P(("groups", "dp"), None, "tensor"),
    )
    return jax.shard_map(shards, mesh=mesh, in_specs=in_specs, out_specs=out_specs, check_vma=False)
```

```python
import functools

import jax
import jax.numpy as jnp
from jax import lax
from jax.experimental import pallas as pl
from jax.experimental.pallas import tpu as pltpu
from jax.sharding import PartitionSpec as P

CAP = 2
PAD = 16
LATE = 16
LANES = 128

adapter_scale = 2.0
loss_scale = 1024.0
clip_eps = 0.2

BF = jnp.bfloat16
F32 = jnp.float32
VMEM_LIMIT = 58 * 1024 * 1024
SMALL_LIMIT = 20 * 1024 * 1024

ANY = pl.BlockSpec(memory_space=pl.ANY)
SMEM = pl.BlockSpec(memory_space=pltpu.SMEM)
VMEM = pl.BlockSpec(memory_space=pltpu.VMEM)


def params(limit=VMEM_LIMIT):
    return pltpu.CompilerParams(vmem_limit_bytes=limit)


def cost(flops, nbytes, share=1):
    return pl.CostEstimate(flops=int(flops) // share, bytes_accessed=int(nbytes) // share, transcendentals=0)


def fetch(source, target, sem):
    copy = pltpu.make_async_copy(source, target, sem)
    copy.start()
    return copy


def dmas(count):
    return pltpu.SemaphoreType.DMA((count,))


def nt(a, b):
    return lax.dot_general(a, b, (((1,), (1,)), ((), ())), preferred_element_type=F32)


def tn(a, b):
    return lax.dot_general(a, b, (((0,), (0,)), ((), ())), preferred_element_type=F32)


def nn(a, b):
    return jnp.dot(a, b, preferred_element_type=F32)


def route_kernel(n, slots, blocks, where, slot_ref, tenant_ref, down_ref, send_ref, pos_ref, out_ref, send_tab, count, sems):
    me = where[0]
    asked = [[slot_ref[tenant_ref[o * blocks + b]] for b in range(blocks)] for o in range(n)]
    for i in range(n * CAP):
        send_tab[i] = -1
    for o in range(n):
        count[o] = 0
    copies = []
    for o in range(n):
        used = jnp.int32(0)
        for slot in asked[o]:
            local = slot - me * slots
            mine = (local >= 0) & (local < slots) & (used < CAP)
            send_tab[jnp.where(mine, o * CAP + used, n * CAP)] = local
            used = used + mine.astype(jnp.int32)
        for r in range(CAP):
            at = o * CAP + r
            copies.append(fetch(down_ref.at[jnp.maximum(send_tab[at], 0)], out_ref.at[o, r], sems.at[at]))
    for b in range(blocks):
        o = slot_ref[tenant_ref[me * blocks + b]] // slots
        pos_ref[b] = o * CAP + count[o]
        count[o] += 1
    for i in range(n * CAP):
        send_ref[i] = send_tab[i]
    for copy in copies:
        copy.wait()


def route(n, where, slot_of_tenant, seq_tenant, down_t, blocks):
    slots, rank, rows = down_t.shape
    return pl.pallas_call(
        functools.partial(route_kernel, n, slots, blocks),
        out_shape=[
            jax.ShapeDtypeStruct((n * CAP,), jnp.int32),
            jax.ShapeDtypeStruct((blocks,), jnp.int32),
            jax.ShapeDtypeStruct((n, CAP, rank, rows), BF),
        ],
        in_specs=[SMEM] * 3 + [ANY],
        out_specs=[SMEM] * 2 + [VMEM],
        scratch_shapes=[pltpu.SMEM((n * CAP + 1,), jnp.int32), pltpu.SMEM((n,), jnp.int32), dmas(n * CAP)],
        compiler_params=params(),
        cost_estimate=cost(0, 4 * n * CAP * rank * rows),
        name="route",
    )(where, slot_of_tenant, seq_tenant, down_t)


def prepare_kernel(blocks, len_ref, mask_ref, gap_ref, adv_ref, live_ref, cols_ref, rows_ref, square):
    length = mask_ref.shape[1]
    square[...] = jnp.zeros_like(square)
    position = lax.broadcasted_iota(jnp.int32, (1, length), 1)
    for b in range(blocks):
        live = (mask_ref[b : b + 1, :] * (position < len_ref[b]).astype(jnp.int32)).astype(F32)
        live_ref[b] = live
        square[b : b + 1, 0:length] = live
    square[blocks : 2 * blocks, 0:length] = gap_ref[...]
    cols_ref[...] = square[...].T[0:length, :]
    lane = lax.broadcasted_iota(jnp.int32, (1, LANES), 1)
    lengths = jnp.ones((1, LANES), F32)
    for b in range(blocks):
        lengths = jnp.where(lane == b, len_ref[b].astype(F32), lengths)
    rows_ref[...] = jnp.zeros_like(rows_ref)
    rows_ref[0:1, :] = lengths
    rows_ref[1:2, 0:blocks] = adv_ref[...]


def prepare(seq_len, mask, gap, advantage):
    blocks, length = mask.shape
    wide = -(-length // LANES) * LANES
    return pl.pallas_call(
        functools.partial(prepare_kernel, blocks),
        out_shape=[
            jax.ShapeDtypeStruct((blocks, 1, length), F32),
            jax.ShapeDtypeStruct((length, LANES), F32),
            jax.ShapeDtypeStruct((8, LANES), F32),
        ],
        in_specs=[SMEM] + [VMEM] * 3,
        out_specs=[VMEM] * 3,
        scratch_shapes=[pltpu.VMEM((LANES, wide), F32)],
        compiler_params=params(),
        cost_estimate=cost(0, 8 * blocks * length),
        name="prepare",
    )(seq_len, mask, gap, advantage)


def frozen_kernel(t, order, halved, where, x_ref, w_ref, *rest):
    x_buf, w_buf, o_buf, x_sem, w_sem, o_sem = rest[-6:]
    outs = rest[-6 - len(order) - halved : -6]
    z = where[1]
    piece = x_ref.shape[0] // t
    sides, _, wide = w_buf.shape
    half = piece // 2
    loads, weights, stores = [], [], []

    def load(i):
        start = pl.multiple_of((z ^ order[i]) * piece, 16)
        loads.append(fetch(x_ref.at[pl.ds(start, piece), :], x_buf.at[i], x_sem.at[i]))

    load(0)
    for side in range(sides):
        cols = pl.ds(side * wide, wide)
        weights.append(fetch(w_ref.at[:, cols], w_buf.at[side], w_sem.at[side]))
    for i in range(1, len(order)):
        load(i)
    for i in range(len(order)):
        loads[i].wait()
        for side in range(sides):
            if i == 0:
                weights[side].wait()
            o_buf[i, :, side * wide : (side + 1) * wide] = nn(x_buf[i], w_buf[side]).astype(BF)
        if i < halved:
            for p in range(2):
                at = 2 * i + p
                stores.append(fetch(o_buf.at[i, pl.ds(p * half, half)], outs[at], o_sem.at[at]))
        else:
            stores.append(fetch(o_buf.at[i], outs[halved + i], o_sem.at[halved + i]))
    for store in stores:
        store.wait()


def frozen(t, order, halved, where, states, weight, after=()):
    tokens, rows = states.shape
    width = weight.shape[1]
    piece = tokens // t
    count = len(order)
    sides = 2
    return pl.pallas_call(
        functools.partial(frozen_kernel, t, order, halved),
        out_shape=[jax.ShapeDtypeStruct((piece // 2, width), BF)] * (2 * halved)
        + [jax.ShapeDtypeStruct((piece, width), BF)] * (count - halved),
        in_specs=[SMEM, ANY, ANY] + [ANY] * len(after),
        out_specs=[ANY] * (count + halved),
        scratch_shapes=[
            pltpu.VMEM((count, piece, rows), BF),
            pltpu.VMEM((sides, rows, width // sides), BF),
            pltpu.VMEM((count, piece, width), BF),
            dmas(count),
            dmas(sides),
            dmas(count + halved),
        ],
        compiler_params=params(),
        cost_estimate=cost(2 * count * piece * rows * width, 2 * (count * piece * rows + rows * width)),
        name="frozen",
    )(where, states, weight, *after)


def pick_up_kernel(n, t, where, send_ref, *rest):
    parts, outs = rest[:t], rest[-n:]
    me, z = where[0], where[1]
    for k in range(n):
        for r in range(CAP):
            slot = jnp.maximum(send_ref[(me ^ k) * CAP + r], 0)
            for d in range(t):
                outs[k][z ^ d, r] = parts[d][slot]


def pick_up(n, t, where, send_tab, parts, after=()):
    slots, rank, cols = parts[0].shape
    return pl.pallas_call(
        functools.partial(pick_up_kernel, n, t),
        out_shape=[jax.ShapeDtypeStruct((t, CAP, rank, cols), BF)] * n,
        in_specs=[SMEM, SMEM] + [VMEM] * t + [ANY] * len(after),
        out_specs=[VMEM] * n,
        compiler_params=params(),
        cost_estimate=cost(0, 4 * n * t * CAP * rank * cols),
        name="pick_up",
    )(where, send_tab, *parts, *after)


def hidden_kernel(t, per, where, pos_ref, down_ref, states_ref, *rest):
    outs, (state_buf, state_sem) = rest[-2 - t : -2], rest[-2:]
    z = where[1]
    rank = down_ref.shape[2]
    order = list(range(t - 1, -1, -1))
    loads = [
        fetch(states_ref.at[pl.ds((z ^ k) * per, per)], state_buf.at[k], state_sem.at[k]) for k in order
    ]
    for i, k in enumerate(order):
        loads[i].wait()
        for h in range(per):
            at = pos_ref[(z ^ k) * per + h]
            panel = down_ref[at // CAP, lax.rem(at, CAP)]
            outs[k][:, h * rank : (h + 1) * rank] = nt(state_buf[k, h], panel)


def hidden_parts(t, where, pos, state_blocks, down_recv, after=()):
    blocks, length, rows = state_blocks.shape
    rank = down_recv.shape[2]
    per = blocks // t
    return pl.pallas_call(
        functools.partial(hidden_kernel, t, per),
        in_specs=[SMEM, SMEM, VMEM] + [ANY] * (1 + len(after)),
        out_specs=[VMEM] * t,
        out_shape=[jax.ShapeDtypeStruct((length, per * rank), F32)] * t,
        scratch_shapes=[pltpu.VMEM((t, per, length, rows), BF), dmas(t)],
        compiler_params=params(),
        cost_estimate=cost(2 * blocks * length * rows * rank, 2 * blocks * rows * (length + rank)),
        name="hidden",
    )(where, pos, down_recv, state_blocks, *after)


def panel_kernel(ks, where, pos_ref, cols_ref, proj_ref, states_ref, *rest):
    outs, (state_buf, grad_buf, state_sem, grad_sem) = rest[-4 - len(ks) : -4], rest[-4:]
    blocks, length, _ = states_ref.shape
    lanes = lax.broadcasted_iota(jnp.int32, (length, LANES), 1)
    columns = cols_ref[...]
    places = [pos_ref[b] for b in range(blocks)]
    rows, loads = [], []
    for i, k in enumerate(ks):
        for r in range(CAP):
            row = jnp.int32(0)
            for b in range(1, blocks):
                row = jnp.where(places[b] == (where[0] ^ k) * CAP + r, b, row)
            rows.append(row)
            at = i * CAP + r
            loads.append(fetch(states_ref.at[row], state_buf.at[at], state_sem.at[at]))
    stores = []
    for i, k in enumerate(ks):
        for r in range(CAP):
            at = i * CAP + r
            live = jnp.sum(jnp.where(lanes == rows[at], columns, 0.0), axis=1, keepdims=True)
            turned = (adapter_scale * live * proj_ref[rows[at]]).T.astype(BF)
            loads[at].wait()
            grad_buf[i, r] = nn(turned, state_buf[at]).astype(BF)
        stores.append(fetch(grad_buf.at[i], outs[i], grad_sem.at[i]))
    for store in stores:
        store.wait()


def panel_grads(ks, where, pos, columns, proj, state_blocks, after=()):
    blocks, length, rank = proj.shape
    rows = state_blocks.shape[2]
    steps = len(ks) * CAP
    return pl.pallas_call(
        functools.partial(panel_kernel, ks),
        in_specs=[SMEM, SMEM, VMEM, VMEM] + [ANY] * (1 + len(after)),
        out_specs=[ANY] * len(ks),
        scratch_shapes=[
            pltpu.VMEM((steps, length, rows), BF),
            pltpu.VMEM((len(ks), CAP, rank, rows), BF),
            dmas(steps),
            dmas(len(ks)),
        ],
        out_shape=[jax.ShapeDtypeStruct((CAP, rank, rows), BF)] * len(ks),
        compiler_params=params(SMALL_LIMIT),
        cost_estimate=cost(2 * steps * length * rank * rows, 2 * steps * (length * rows + rank * rows)),
        name="panel_grads",
    )(where, pos, columns, proj, state_blocks, *after)


def thirds(value):
    high = value.astype(BF)
    rest = value - high.astype(F32)
    middle = rest.astype(BF)
    return high, middle, (rest - middle.astype(F32)).astype(BF)


def own_kernel(t, per, rank, blocks, where, proj_ref, cols_ref, rows_ref, *rest):
    parts = rest[:t]
    out_ref, proj_buf, sem = rest[-3:]
    z = where[1]
    load = fetch(proj_ref.at[pl.ds(z * per, per)], proj_buf, sem)
    length = parts[0].shape[0]
    total = parts[0][...]
    for part in parts[1:]:
        total = total + part[...]
    hidden = total.astype(BF)
    out_ref[0:length, 0 : per * rank] = hidden
    lane = lax.broadcasted_iota(jnp.int32, (1, LANES), 1)
    lanes = lax.broadcasted_iota(jnp.int32, (length, LANES), 1)
    columns = cols_ref[...]
    load.wait()
    seq_log = jnp.zeros((1, LANES), F32)
    for h in range(per):
        b = z * per + h
        product = hidden[:, h * rank : (h + 1) * rank].astype(F32) * proj_buf[h]
        live = jnp.sum(jnp.where(lanes == b, columns, 0.0), axis=1, keepdims=True)
        gap = jnp.sum(jnp.where(lanes == b + blocks, columns, 0.0), axis=1, keepdims=True)
        linear = adapter_scale * jnp.sum(product, axis=1, keepdims=True)
        value = jnp.sum(live * (gap + linear), axis=0, keepdims=True)
        seq_log = seq_log + jnp.where(lane == b, value, 0.0)
    seq_log = seq_log / rows_ref[0:1, :]
    row = lax.broadcasted_iota(jnp.int32, (PAD, LANES), 0)
    tail = jnp.zeros((PAD, LANES), F32)
    for i, piece in enumerate(thirds(seq_log)):
        tail = jnp.where(row == i, piece.astype(F32), tail)
    out_ref[length : length + PAD, 0:LANES] = tail.astype(BF)


def own_hidden(t, where, parts, proj, columns, rows, per, rank, after=()):
    length, packed = parts[0].shape
    wide = max(packed, LANES)
    return pl.pallas_call(
        functools.partial(own_kernel, t, per, rank, per * t),
        out_shape=jax.ShapeDtypeStruct((length + PAD, wide), BF),
        in_specs=[SMEM, ANY] + [VMEM] * (2 + t) + [ANY] * len(after),
        out_specs=VMEM,
        scratch_shapes=[pltpu.VMEM((per, length, rank), F32), pltpu.SemaphoreType.DMA],
        compiler_params=params(SMALL_LIMIT),
        cost_estimate=cost(0, 4 * t * length * wide, LATE),
        name="own_hidden",
    )(where, proj, columns, rows, *parts, *after)


def up_grad_kernel(n, t, per, rank, where, pos_ref, sens_ref, cols_ref, rows_ref, *rest):
    msgs = rest[:t]
    factor_ref, loss_ref, ups, stack, sens_buf, sem = rest[-6:]
    z = where[1]
    blocks, length, width = sens_ref.shape
    cols = width // t
    start = pl.multiple_of(z * cols, LANES)
    load = fetch(sens_ref.at[:, :, pl.ds(start, cols)], sens_buf, sem)
    seq_log = jnp.zeros((PAD, LANES), F32)
    for d in range(t):
        stack[z ^ d] = msgs[d][...]
        seq_log = seq_log + msgs[d][length : length + PAD, 0:LANES].astype(F32)
    seq_log = seq_log[0:1] + seq_log[1:2] + seq_log[2:3]
    advantage = rows_ref[1:2, :]
    ratio = jnp.exp(seq_log)
    clipped = jnp.clip(ratio, 1.0 - clip_eps, 1.0 + clip_eps)
    loss_ref[...] = -jnp.minimum(ratio * advantage, clipped * advantage)
    active = ((advantage >= 0) & (ratio <= 1.0 + clip_eps)) | ((advantage < 0) & (ratio >= 1.0 - clip_eps))
    ratio_grad = jnp.where(active, -advantage * ratio, 0.0)
    factor = loss_scale * ratio_grad / rows_ref[0:1, :]
    factor_ref[...] = factor
    row = lax.broadcasted_iota(jnp.int32, (PAD, cols), 0)
    load.wait()
    for b in range(blocks):
        j, h = b // per, b % per
        mine = factor[:, b : b + 1]
        weight = mine * cols_ref[:, b : b + 1]
        out_cot = (weight * sens_buf[b].astype(F32)).astype(BF)
        hidden = stack[j, 0:length, h * rank : (h + 1) * rank]
        at = pos_ref[b]
        at = (at // CAP, lax.rem(at, CAP))
        ups[at[0], at[1], 0:rank, :] = (adapter_scale * tn(hidden, out_cot)).astype(BF)
        tail = jnp.zeros((PAD, cols), F32)
        for i, piece in enumerate(thirds(mine)):
            tail = jnp.where(row == i, piece.astype(F32), tail)
        ups[at[0], at[1], rank : rank + PAD, :] = tail.astype(BF)


def up_grads(n, t, where, pos, sens_blocks, columns, rows, msgs, rank, after=()):
    blocks, length, width = sens_blocks.shape
    cols = width // t
    row = jax.ShapeDtypeStruct((1, LANES), F32)
    out = pl.pallas_call(
        functools.partial(up_grad_kernel, n, t, blocks // t, rank),
        in_specs=[SMEM, SMEM, ANY] + [VMEM] * (2 + t) + [ANY] * len(after),
        out_specs=[VMEM] * 3,
        scratch_shapes=[
            pltpu.VMEM((t,) + msgs[0].shape, BF),
            pltpu.VMEM((blocks, length, cols), BF),
            pltpu.SemaphoreType.DMA,
        ],
        out_shape=[row, row, jax.ShapeDtypeStruct((n, CAP, rank + PAD, cols), BF)],
        compiler_params=params(SMALL_LIMIT),
        cost_estimate=cost(2 * blocks * length * cols * rank, 2 * blocks * length * cols, LATE),
        name="up_grads",
    )(where, pos, sens_blocks, columns, rows, *msgs, *after)
    return out


def back_kernel(n, per, where, pos_ref, sens_ref, w_ref, *rest):
    ups = rest[:n]
    o_ref, proj_ref, own_ref, s_buf, w_buf, o_buf, up_buf, s_sem, w_sem, o_sem, up_sem = rest[-11:]
    me, z = where[0], where[1]
    t = ups[0].shape[0]
    tiles, tile, _ = w_buf.shape
    blocks, length, _ = s_buf.shape
    half = blocks // 2
    loads = [fetch(sens_ref.at[pl.ds(p * half, half)], s_buf.at[pl.ds(p * half, half)], s_sem.at[p]) for p in range(2)]
    weights = [fetch(w_ref.at[pl.ds(0, tile), :], w_buf.at[0], w_sem.at[0])]
    loads += [fetch(ups[k], up_buf.at[me ^ k], up_sem.at[k]) for k in range(n)]
    for i in range(1, tiles):
        weights.append(fetch(w_ref.at[pl.ds(i * tile, tile), :], w_buf.at[i], w_sem.at[i]))

    def panel(at):
        o, r = at // CAP, lax.rem(at, CAP)
        return jnp.concatenate([up_buf[o, c, r] for c in range(t)], axis=1)

    stores = []
    for i in range(tiles):
        weights[i].wait()
        for p in range(2):
            if i == 0:
                loads[p].wait()
            rows = slice(p * half, (p + 1) * half)
            o_buf[i, p * half * length : (p + 1) * half * length, :] = nt(
                s_buf[rows].reshape(half * length, s_buf.shape[2]), w_buf[i]
            ).astype(BF)
        stores.append(fetch(o_buf.at[i], o_ref.at[:, pl.ds(i * tile, tile)], o_sem.at[i]))
    for load in loads[2:]:
        load.wait()
    for b in range(blocks):
        proj_ref[b] = nt(s_buf[b], panel(pos_ref[b]))
    for h in range(per):
        own_ref[h] = panel(pos_ref[z * per + h])
    for store in stores:
        store.wait()


def back(n, where, pos, sens_blocks, weight, ups, after=()):
    blocks, length, width = sens_blocks.shape
    t, _, rank, cols = ups[0].shape
    per = blocks // t
    tokens = blocks * length
    rows = weight.shape[0]
    tiles = max(rows // 512, 1)
    return pl.pallas_call(
        functools.partial(back_kernel, n, per),
        out_shape=[
            jax.ShapeDtypeStruct((tokens, rows), BF),
            jax.ShapeDtypeStruct((blocks, length, rank), F32),
            jax.ShapeDtypeStruct((per, rank, width), BF),
        ],
        in_specs=[SMEM, SMEM] + [ANY] * (2 + n + len(after)),
        out_specs=[ANY, VMEM, VMEM],
        scratch_shapes=[
            pltpu.VMEM((blocks, length, width), BF),
            pltpu.VMEM((tiles, rows // tiles, width), BF),
            pltpu.VMEM((tiles, tokens, rows // tiles), BF),
            pltpu.VMEM((n, t, CAP, rank, cols), BF),
            dmas(2),
            dmas(tiles),
            dmas(tiles),
            dmas(n),
        ],
        compiler_params=params(),
        cost_estimate=cost(2 * tokens * rows * width, 2 * (tokens * (width + rows) + rows * width)),
        name="back",
    )(where, pos, sens_blocks, weight, *ups, *after)


def state_grad_kernel(pos_ref, factor_ref, cols_ref, proj_ref, back_ref, down_ref, o_ref, *rest):
    in_buf, out_buf, in_sem, out_sem = rest
    blocks, length, _ = back_ref.shape
    half = blocks // 2
    loads = []
    for p in range(half):
        some = pl.ds(2 * p, 2)
        loads.append(fetch(back_ref.at[some], in_buf.at[some], in_sem.at[p]))
    weight = factor_ref[...] * cols_ref[...]
    stores = []
    for b in range(blocks):
        if b % 2 == 0:
            loads[b // 2].wait()
        hcot = (adapter_scale * proj_ref[b]).astype(BF)
        at = pos_ref[b]
        total = in_buf[b].astype(F32) + nn(hcot, down_ref[at // CAP, lax.rem(at, CAP)])
        out_buf[b] = (weight[:, b : b + 1] * total).astype(BF)
        if b % 2 == 1:
            some = pl.ds(b - 1, 2)
            stores.append(fetch(out_buf.at[some], o_ref.at[some], out_sem.at[b // 2]))
    for store in stores:
        store.wait()


def state_grad(pos, factor, columns, proj, backward, down_recv):
    blocks, length, rows = backward.shape
    rank = down_recv.shape[2]
    return pl.pallas_call(
        state_grad_kernel,
        out_shape=jax.ShapeDtypeStruct((blocks, length, rows), BF),
        in_specs=[SMEM, VMEM, VMEM, VMEM, ANY, VMEM],
        out_specs=ANY,
        scratch_shapes=[
            pltpu.VMEM((blocks, length, rows), BF),
            pltpu.VMEM((blocks, length, rows), BF),
            dmas(blocks // 2),
            dmas(blocks // 2),
        ],
        compiler_params=params(),
        cost_estimate=cost(2 * blocks * length * rows * rank, 4 * blocks * length * rows, LATE),
        name="state_grad",
    )(pos, factor, columns, proj, backward, down_recv)


def slot_sum_kernel(n, rank, where, send_ref, *rest):
    grads, rest = rest[:n], rest[n:]
    msg_ref, (down_ref, up_ref, acc, up_acc, out_buf, out_sems) = rest[0], rest[-6:]
    me = where[0]
    slots = acc.shape[0]
    acc[...] = jnp.zeros_like(acc)
    up_acc[...] = jnp.zeros_like(up_acc)
    for k in range(n):
        for r in range(CAP):
            slot = send_ref[(me ^ k) * CAP + r]
            used = slot >= 0
            slot = jnp.maximum(slot, 0)
            tail = jnp.sum(msg_ref[me ^ k, r, rank : rank + PAD, 0:LANES].astype(F32), axis=0, keepdims=True)
            part = tail[:, 0:1] * grads[k][r].astype(F32)
            acc[slot] += jnp.where(used, part, 0.0)
            up_acc[slot] += jnp.where(used, msg_ref[me ^ k, r, 0:rank, :].astype(F32), 0.0)
    stores = []
    for s in range(slots):
        out_buf[s] = acc[s].astype(BF)
        stores.append(fetch(out_buf.at[s], down_ref.at[s], out_sems.at[s]))
    up_ref[...] = up_acc[...].astype(BF)
    for store in stores:
        store.wait()


def slot_sum(slots, where, send_tab, grads, msgs, after=()):
    n = len(grads)
    _, rank, rows = grads[0].shape
    cols = msgs.shape[3]
    return pl.pallas_call(
        functools.partial(slot_sum_kernel, n, rank),
        in_specs=[SMEM, SMEM] + [VMEM] * (n + 1) + [ANY] * len(after),
        out_specs=[ANY, VMEM],
        scratch_shapes=[
            pltpu.VMEM((slots, rank, rows), F32),
            pltpu.VMEM((slots, rank, cols), F32),
            pltpu.VMEM((slots, rank, rows), BF),
            dmas(slots),
        ],
        out_shape=[
            jax.ShapeDtypeStruct((slots, rank, rows), BF),
            jax.ShapeDtypeStruct((slots, rank, cols), BF),
        ],
        compiler_params=params(SMALL_LIMIT),
        cost_estimate=cost(0, 2 * (n * CAP + slots) * rank * rows, LATE),
        name="slot_sum",
    )(where, send_tab, *grads, msgs, *after)


def layer_out_kernel(per, whole, halved, msg_ref, up_ref, *rest):
    parts, o_ref = rest[: whole + 2 * halved], rest[-1]
    length = msg_ref.shape[0] - PAD
    rank = up_ref.shape[1]
    piece = o_ref.shape[0]
    for h in range(per):
        hidden = msg_ref[0:length, h * rank : (h + 1) * rank]
        adapter = adapter_scale * nn(hidden, up_ref[h])
        cuts = sorted({h * length, (h + 1) * length} | ({piece // 2} if per == 1 else set()))
        for low, high in zip(cuts[:-1], cuts[1:]):
            total = adapter[low - h * length : high - h * length]
            for part in parts[:whole]:
                total = total + part[low:high, :].astype(F32)
            p = low // (piece // 2)
            base = p * (piece // 2)
            for i in range(halved):
                total = total + parts[whole + 2 * i + p][low - base : high - base, :].astype(F32)
            o_ref[low:high, :] = total.astype(BF)


def layer_out(own_msg, up_own, whole, halves, after=()):
    piece, width = whole[0].shape
    per, rank, _ = up_own.shape
    return pl.pallas_call(
        functools.partial(layer_out_kernel, per, len(whole), len(halves) // 2),
        in_specs=[VMEM] * (2 + len(whole) + len(halves)) + [ANY] * len(after),
        out_specs=VMEM,
        out_shape=jax.ShapeDtypeStruct((piece, width), BF),
        compiler_params=params(),
        cost_estimate=cost(2 * piece * rank * width, 2 * piece * width * (2 + len(whole)), LATE),
        name="layer_out",
    )(own_msg, up_own, *whole, *halves, *after)


def exchange(value, axis):
    return lax.all_to_all(value, axis, 0, 0, tiled=True)


def swap(value, axis, k):
    size = lax.axis_size(axis)
    return lax.ppermute(value, axis, [(i, i ^ k) for i in range(size)])


def shards(
    token_states,
    base_weight,
    adapter_down,
    adapter_up,
    slot_of_tenant,
    seq_tenant,
    seq_len,
    token_mask,
    logp_gap,
    out_sens,
    advantage,
):
    n = lax.axis_size("dp")
    t = lax.axis_size("tensor")
    slots, rows, rank = adapter_down.shape
    width = out_sens.shape[1]
    blocks = seq_len.shape[0]
    length = token_states.shape[0] // blocks
    per = blocks // t
    where = jnp.stack([lax.axis_index("dp"), lax.axis_index("tensor")]).astype(jnp.int32)
    state_blocks = token_states.reshape(blocks, length, rows)
    sens_blocks = out_sens.reshape(blocks, length, width)
    down_t = jnp.swapaxes(adapter_down, 1, 2)

    up_parts = [adapter_up] + [swap(adapter_up, "tensor", k) for k in range(1, t)]
    send_tab, pos, down_send = route(n, where, slot_of_tenant, seq_tenant, down_t, blocks)
    down_recv = exchange(down_send, "dp")
    live, columns, seq_rows = prepare(
        seq_len, token_mask.reshape(blocks, length), logp_gap.reshape(blocks, length), advantage[None]
    )
    middle = t // 2
    halved = [middle]
    others = [k for k in range(t - 1, -1, -1) if k not in halved]
    parts = frozen(t, halved + others, 1, where, token_states, base_weight, (down_send, up_parts[1], columns))
    chunks = dict(zip(others, parts[2:]))
    up_send = pick_up(n, t, where, send_tab, up_parts, (chunks[0],))
    ups = [up_send[0]] + [swap(up_send[k], "dp", k) for k in range(1, n)]
    hidden = hidden_parts(t, where, pos, state_blocks, down_recv, (up_send[0],))
    hidden = [hidden[0]] + [swap(hidden[k], "tensor", k) for k in range(1, t)]
    early = [swap(parts[0], "tensor", middle)]
    piece, _ = lax.optimization_barrier((parts[1], hidden[0]))
    early.append(swap(piece, "tensor", middle))
    backward, proj, up_own = back(n, where, pos, sens_blocks, base_weight, ups, (hidden[0], early[0]))
    own_msg = own_hidden(t, where, hidden, proj, columns, seq_rows, per, rank)
    msgs = [own_msg] + [swap(own_msg, "tensor", k) for k in range(1, t)]
    far, near = list(range(2, n)), list(range(min(n, 2)))
    grads = dict(zip(far, panel_grads(far, where, pos, columns, proj, state_blocks, (own_msg,))))
    grads |= dict(zip(near, panel_grads(near, where, pos, columns, proj, state_blocks, (*msgs[1:], early[1]))))
    grads_in = [grads[0]] + [swap(grads[k], "dp", k) for k in range(1, n)]
    factor, loss, up_out = up_grads(n, t, where, pos, sens_blocks, columns, seq_rows, msgs, rank)
    up_in = exchange(up_out, "dp")
    token_state_gradient = state_grad(
        pos, factor, columns, proj, backward.reshape(blocks, length, rows), down_recv
    )
    late = {}
    for k in others[:-1]:
        piece, _ = lax.optimization_barrier((chunks[k], (msgs[1:], [grads[i] for i in far])))
        late[k] = swap(piece, "tensor", k)
    whole = [chunks[0]] + [late[k] for k in others[:-1]]
    down_grad, up_grad = slot_sum(slots, where, send_tab, grads_in, up_in)
    out = layer_out(own_msg, up_own, whole, early, (up_grad,))
    return (
        out,
        loss[0, :blocks],
        token_state_gradient.reshape(blocks * length, rows),
        jnp.swapaxes(down_grad, 1, 2),
        up_grad,
    )


def solution(mesh):
    in_specs = (
        P(("groups", "dp"), "tensor"),
        P("tensor", None),
        P(("groups", "dp"), "tensor", None),
        P(("groups", "dp"), None, "tensor"),
        P("groups"),
        P("groups"),
        P(("groups", "dp")),
        P(("groups", "dp")),
        P(("groups", "dp")),
        P(("groups", "dp"), None),
        P(("groups", "dp")),
    )
    out_specs = (
        P(("groups", "dp", "tensor"), None),
        P(("groups", "dp")),
        P(("groups", "dp"), "tensor"),
        P(("groups", "dp"), "tensor", None),
        P(("groups", "dp"), None, "tensor"),
    )
    return jax.shard_map(shards, mesh=mesh, in_specs=in_specs, out_specs=out_specs, check_vma=False)
```

```python
import functools

import jax
import jax.numpy as jnp
from jax import lax
from jax.experimental import pallas as pl
from jax.experimental.pallas import tpu as pltpu
from jax.sharding import PartitionSpec as P

CAP = 2
PAD = 16
LATE = 16
LANES = 128

adapter_scale = 2.0
loss_scale = 1024.0
clip_eps = 0.2

BF = jnp.bfloat16
F32 = jnp.float32
VMEM_LIMIT = 58 * 1024 * 1024
SMALL_LIMIT = 20 * 1024 * 1024

ANY = pl.BlockSpec(memory_space=pl.ANY)
SMEM = pl.BlockSpec(memory_space=pltpu.SMEM)
VMEM = pl.BlockSpec(memory_space=pltpu.VMEM)


def params(limit=VMEM_LIMIT):
    return pltpu.CompilerParams(vmem_limit_bytes=limit)


def cost(flops, nbytes, share=1):
    return pl.CostEstimate(flops=int(flops) // share, bytes_accessed=int(nbytes) // share, transcendentals=0)


def fetch(source, target, sem):
    copy = pltpu.make_async_copy(source, target, sem)
    copy.start()
    return copy


def dmas(count):
    return pltpu.SemaphoreType.DMA((count,))


def nt(a, b):
    return lax.dot_general(a, b, (((1,), (1,)), ((), ())), preferred_element_type=F32)


def tn(a, b):
    return lax.dot_general(a, b, (((0,), (0,)), ((), ())), preferred_element_type=F32)


def nn(a, b):
    return jnp.dot(a, b, preferred_element_type=F32)


def route_kernel(n, slots, blocks, where, slot_ref, tenant_ref, down_ref, send_ref, pos_ref, out_ref, send_tab, count, sems):
    me = where[0]
    asked = [[slot_ref[tenant_ref[o * blocks + b]] for b in range(blocks)] for o in range(n)]
    for i in range(n * CAP):
        send_tab[i] = -1
    for o in range(n):
        count[o] = 0
    copies = []
    for o in range(n):
        used = jnp.int32(0)
        for slot in asked[o]:
            local = slot - me * slots
            mine = (local >= 0) & (local < slots) & (used < CAP)
            send_tab[jnp.where(mine, o * CAP + used, n * CAP)] = local
            used = used + mine.astype(jnp.int32)
        for r in range(CAP):
            at = o * CAP + r
            copies.append(fetch(down_ref.at[jnp.maximum(send_tab[at], 0)], out_ref.at[o, r], sems.at[at]))
    for b in range(blocks):
        o = slot_ref[tenant_ref[me * blocks + b]] // slots
        pos_ref[b] = o * CAP + count[o]
        count[o] += 1
    for i in range(n * CAP):
        send_ref[i] = send_tab[i]
    for copy in copies:
        copy.wait()


def route(n, where, slot_of_tenant, seq_tenant, down_t, blocks):
    slots, rank, rows = down_t.shape
    return pl.pallas_call(
        functools.partial(route_kernel, n, slots, blocks),
        out_shape=[
            jax.ShapeDtypeStruct((n * CAP,), jnp.int32),
            jax.ShapeDtypeStruct((blocks,), jnp.int32),
            jax.ShapeDtypeStruct((n, CAP, rank, rows), BF),
        ],
        in_specs=[SMEM] * 3 + [ANY],
        out_specs=[SMEM] * 2 + [VMEM],
        scratch_shapes=[pltpu.SMEM((n * CAP + 1,), jnp.int32), pltpu.SMEM((n,), jnp.int32), dmas(n * CAP)],
        compiler_params=params(),
        cost_estimate=cost(0, 4 * n * CAP * rank * rows),
        name="route",
    )(where, slot_of_tenant, seq_tenant, down_t)


def prepare_kernel(blocks, len_ref, mask_ref, gap_ref, adv_ref, cols_ref, rows_ref, square):
    length = mask_ref.shape[1]
    square[...] = jnp.zeros_like(square)
    position = lax.broadcasted_iota(jnp.int32, (1, length), 1)
    for b in range(blocks):
        live = (mask_ref[b : b + 1, :] * (position < len_ref[b]).astype(jnp.int32)).astype(F32)
        square[b : b + 1, 0:length] = live
    square[blocks : 2 * blocks, 0:length] = gap_ref[...]
    cols_ref[...] = square[...].T[0:length, :]
    lane = lax.broadcasted_iota(jnp.int32, (1, LANES), 1)
    lengths = jnp.ones((1, LANES), F32)
    for b in range(blocks):
        lengths = jnp.where(lane == b, len_ref[b].astype(F32), lengths)
    rows_ref[...] = jnp.zeros_like(rows_ref)
    rows_ref[0:1, :] = lengths
    rows_ref[1:2, 0:blocks] = adv_ref[...]


def prepare(seq_len, mask, gap, advantage):
    blocks, length = mask.shape
    wide = -(-length // LANES) * LANES
    return pl.pallas_call(
        functools.partial(prepare_kernel, blocks),
        out_shape=[
            jax.ShapeDtypeStruct((length, LANES), F32),
            jax.ShapeDtypeStruct((8, LANES), F32),
        ],
        in_specs=[SMEM] + [VMEM] * 3,
        out_specs=[VMEM] * 2,
        scratch_shapes=[pltpu.VMEM((LANES, wide), F32)],
        compiler_params=params(),
        cost_estimate=cost(0, 8 * blocks * length),
        name="prepare",
    )(seq_len, mask, gap, advantage)


def frozen_kernel(t, order, halved, where, x_ref, w_ref, *rest):
    x_buf, w_buf, o_buf, x_sem, w_sem, o_sem = rest[-6:]
    outs = rest[-6 - len(order) - halved : -6]
    z = where[1]
    piece = x_ref.shape[0] // t
    sides, _, wide = w_buf.shape
    half = piece // 2
    loads, weights, stores = [], [], []

    def load(i):
        start = pl.multiple_of((z ^ order[i]) * piece, 16)
        loads.append(fetch(x_ref.at[pl.ds(start, piece), :], x_buf.at[i], x_sem.at[i]))

    load(0)
    for side in range(sides):
        cols = pl.ds(side * wide, wide)
        weights.append(fetch(w_ref.at[:, cols], w_buf.at[side], w_sem.at[side]))
    for i in range(1, len(order)):
        load(i)
    for i in range(len(order)):
        loads[i].wait()
        for side in range(sides):
            if i == 0:
                weights[side].wait()
            o_buf[i, :, side * wide : (side + 1) * wide] = nn(x_buf[i], w_buf[side]).astype(BF)
        if i < halved:
            for p in range(2):
                at = 2 * i + p
                stores.append(fetch(o_buf.at[i, pl.ds(p * half, half)], outs[at], o_sem.at[at]))
        else:
            stores.append(fetch(o_buf.at[i], outs[halved + i], o_sem.at[halved + i]))
    for store in stores:
        store.wait()


def frozen(t, order, halved, where, states, weight, after=()):
    tokens, rows = states.shape
    width = weight.shape[1]
    piece = tokens // t
    count = len(order)
    sides = 2
    return pl.pallas_call(
        functools.partial(frozen_kernel, t, order, halved),
        out_shape=[jax.ShapeDtypeStruct((piece // 2, width), BF)] * (2 * halved)
        + [jax.ShapeDtypeStruct((piece, width), BF)] * (count - halved),
        in_specs=[SMEM, ANY, ANY] + [ANY] * len(after),
        out_specs=[ANY] * (count + halved),
        scratch_shapes=[
            pltpu.VMEM((count, piece, rows), BF),
            pltpu.VMEM((sides, rows, width // sides), BF),
            pltpu.VMEM((count, piece, width), BF),
            dmas(count),
            dmas(sides),
            dmas(count + halved),
        ],
        compiler_params=params(),
        cost_estimate=cost(2 * count * piece * rows * width, 2 * (count * piece * rows + rows * width)),
        name="frozen",
    )(where, states, weight, *after)


def pick_up_kernel(n, t, where, send_ref, *rest):
    parts, outs = rest[:t], rest[-n:]
    me, z = where[0], where[1]
    for k in range(n):
        for r in range(CAP):
            slot = jnp.maximum(send_ref[(me ^ k) * CAP + r], 0)
            for d in range(t):
                outs[k][z ^ d, r] = parts[d][slot]


def pick_up(n, t, where, send_tab, parts, after=()):
    slots, rank, cols = parts[0].shape
    return pl.pallas_call(
        functools.partial(pick_up_kernel, n, t),
        out_shape=[jax.ShapeDtypeStruct((t, CAP, rank, cols), BF)] * n,
        in_specs=[SMEM, SMEM] + [VMEM] * t + [ANY] * len(after),
        out_specs=[VMEM] * n,
        compiler_params=params(),
        cost_estimate=cost(0, 4 * n * t * CAP * rank * cols),
        name="pick_up",
    )(where, send_tab, *parts, *after)


def hidden_kernel(t, per, where, pos_ref, down_ref, states_ref, *rest):
    outs, (state_buf, state_sem) = rest[-2 - t : -2], rest[-2:]
    z = where[1]
    rank = down_ref.shape[2]
    order = list(range(t - 1, -1, -1))
    loads = [
        fetch(states_ref.at[pl.ds((z ^ k) * per, per)], state_buf.at[k], state_sem.at[k]) for k in order
    ]
    for i, k in enumerate(order):
        loads[i].wait()
        for h in range(per):
            at = pos_ref[(z ^ k) * per + h]
            panel = down_ref[at // CAP, lax.rem(at, CAP)]
            outs[k][:, h * rank : (h + 1) * rank] = nt(state_buf[k, h], panel)


def hidden_parts(t, where, pos, state_blocks, down_recv, after=()):
    blocks, length, rows = state_blocks.shape
    rank = down_recv.shape[2]
    per = blocks // t
    return pl.pallas_call(
        functools.partial(hidden_kernel, t, per),
        in_specs=[SMEM, SMEM, VMEM] + [ANY] * (1 + len(after)),
        out_specs=[VMEM] * t,
        out_shape=[jax.ShapeDtypeStruct((length, per * rank), F32)] * t,
        scratch_shapes=[pltpu.VMEM((t, per, length, rows), BF), dmas(t)],
        compiler_params=params(),
        cost_estimate=cost(2 * blocks * length * rows * rank, 2 * blocks * rows * (length + rank)),
        name="hidden",
    )(where, pos, down_recv, state_blocks, *after)


def panel_kernel(ks, where, pos_ref, cols_ref, proj_ref, states_ref, *rest):
    outs, (state_buf, grad_buf, state_sem, grad_sem) = rest[-4 - len(ks) : -4], rest[-4:]
    blocks, length, _ = states_ref.shape
    lanes = lax.broadcasted_iota(jnp.int32, (length, LANES), 1)
    columns = cols_ref[...]
    places = [pos_ref[b] for b in range(blocks)]
    rows, loads = [], []
    for i, k in enumerate(ks):
        for r in range(CAP):
            row = jnp.int32(0)
            for b in range(1, blocks):
                row = jnp.where(places[b] == (where[0] ^ k) * CAP + r, b, row)
            rows.append(row)
            at = i * CAP + r
            loads.append(fetch(states_ref.at[row], state_buf.at[at], state_sem.at[at]))
    stores = []
    for i, k in enumerate(ks):
        for r in range(CAP):
            at = i * CAP + r
            live = jnp.sum(jnp.where(lanes == rows[at], columns, 0.0), axis=1, keepdims=True)
            turned = (adapter_scale * live * proj_ref[rows[at]]).T.astype(BF)
            loads[at].wait()
            grad_buf[i, r] = nn(turned, state_buf[at]).astype(BF)
        stores.append(fetch(grad_buf.at[i], outs[i], grad_sem.at[i]))
    for store in stores:
        store.wait()


def panel_grads(ks, where, pos, columns, proj, state_blocks, after=()):
    blocks, length, rank = proj.shape
    rows = state_blocks.shape[2]
    steps = len(ks) * CAP
    return pl.pallas_call(
        functools.partial(panel_kernel, ks),
        in_specs=[SMEM, SMEM, VMEM, VMEM] + [ANY] * (1 + len(after)),
        out_specs=[ANY] * len(ks),
        scratch_shapes=[
            pltpu.VMEM((steps, length, rows), BF),
            pltpu.VMEM((len(ks), CAP, rank, rows), BF),
            dmas(steps),
            dmas(len(ks)),
        ],
        out_shape=[jax.ShapeDtypeStruct((CAP, rank, rows), BF)] * len(ks),
        compiler_params=params(SMALL_LIMIT),
        cost_estimate=cost(2 * steps * length * rank * rows, 2 * steps * (length * rows + rank * rows)),
        name="panel_grads",
    )(where, pos, columns, proj, state_blocks, *after)


def thirds(value):
    high = value.astype(BF)
    rest = value - high.astype(F32)
    middle = rest.astype(BF)
    return high, middle, (rest - middle.astype(F32)).astype(BF)


def own_kernel(t, per, rank, blocks, where, proj_ref, cols_ref, rows_ref, *rest):
    parts = rest[:t]
    out_ref, proj_buf, sem = rest[-3:]
    z = where[1]
    load = fetch(proj_ref.at[pl.ds(z * per, per)], proj_buf, sem)
    length = parts[0].shape[0]
    total = parts[0][...]
    for part in parts[1:]:
        total = total + part[...]
    hidden = total.astype(BF)
    out_ref[0:length, 0 : per * rank] = hidden
    lane = lax.broadcasted_iota(jnp.int32, (1, LANES), 1)
    lanes = lax.broadcasted_iota(jnp.int32, (length, LANES), 1)
    columns = cols_ref[...]
    load.wait()
    seq_log = jnp.zeros((1, LANES), F32)
    for h in range(per):
        b = z * per + h
        product = hidden[:, h * rank : (h + 1) * rank].astype(F32) * proj_buf[h]
        live = jnp.sum(jnp.where(lanes == b, columns, 0.0), axis=1, keepdims=True)
        gap = jnp.sum(jnp.where(lanes == b + blocks, columns, 0.0), axis=1, keepdims=True)
        linear = adapter_scale * jnp.sum(product, axis=1, keepdims=True)
        value = jnp.sum(live * (gap + linear), axis=0, keepdims=True)
        seq_log = seq_log + jnp.where(lane == b, value, 0.0)
    seq_log = seq_log / rows_ref[0:1, :]
    row = lax.broadcasted_iota(jnp.int32, (PAD, LANES), 0)
    tail = jnp.zeros((PAD, LANES), F32)
    for i, piece in enumerate(thirds(seq_log)):
        tail = jnp.where(row == i, piece.astype(F32), tail)
    out_ref[length : length + PAD, 0:LANES] = tail.astype(BF)


def own_hidden(t, where, parts, proj, columns, rows, per, rank, after=()):
    length, packed = parts[0].shape
    wide = max(packed, LANES)
    return pl.pallas_call(
        functools.partial(own_kernel, t, per, rank, per * t),
        out_shape=jax.ShapeDtypeStruct((length + PAD, wide), BF),
        in_specs=[SMEM, ANY] + [VMEM] * (2 + t) + [ANY] * len(after),
        out_specs=VMEM,
        scratch_shapes=[pltpu.VMEM((per, length, rank), F32), pltpu.SemaphoreType.DMA],
        compiler_params=params(SMALL_LIMIT),
        cost_estimate=cost(0, 4 * t * length * wide, LATE),
        name="own_hidden",
    )(where, proj, columns, rows, *parts, *after)


def up_grad_kernel(n, t, per, rank, where, pos_ref, sens_ref, cols_ref, rows_ref, *rest):
    msgs = rest[:t]
    factor_ref, loss_ref, ups, stack, sens_buf, sem = rest[-6:]
    z = where[1]
    blocks, length, width = sens_ref.shape
    cols = width // t
    start = pl.multiple_of(z * cols, LANES)
    load = fetch(sens_ref.at[:, :, pl.ds(start, cols)], sens_buf, sem)
    seq_log = jnp.zeros((PAD, LANES), F32)
    for d in range(t):
        stack[z ^ d] = msgs[d][...]
        seq_log = seq_log + msgs[d][length : length + PAD, 0:LANES].astype(F32)
    seq_log = seq_log[0:1] + seq_log[1:2] + seq_log[2:3]
    advantage = rows_ref[1:2, :]
    ratio = jnp.exp(seq_log)
    clipped = jnp.clip(ratio, 1.0 - clip_eps, 1.0 + clip_eps)
    loss_ref[...] = -jnp.minimum(ratio * advantage, clipped * advantage)
    active = ((advantage >= 0) & (ratio <= 1.0 + clip_eps)) | ((advantage < 0) & (ratio >= 1.0 - clip_eps))
    ratio_grad = jnp.where(active, -advantage * ratio, 0.0)
    factor = loss_scale * ratio_grad / rows_ref[0:1, :]
    factor_ref[...] = factor
    row = lax.broadcasted_iota(jnp.int32, (PAD, cols), 0)
    load.wait()
    for b in range(blocks):
        j, h = b // per, b % per
        mine = factor[:, b : b + 1]
        weight = mine * cols_ref[:, b : b + 1]
        out_cot = (weight * sens_buf[b].astype(F32)).astype(BF)
        hidden = stack[j, 0:length, h * rank : (h + 1) * rank]
        at = pos_ref[b]
        at = (at // CAP, lax.rem(at, CAP))
        ups[at[0], at[1], 0:rank, :] = (adapter_scale * tn(hidden, out_cot)).astype(BF)
        tail = jnp.zeros((PAD, cols), F32)
        for i, piece in enumerate(thirds(mine)):
            tail = jnp.where(row == i, piece.astype(F32), tail)
        ups[at[0], at[1], rank : rank + PAD, :] = tail.astype(BF)


def up_grads(n, t, where, pos, sens_blocks, columns, rows, msgs, rank, after=()):
    blocks, length, width = sens_blocks.shape
    cols = width // t
    row = jax.ShapeDtypeStruct((1, LANES), F32)
    out = pl.pallas_call(
        functools.partial(up_grad_kernel, n, t, blocks // t, rank),
        in_specs=[SMEM, SMEM, ANY] + [VMEM] * (2 + t) + [ANY] * len(after),
        out_specs=[VMEM] * 3,
        scratch_shapes=[
            pltpu.VMEM((t,) + msgs[0].shape, BF),
            pltpu.VMEM((blocks, length, cols), BF),
            pltpu.SemaphoreType.DMA,
        ],
        out_shape=[row, row, jax.ShapeDtypeStruct((n, CAP, rank + PAD, cols), BF)],
        compiler_params=params(SMALL_LIMIT),
        cost_estimate=cost(2 * blocks * length * cols * rank, 2 * blocks * length * cols, LATE),
        name="up_grads",
    )(where, pos, sens_blocks, columns, rows, *msgs, *after)
    return out


def back_kernel(n, per, where, pos_ref, sens_ref, w_ref, *rest):
    ups = rest[:n]
    o_ref, proj_ref, own_ref, s_buf, w_buf, o_buf, up_buf, s_sem, w_sem, o_sem, up_sem = rest[-11:]
    me, z = where[0], where[1]
    t = ups[0].shape[0]
    tiles, tile, _ = w_buf.shape
    blocks, length, _ = s_buf.shape
    half = blocks // 2
    loads = [fetch(sens_ref.at[pl.ds(p * half, half)], s_buf.at[pl.ds(p * half, half)], s_sem.at[p]) for p in range(2)]
    weights = [fetch(w_ref.at[pl.ds(0, tile), :], w_buf.at[0], w_sem.at[0])]
    loads += [fetch(ups[k], up_buf.at[me ^ k], up_sem.at[k]) for k in range(n)]
    for i in range(1, tiles):
        weights.append(fetch(w_ref.at[pl.ds(i * tile, tile), :], w_buf.at[i], w_sem.at[i]))

    def panel(at):
        o, r = at // CAP, lax.rem(at, CAP)
        return jnp.concatenate([up_buf[o, c, r] for c in range(t)], axis=1)

    stores = []
    for i in range(tiles):
        weights[i].wait()
        for p in range(2):
            if i == 0:
                loads[p].wait()
            rows = slice(p * half, (p + 1) * half)
            o_buf[i, p * half * length : (p + 1) * half * length, :] = nt(
                s_buf[rows].reshape(half * length, s_buf.shape[2]), w_buf[i]
            ).astype(BF)
        stores.append(fetch(o_buf.at[i], o_ref.at[:, pl.ds(i * tile, tile)], o_sem.at[i]))
    for load in loads[2:]:
        load.wait()
    for b in range(blocks):
        proj_ref[b] = nt(s_buf[b], panel(pos_ref[b]))
    for h in range(per):
        own_ref[h] = panel(pos_ref[z * per + h])
    for store in stores:
        store.wait()


def back(n, where, pos, sens_blocks, weight, ups, after=()):
    blocks, length, width = sens_blocks.shape
    t, _, rank, cols = ups[0].shape
    per = blocks // t
    tokens = blocks * length
    rows = weight.shape[0]
    tiles = max(rows // 512, 1)
    return pl.pallas_call(
        functools.partial(back_kernel, n, per),
        out_shape=[
            jax.ShapeDtypeStruct((tokens, rows), BF),
            jax.ShapeDtypeStruct((blocks, length, rank), F32),
            jax.ShapeDtypeStruct((per, rank, width), BF),
        ],
        in_specs=[SMEM, SMEM] + [ANY] * (2 + n + len(after)),
        out_specs=[ANY, VMEM, VMEM],
        scratch_shapes=[
            pltpu.VMEM((blocks, length, width), BF),
            pltpu.VMEM((tiles, rows // tiles, width), BF),
            pltpu.VMEM((tiles, tokens, rows // tiles), BF),
            pltpu.VMEM((n, t, CAP, rank, cols), BF),
            dmas(2),
            dmas(tiles),
            dmas(tiles),
            dmas(n),
        ],
        compiler_params=params(),
        cost_estimate=cost(2 * tokens * rows * width, 2 * (tokens * (width + rows) + rows * width)),
        name="back",
    )(where, pos, sens_blocks, weight, *ups, *after)


def state_grad_kernel(pos_ref, factor_ref, cols_ref, proj_ref, back_ref, down_ref, o_ref, *rest):
    in_buf, out_buf, in_sem, out_sem = rest
    blocks, length, _ = back_ref.shape
    half = blocks // 2
    loads = []
    for p in range(half):
        some = pl.ds(2 * p, 2)
        loads.append(fetch(back_ref.at[some], in_buf.at[some], in_sem.at[p]))
    weight = factor_ref[...] * cols_ref[...]
    stores = []
    for b in range(blocks):
        if b % 2 == 0:
            loads[b // 2].wait()
        hcot = (adapter_scale * proj_ref[b]).astype(BF)
        at = pos_ref[b]
        total = in_buf[b].astype(F32) + nn(hcot, down_ref[at // CAP, lax.rem(at, CAP)])
        out_buf[b] = (weight[:, b : b + 1] * total).astype(BF)
        if b % 2 == 1:
            some = pl.ds(b - 1, 2)
            stores.append(fetch(out_buf.at[some], o_ref.at[some], out_sem.at[b // 2]))
    for store in stores:
        store.wait()


def state_grad(pos, factor, columns, proj, backward, down_recv):
    blocks, length, rows = backward.shape
    rank = down_recv.shape[2]
    return pl.pallas_call(
        state_grad_kernel,
        out_shape=jax.ShapeDtypeStruct((blocks, length, rows), BF),
        in_specs=[SMEM, VMEM, VMEM, VMEM, ANY, VMEM],
        out_specs=ANY,
        scratch_shapes=[
            pltpu.VMEM((blocks, length, rows), BF),
            pltpu.VMEM((blocks, length, rows), BF),
            dmas(blocks // 2),
            dmas(blocks // 2),
        ],
        compiler_params=params(),
        cost_estimate=cost(2 * blocks * length * rows * rank, 4 * blocks * length * rows, LATE),
        name="state_grad",
    )(pos, factor, columns, proj, backward, down_recv)


def slot_sum_kernel(n, rank, where, send_ref, *rest):
    grads, rest = rest[:n], rest[n:]
    msg_ref, (down_ref, up_ref, acc, up_acc, out_buf, out_sems) = rest[0], rest[-6:]
    me = where[0]
    slots = acc.shape[0]
    acc[...] = jnp.zeros_like(acc)
    up_acc[...] = jnp.zeros_like(up_acc)
    for k in range(n):
        for r in range(CAP):
            slot = send_ref[(me ^ k) * CAP + r]
            used = slot >= 0
            slot = jnp.maximum(slot, 0)
            tail = jnp.sum(msg_ref[me ^ k, r, rank : rank + PAD, 0:LANES].astype(F32), axis=0, keepdims=True)
            part = tail[:, 0:1] * grads[k][r].astype(F32)
            acc[slot] += jnp.where(used, part, 0.0)
            up_acc[slot] += jnp.where(used, msg_ref[me ^ k, r, 0:rank, :].astype(F32), 0.0)
    stores = []
    for s in range(slots):
        out_buf[s] = acc[s].astype(BF)
        stores.append(fetch(out_buf.at[s], down_ref.at[s], out_sems.at[s]))
    up_ref[...] = up_acc[...].astype(BF)
    for store in stores:
        store.wait()


def slot_sum(slots, where, send_tab, grads, msgs, after=()):
    n = len(grads)
    _, rank, rows = grads[0].shape
    cols = msgs.shape[3]
    return pl.pallas_call(
        functools.partial(slot_sum_kernel, n, rank),
        in_specs=[SMEM, SMEM] + [VMEM] * (n + 1) + [ANY] * len(after),
        out_specs=[ANY, VMEM],
        scratch_shapes=[
            pltpu.VMEM((slots, rank, rows), F32),
            pltpu.VMEM((slots, rank, cols), F32),
            pltpu.VMEM((slots, rank, rows), BF),
            dmas(slots),
        ],
        out_shape=[
            jax.ShapeDtypeStruct((slots, rank, rows), BF),
            jax.ShapeDtypeStruct((slots, rank, cols), BF),
        ],
        compiler_params=params(SMALL_LIMIT),
        cost_estimate=cost(0, 2 * (n * CAP + slots) * rank * rows, LATE),
        name="slot_sum",
    )(where, send_tab, *grads, msgs, *after)


def layer_out_kernel(per, whole, halved, msg_ref, up_ref, *rest):
    parts, o_ref = rest[: whole + 2 * halved], rest[-1]
    length = msg_ref.shape[0] - PAD
    rank = up_ref.shape[1]
    piece = o_ref.shape[0]
    for h in range(per):
        hidden = msg_ref[0:length, h * rank : (h + 1) * rank]
        adapter = adapter_scale * nn(hidden, up_ref[h])
        cuts = sorted({h * length, (h + 1) * length} | ({piece // 2} if per == 1 else set()))
        for low, high in zip(cuts[:-1], cuts[1:]):
            total = adapter[low - h * length : high - h * length]
            for part in parts[:whole]:
                total = total + part[low:high, :].astype(F32)
            p = low // (piece // 2)
            base = p * (piece // 2)
            for i in range(halved):
                total = total + parts[whole + 2 * i + p][low - base : high - base, :].astype(F32)
            o_ref[low:high, :] = total.astype(BF)


def layer_out(own_msg, up_own, whole, halves, after=()):
    piece, width = whole[0].shape
    per, rank, _ = up_own.shape
    return pl.pallas_call(
        functools.partial(layer_out_kernel, per, len(whole), len(halves) // 2),
        in_specs=[VMEM] * (2 + len(whole) + len(halves)) + [ANY] * len(after),
        out_specs=VMEM,
        out_shape=jax.ShapeDtypeStruct((piece, width), BF),
        compiler_params=params(),
        cost_estimate=cost(2 * piece * rank * width, 2 * piece * width * (2 + len(whole)), LATE),
        name="layer_out",
    )(own_msg, up_own, *whole, *halves, *after)


def exchange(value, axis):
    return lax.all_to_all(value, axis, 0, 0, tiled=True)


def swap(value, axis, k):
    size = lax.axis_size(axis)
    return lax.ppermute(value, axis, [(i, i ^ k) for i in range(size)])


def shards(
    token_states,
    base_weight,
    adapter_down,
    adapter_up,
    slot_of_tenant,
    seq_tenant,
    seq_len,
    token_mask,
    logp_gap,
    out_sens,
    advantage,
):
    n = lax.axis_size("dp")
    t = lax.axis_size("tensor")
    slots, rows, rank = adapter_down.shape
    width = out_sens.shape[1]
    blocks = seq_len.shape[0]
    length = token_states.shape[0] // blocks
    per = blocks // t
    where = jnp.stack([lax.axis_index("dp"), lax.axis_index("tensor")]).astype(jnp.int32)
    state_blocks = token_states.reshape(blocks, length, rows)
    sens_blocks = out_sens.reshape(blocks, length, width)
    down_t = jnp.swapaxes(adapter_down, 1, 2)

    up_parts = [adapter_up] + [swap(adapter_up, "tensor", k) for k in range(1, t)]
    send_tab, pos, down_send = route(n, where, slot_of_tenant, seq_tenant, down_t, blocks)
    down_recv = exchange(down_send, "dp")
    columns, seq_rows = prepare(
        seq_len, token_mask.reshape(blocks, length), logp_gap.reshape(blocks, length), advantage[None]
    )
    middle = t // 2
    halved = [middle]
    others = [k for k in range(t - 1, -1, -1) if k not in halved]
    parts = frozen(t, halved + others, 1, where, token_states, base_weight, (down_send, up_parts[1], columns))
    chunks = dict(zip(others, parts[2:]))
    up_send = pick_up(n, t, where, send_tab, up_parts, (chunks[0],))
    ups = [up_send[0]] + [swap(up_send[k], "dp", k) for k in range(1, n)]
    hidden = hidden_parts(t, where, pos, state_blocks, down_recv, (up_send[0],))
    hidden = [hidden[0]] + [swap(hidden[k], "tensor", k) for k in range(1, t)]
    early = [swap(parts[0], "tensor", middle)]
    piece, _ = lax.optimization_barrier((parts[1], hidden[0]))
    early.append(swap(piece, "tensor", middle))
    backward, proj, up_own = back(n, where, pos, sens_blocks, base_weight, ups, (hidden[0], early[0]))
    own_msg = own_hidden(t, where, hidden, proj, columns, seq_rows, per, rank)
    msgs = [own_msg] + [swap(own_msg, "tensor", k) for k in range(1, t)]
    far, near = list(range(2, n)), list(range(min(n, 2)))
    grads = dict(zip(far, panel_grads(far, where, pos, columns, proj, state_blocks, (own_msg,))))
    grads |= dict(zip(near, panel_grads(near, where, pos, columns, proj, state_blocks, (*msgs[1:], early[1]))))
    grads_in = [grads[0]] + [swap(grads[k], "dp", k) for k in range(1, n)]
    factor, loss, up_out = up_grads(n, t, where, pos, sens_blocks, columns, seq_rows, msgs, rank)
    up_in = exchange(up_out, "dp")
    token_state_gradient = state_grad(
        pos, factor, columns, proj, backward.reshape(blocks, length, rows), down_recv
    )
    late = {}
    for k in others[:-1]:
        piece, _ = lax.optimization_barrier((chunks[k], (msgs[1:], [grads[i] for i in far])))
        late[k] = swap(piece, "tensor", k)
    whole = [chunks[0]] + [late[k] for k in others[:-1]]
    down_grad, up_grad = slot_sum(slots, where, send_tab, grads_in, up_in)
    out = layer_out(own_msg, up_own, whole, early, (up_grad,))
    return (
        out,
        loss[0, :blocks],
        token_state_gradient.reshape(blocks * length, rows),
        jnp.swapaxes(down_grad, 1, 2),
        up_grad,
    )


def solution(mesh):
    in_specs = (
        P(("groups", "dp"), "tensor"),
        P("tensor", None),
        P(("groups", "dp"), "tensor", None),
        P(("groups", "dp"), None, "tensor"),
        P("groups"),
        P("groups"),
        P(("groups", "dp")),
        P(("groups", "dp")),
        P(("groups", "dp")),
        P(("groups", "dp"), None),
        P(("groups", "dp")),
    )
    out_specs = (
        P(("groups", "dp", "tensor"), None),
        P(("groups", "dp")),
        P(("groups", "dp"), "tensor"),
        P(("groups", "dp"), "tensor", None),
        P(("groups", "dp"), None, "tensor"),
    )
    return jax.shard_map(shards, mesh=mesh, in_specs=in_specs, out_specs=out_specs, check_vma=False)
```
